32 devices in a mesh: dp: 4 (over y, x), seq: 8 (over z, core).
Axes of the slice: x: 2, y: 2, z: 4, core: 2. Of those that a mesh axis runs over, the one named last changes fastest.
Arguments:
- frames: bfloat16 [8, 1024, 1024], P('dp', 'seq'), may hold values from -6 to 6
- segments: int32 [8, 1024], P('dp', 'seq'), may hold values from 0 to 16, as said below
- cotangent: bfloat16 [8, 1024, 1024], P('dp', 'seq'), may hold values from -6 to 6
- norm_gains: bfloat16 [6, 1024], P(None, 'seq'), may hold values from 0.5 to 1.5
- norm_biases: bfloat16 [6, 1024], P(None, 'seq'), may hold values from -3 to 3
- front_up: bfloat16 [1024, 4096], P('seq'), may hold values from -0.1875 to 0.1875
- front_down: bfloat16 [4096, 1024], P('seq'), may hold values from -0.09375 to 0.09375
- attend_in: bfloat16 [1024, 3072], P('seq'), may hold values from -0.1875 to 0.1875
- attend_out: bfloat16 [1024, 1024], P('seq'), may hold values from -0.75 to 0.75
- slopes: float32 [16], replicated, may hold values from 0.05 to 0.6
- point_in: bfloat16 [1024, 2048], P('seq'), may hold values from -0.1875 to 0.1875
- depthwise: bfloat16 [31, 1024], P(None, 'seq'), may hold values from -1 to 1
- point_out: bfloat16 [1024, 1024], P('seq'), may hold values from -0.1875 to 0.1875
- rear_up: bfloat16 [1024, 4096], P('seq'), may hold values from -0.1875 to 0.1875
- rear_down: bfloat16 [4096, 1024], P('seq'), may hold values from -0.09375 to 0.09375
Outputs:
- result: bfloat16 [8, 1024, 1024], P('dp', 'seq')
- frames_grad: bfloat16 [8, 1024, 1024], P('dp', 'seq')
- gains_grad: float32 [6, 1024], P(None, 'seq')
- biases_grad: float32 [6, 1024], P(None, 'seq')
- front_up_grad: float32 [1024, 4096], P('seq')
- front_down_grad: float32 [4096, 1024], P('seq')
- attend_in_grad: float32 [1024, 3072], P('seq')
- attend_out_grad: float32 [1024, 1024], P('seq')
- slopes_grad: float32 [16], replicated
- point_in_grad: float32 [1024, 2048], P('seq')
- depthwise_grad: float32 [31, 1024], P(None, 'seq')
- point_out_grad: float32 [1024, 1024], P('seq')
- rear_up_grad: float32 [1024, 4096], P('seq')
- rear_down_grad: float32 [4096, 1024], P('seq')
The draws below stay inside these ranges and needn't reach their ends.
Inputs may be any that keep to these rules, and one draw needn't show every extreme that they name: `segments`: each row's numbers start at 0 and rise by 0 or 1 from one frame to the next, so an utterance is a run of frames. In each group of 2 rows of one index of dp, one row drawn from the seed holds exactly three utterances, the middle one starting within the first 128 frames and ending within the last 128; every other row ends at the number 2 * 8.
All inputs are finite; a program needn't handle non-finite values.
Results may differ from the reference program's by a relative error of at most 0.03.
Values may be sent and summed in bfloat16 or wider, within the bound.
A program may use at most 320 MiB of HBM per device.

```python
import math
import jax
import jax.numpy as jnp
from jax import lax

D = 1024
HEADS = 16
HEAD_DIM = 64
FF = 4096
KERNEL = 31
ROWS_DEV = 2
FR_DEV = 128
ROWS = 8
LENGTH = 1024


def draw_segments(key, part):
    key = jax.random.fold_in(key, 7)
    key_cut, key_force, key_pick, key_start, key_end = jax.random.split(key, 5)
    half_span = FR_DEV // 2
    stretch_count = 2 * (LENGTH // FR_DEV)
    frame_place = jnp.arange(LENGTH, dtype=jnp.int32)[None, :]
    cut_draw = jax.random.randint(key_cut, (ROWS, LENGTH), 0, FR_DEV)
    offsets = jax.random.randint(key_force, (ROWS, stretch_count), 1, half_span)
    offset_full = jnp.repeat(offsets, half_span, axis=1)
    is_forced = frame_place % half_span == offset_full
    is_cut = jnp.logical_or(jnp.logical_and(cut_draw == 0, frame_place > 0), is_forced)
    packed_ids = jnp.minimum(jnp.cumsum(is_cut.astype(jnp.int32), axis=1), stretch_count)
    chosen = jax.random.randint(key_pick, (ROWS // ROWS_DEV, 1), 0, ROWS_DEV)
    row_place = jnp.arange(ROWS, dtype=jnp.int32).reshape(ROWS // ROWS_DEV, ROWS_DEV)
    is_span = (row_place % ROWS_DEV == chosen).reshape(ROWS, 1)
    first_cut = jax.random.randint(key_start, (ROWS, 1), 1, FR_DEV)
    last_cut = jax.random.randint(key_end, (ROWS, 1), LENGTH - FR_DEV + 1, LENGTH)
    span_ids = (frame_place >= first_cut).astype(jnp.int32) + (frame_place >= last_cut).astype(jnp.int32)
    return jnp.where(is_span, span_ids, packed_ids).astype(jnp.int32)


def level_of(own_key, extent, cuts, low, largest):
    level = 1.0
    for axis_at, parts in cuts:
        draws = jax.random.uniform(jax.random.fold_in(jax.random.fold_in(own_key, 6), axis_at), (parts,), jnp.float32, low / len(cuts), largest / len(cuts))
        level = level * jnp.repeat(jnp.exp(draws), extent[axis_at] // parts).reshape((-1,) + (1,) * (len(extent) - 1 - axis_at))
    return level


def gaussian(key, shape, scale, limit, pieces=(), kind=jnp.bfloat16):
    gain = level_of(key, shape, pieces, -0.22, 0.18) if pieces else 1.0
    values = jax.random.normal(key, shape, jnp.float32) * scale * gain
    return jnp.minimum(jnp.maximum(values, -limit), limit).astype(kind)


def setup_inputs(seed: int = 0) -> dict:
    keys = jax.random.split(jax.random.key(seed), 16)
    frames = gaussian(keys[0], (ROWS, LENGTH, D), 1.0, 6.0, ((0, 4), (1, 8)))
    segments = draw_segments(jax.random.fold_in(keys[15], 71), 0)
    cotangent = gaussian(keys[2], (ROWS, LENGTH, D), 1.0, 6.0, ((0, 4), (1, 8)))
    norm_gains = jnp.clip(1.0 + 0.1 * jax.random.normal(keys[3], (6, D), jnp.float32), 0.5, 1.5).astype(jnp.bfloat16)
    norm_biases = gaussian(keys[4], (6, D), 0.3, 3.0, ((1, 8),))
    front_up = gaussian(keys[5], (D, FF), D ** -0.5, 0.1875, ((0, 8),))
    front_down = gaussian(keys[6], (FF, D), FF ** -0.5, 0.09375, ((0, 8),))
    attend_in = gaussian(keys[7], (D, 3 * D), D ** -0.5, 0.1875, ((0, 8),))
    attend_out = gaussian(keys[8], (D, D), (D // 16) ** -0.5, 0.75, ((0, 8),))
    slopes = jnp.clip(jnp.exp(jax.random.uniform(keys[9], (HEADS,), jnp.float32, math.log(0.05), math.log(0.6))), 0.05, 0.6)
    point_in = gaussian(keys[10], (D, 2 * D), D ** -0.5, 0.1875, ((0, 8),))
    depthwise = gaussian(keys[11], (KERNEL, D), KERNEL ** -0.5, 1.0, ((1, 8),))
    point_out = gaussian(keys[12], (D, D), D ** -0.5, 0.1875, ((0, 8),))
    rear_up = gaussian(keys[13], (D, FF), D ** -0.5, 0.1875, ((0, 8),))
    rear_down = gaussian(keys[14], (FF, D), FF ** -0.5, 0.09375, ((0, 8),))
    return dict(frames=frames, segments=segments, cotangent=cotangent, norm_gains=norm_gains, norm_biases=norm_biases, front_up=front_up, front_down=front_down, attend_in=attend_in, attend_out=attend_out, slopes=slopes, point_in=point_in, depthwise=depthwise, point_out=point_out, rear_up=rear_up, rear_down=rear_down)


@jax.custom_vjp
def low(v):
    return lax.optimization_barrier(v.astype(jnp.bfloat16)).astype(jnp.float32)

@jax.custom_vjp
def low_back(v):
    return v

def low_keep(v):
    return (low(v), None)

def low_pass(kept, grad):
    return (grad,)

def back_keep(v):
    return (v, None)

def back_low(kept, grad):
    return (low(grad),)
low.defvjp(low_keep, low_pass)
low_back.defvjp(back_keep, back_low)
HIGHEST = lax.Precision.HIGHEST

def matmul(left, right):
    return jnp.dot(left, right, precision=HIGHEST, preferred_element_type=jnp.float32)

def layer_norm(stream, norm_gain, norm_bias):
    average = lax.optimization_barrier(jnp.mean(stream, axis=-1, keepdims=True))
    centred = stream - average
    spread = lax.optimization_barrier(jnp.mean(centred * centred, axis=-1, keepdims=True))
    return centred * lax.rsqrt(spread + 1e-05) * norm_gain + norm_bias

def feed_forward(stream, norm_gain, norm_bias, weight_up, weight_down):
    normed = low(layer_norm(stream, norm_gain, norm_bias))
    inner_act = low_back(matmul(normed, weight_up))
    hidden = low(jax.nn.silu(inner_act))
    return stream + 0.5 * low_back(matmul(hidden, weight_down))

def attention(stream, segment, norm_gain, norm_bias, weight_in, weight_out, slopes):
    row_length = stream.shape[0]
    feature_count = stream.shape[1]
    normed = low(layer_norm(stream, norm_gain, norm_bias))
    packed = low(low_back(matmul(normed, weight_in)))
    query_heads = packed[:, :feature_count].reshape(row_length, HEADS, HEAD_DIM)
    key_heads = packed[:, feature_count:2 * feature_count].reshape(row_length, HEADS, HEAD_DIM)
    value_heads = packed[:, 2 * feature_count:].reshape(row_length, HEADS, HEAD_DIM)
    block_len = 2 * FR_DEV
    block_count = row_length // block_len
    score_scale = HEAD_DIM ** (-0.5)
    key_place = jnp.arange(row_length, dtype=jnp.int32)

    def one_block(element):
        query_block, segment_block, block_start = element
        raw_score = low_back(jnp.einsum('qhd,khd->hqk', query_block, key_heads, precision=HIGHEST) * score_scale)
        query_place = block_start + jnp.arange(block_len, dtype=jnp.int32)
        distance = jnp.abs(query_place[:, None] - key_place[None, :]).astype(jnp.float32)
        logits = raw_score - slopes[:, None, None] * jnp.log1p(distance)[None]
        is_live = (segment_block[:, None] == segment[None, :])[None]
        logits = jnp.where(is_live, logits, -1e+30)
        row_top = lax.optimization_barrier(jnp.max(logits, axis=-1, keepdims=True))
        row_exp = jnp.exp(logits - row_top)
        row_prob = row_exp / lax.optimization_barrier(jnp.sum(row_exp, axis=-1, keepdims=True))
        return jnp.einsum('hqk,khd->qhd', low(row_prob), value_heads, precision=HIGHEST)
    block_starts = jnp.arange(block_count, dtype=jnp.int32) * block_len
    attended_blocks = lax.map(jax.checkpoint(one_block), (query_heads.reshape(block_count, block_len, HEADS, HEAD_DIM), segment.reshape(block_count, block_len), block_starts))
    attended = low(low_back(attended_blocks.reshape(row_length, feature_count)))
    return stream + low_back(matmul(attended, weight_out))

def convolution(stream, segment, gain_one, bias_one, gain_two, bias_two, weight_in, depth_taps, weight_out):
    row_length = stream.shape[0]
    feature_count = stream.shape[1]
    half_k = KERNEL // 2
    normed = low(layer_norm(stream, gain_one, bias_one))
    inner_act = low_back(matmul(normed, weight_in))
    gated_u = low(inner_act[:, :feature_count] * jax.nn.sigmoid(inner_act[:, feature_count:]))
    padded = jnp.pad(gated_u, ((half_k, half_k), (0, 0)))
    padded_seg = jnp.pad(segment, (half_k, half_k), constant_values=-1)
    mixed_conv = jnp.zeros((row_length, feature_count), jnp.float32)
    for offset in range(KERNEL):
        same_seg = (padded_seg[offset:offset + row_length] == segment)[:, None]
        mixed_conv = mixed_conv + jnp.where(same_seg, depth_taps[offset] * padded[offset:offset + row_length], 0.0)
    mixed_conv = low_back(mixed_conv)
    activated = low(jax.nn.silu(layer_norm(mixed_conv, gain_two, bias_two)))
    return stream + low_back(matmul(activated, weight_out))

def row_forward(parameters, stream, segment):
    gains, biases, front_up, front_down, attend_in, attend_out, slopes, point_in, depthwise, point_out, rear_up, rear_down = parameters
    stream = feed_forward(stream, gains[0], biases[0], front_up, front_down)
    stream = attention(stream, segment, gains[1], biases[1], attend_in, attend_out, slopes)
    stream = convolution(stream, segment, gains[2], biases[2], gains[3], biases[3], point_in, depthwise, point_out)
    stream = feed_forward(stream, gains[4], biases[4], rear_up, rear_down)
    return layer_norm(stream, gains[5], biases[5])

def reference(frames, segments, cotangent, norm_gains, norm_biases, front_up, front_down, attend_in, attend_out, slopes, point_in, depthwise, point_out, rear_up, rear_down):
    parameters = tuple((weight.astype(jnp.float32) for weight in (norm_gains, norm_biases, front_up, front_down, attend_in, attend_out, slopes, point_in, depthwise, point_out, rear_up, rear_down)))

    def forward(weights_now, inputs):

        def per_row(element):
            return row_forward(weights_now, element[0], element[1])
        return lax.map(jax.checkpoint(per_row), (inputs, segments))
    output, pull_back = jax.vjp(forward, parameters, frames.astype(jnp.float32))
    gradients, frames_grad = pull_back(cotangent.astype(jnp.float32))
    return (output.astype(jnp.bfloat16), frames_grad.astype(jnp.bfloat16), gradients[0], gradients[1], gradients[2], gradients[3], gradients[4], gradients[5], gradients[6], gradients[7], gradients[8], gradients[9], gradients[10], gradients[11])
```

```python
import functools

import jax
import jax.numpy as jnp
from jax import lax
from jax.experimental import pallas as pl
from jax.experimental.pallas import tpu as pltpu
from jax.sharding import PartitionSpec as P


def padded(value, sides, width):
    for axis, dim in sides:
        peers, length = (lax.axis_size(axis), value.shape[dim])
        up = [(i, (i + 1) % peers) for i in range(peers - 1)]
        down = [(j, i) for i, j in up]
        last = lax.slice_in_dim(value, length - width, length, axis=dim)
        leading = lax.slice_in_dim(value, 0, width, axis=dim)
        before = lax.ppermute(last, axis, up)
        after = lax.ppermute(leading, axis, down)
        value = jnp.concatenate([before, value, after], axis=dim)
    return value


def shifted(block, axis, distance):
    devices = range(lax.axis_size(axis))
    route = [((i - distance) % len(devices), i) for i in devices]
    return lax.ppermute(block, axis, route)


def layer_norm(stream, norm_gain, norm_bias):
    average = jnp.mean(stream, axis=-1, keepdims=True)
    centred = stream - average
    spread = jnp.mean(centred * centred, axis=-1, keepdims=True)
    return centred * lax.rsqrt(spread + 1e-05) * norm_gain + norm_bias


def feed_forward(stream, norm_gain, norm_bias, weight_up, weight_down):
    normed, norm_pull = jax.vjp(layer_norm, stream, norm_gain, norm_bias)
    normed_low = normed.astype(jnp.bfloat16)
    inner_act = jnp.dot(normed_low, weight_up, preferred_element_type=jnp.float32)
    hidden, act_pull = jax.vjp(jax.nn.silu, inner_act)
    hidden_low = hidden.astype(jnp.bfloat16)
    branch = jnp.dot(hidden_low, weight_down, preferred_element_type=jnp.float32)
    return (stream + 0.5 * branch, (norm_pull, normed_low, act_pull, hidden_low))


def feed_backward(grad_in, saved_state, weight_up, weight_down):
    norm_pull, normed_low, act_pull, hidden_low = saved_state
    branch_low = (0.5 * grad_in).astype(jnp.bfloat16)
    down_grad = jnp.einsum("tf,td->fd", hidden_low, branch_low, preferred_element_type=jnp.float32)
    hidden_grad = jnp.einsum(
        "td,fd->tf", branch_low, weight_down, preferred_element_type=jnp.float32
    )
    inner_grad = act_pull(hidden_grad)[0].astype(jnp.bfloat16)
    up_grad = jnp.einsum("td,tf->df", normed_low, inner_grad, preferred_element_type=jnp.float32)
    normed_grad = jnp.einsum("tf,df->td", inner_grad, weight_up, preferred_element_type=jnp.float32)
    stream_grad, gain_grad, bias_grad = norm_pull(normed_grad)
    return (grad_in + stream_grad, gain_grad, bias_grad, up_grad, down_grad)


def score_block(query_heads, key_piece, query_start, key_start, query_seg, key_seg, slopes):
    row_count, key_count, feature_count = key_piece.shape
    head_count = query_heads.shape[2]
    head_size = query_heads.shape[3]
    key_heads = key_piece.reshape(row_count, key_count, head_count, head_size)
    raw_score = jnp.einsum(
        "rqhd,rkhd->rqhk", query_heads, key_heads, preferred_element_type=jnp.float32
    ) * head_size ** (-0.5)
    query_place = query_start + jnp.arange(query_heads.shape[1], dtype=jnp.int32)
    key_place = key_start + jnp.arange(key_count, dtype=jnp.int32)
    log_distance = jnp.log1p(jnp.abs(query_place[:, None] - key_place[None, :]).astype(jnp.float32))
    is_live = (query_seg[:, :, None] == key_seg[:, None, :])[:, :, None, :]
    logits = jnp.where(
        is_live, raw_score - slopes[None, None, :, None] * log_distance[None, :, None, :], -1e30
    )
    return (logits, is_live, log_distance, key_heads)


def prob_grads(
    query_heads,
    grad_heads,
    log_sum,
    row_delta,
    query_start,
    query_seg,
    key_piece,
    value_piece,
    key_start,
    key_seg,
    slopes,
):
    logits, is_live, log_distance, key_heads = score_block(
        query_heads, key_piece, query_start, key_start, query_seg, key_seg, slopes
    )
    row_prob = jnp.where(is_live, jnp.exp(logits - log_sum[..., None]), 0.0)
    value_heads = value_piece.reshape(key_heads.shape)
    prob_grad = jnp.einsum(
        "rqhd,rkhd->rqhk", grad_heads, value_heads, preferred_element_type=jnp.float32
    )
    score_grad = row_prob * (prob_grad - row_delta[..., None])
    return (row_prob, score_grad, score_grad.astype(jnp.bfloat16), log_distance, key_heads)


def body(
    frames,
    segments,
    cotangent,
    norm_gains,
    norm_biases,
    front_up,
    front_down,
    attend_in,
    attend_out,
    slopes,
    point_in,
    depthwise,
    point_out,
    rear_up,
    rear_down,
):
    row_count, frame_count, feature_count = frames.shape
    head_count = slopes.shape[0]
    head_size = feature_count // head_count
    token_count = row_count * frame_count
    seq_size = lax.axis_size("seq")
    seq_index = lax.axis_index("seq")
    query_start = seq_index * frame_count
    score_scale = head_size ** (-0.5)
    (
        gains_w,
        biases_w,
        front_up_w,
        front_down_w,
        attend_in_w,
        attend_out_w,
        point_in_w,
        depth_w,
        point_out_w,
        rear_up_w,
        rear_down_w,
    ) = (
        lax.all_gather(norm_gains, "seq", axis=1, tiled=True),
        lax.all_gather(norm_biases, "seq", axis=1, tiled=True),
        lax.all_gather(front_up, "seq", axis=0, tiled=True),
        lax.all_gather(front_down, "seq", axis=0, tiled=True),
        lax.all_gather(attend_in, "seq", axis=0, tiled=True),
        lax.all_gather(attend_out, "seq", axis=0, tiled=True),
        lax.all_gather(point_in, "seq", axis=0, tiled=True),
        lax.all_gather(depthwise, "seq", axis=1, tiled=True),
        lax.all_gather(point_out, "seq", axis=0, tiled=True),
        lax.all_gather(rear_up, "seq", axis=0, tiled=True),
        lax.all_gather(rear_down, "seq", axis=0, tiled=True),
    )
    gains_f = gains_w.astype(jnp.float32)
    biases_f = biases_w.astype(jnp.float32)
    depth_f = depth_w.astype(jnp.float32)
    kernel_len = depth_f.shape[0]
    half_k = kernel_len // 2
    segment_row = lax.all_gather(segments, "seq", axis=1, tiled=True)
    start_stream = frames.astype(jnp.float32).reshape(token_count, feature_count)
    after_front, front_saved = feed_forward(
        start_stream, gains_f[0], biases_f[0], front_up_w, front_down_w
    )
    attend_normed, attend_pull = jax.vjp(layer_norm, after_front, gains_f[1], biases_f[1])
    attend_low = attend_normed.astype(jnp.bfloat16)
    projected = jnp.dot(attend_low, attend_in_w, preferred_element_type=jnp.float32).astype(
        jnp.bfloat16
    )
    query_heads = projected[:, :feature_count].reshape(
        row_count, frame_count, head_count, head_size
    )
    key_low = projected[:, feature_count : 2 * feature_count].reshape(
        row_count, frame_count, feature_count
    )
    value_low = projected[:, 2 * feature_count :].reshape(row_count, frame_count, feature_count)
    stat_shape = (row_count, frame_count, head_count)
    start = jnp.int32(0)
    key_piece = lax.all_gather(key_low, "seq", axis=1, tiled=True)
    value_piece = lax.all_gather(value_low, "seq", axis=1, tiled=True)
    key_seg = segment_row
    row_top = jnp.full(stat_shape, -1e30, jnp.float32)
    logits, is_live, log_distance, key_heads = score_block(
        query_heads, key_piece, query_start, start, segments, key_seg, slopes
    )
    new_top = jnp.maximum(row_top, jnp.max(logits, axis=-1))
    row_exp = jnp.where(is_live, jnp.exp(logits - new_top[..., None]), 0.0)
    value_heads = value_piece.reshape(key_heads.shape)
    accum = jnp.einsum(
        "rqhk,rkhd->rqhd",
        row_exp.astype(jnp.bfloat16),
        value_heads,
        preferred_element_type=jnp.float32,
    )
    row_top, row_total, accum = (new_top, jnp.sum(row_exp, axis=-1), accum)
    attended = accum / row_total[..., None]
    log_sum = row_top + jnp.log(row_total)
    attended_low = attended.reshape(token_count, feature_count).astype(jnp.bfloat16)
    after_attend = after_front + jnp.dot(
        attended_low, attend_out_w, preferred_element_type=jnp.float32
    )
    conv_normed, conv_pull = jax.vjp(layer_norm, after_attend, gains_f[2], biases_f[2])
    conv_low = conv_normed.astype(jnp.bfloat16)
    conv_pre = jnp.dot(conv_low, point_in_w, preferred_element_type=jnp.float32)

    def gate_unit(inner_act):
        return inner_act[:, :feature_count] * jax.nn.sigmoid(inner_act[:, feature_count:])

    gated, gate_pull = jax.vjp(gate_unit, conv_pre)
    gated_low = gated.astype(jnp.bfloat16).reshape(row_count, frame_count, feature_count)
    gated_wide = padded(gated_low, (("seq", 1),), half_k).astype(jnp.float32)
    padded_seg = jnp.pad(segment_row, ((0, 0), (half_k, half_k)), constant_values=-1)
    seg_window = lax.dynamic_slice_in_dim(padded_seg, query_start, frame_count + 2 * half_k, 1)
    same_list = [
        (seg_window[:, offset : offset + frame_count] == segments)[..., None]
        for offset in range(kernel_len)
    ]
    mixed_conv = jnp.zeros((row_count, frame_count, feature_count), jnp.float32)
    for offset in range(kernel_len):
        mixed_conv = mixed_conv + jnp.where(
            same_list[offset], depth_f[offset] * gated_wide[:, offset : offset + frame_count], 0.0
        )

    def norm_silu(stream, norm_gain, norm_bias):
        return jax.nn.silu(layer_norm(stream, norm_gain, norm_bias))

    activated, activated_pull = jax.vjp(
        norm_silu, mixed_conv.reshape(token_count, feature_count), gains_f[3], biases_f[3]
    )
    activated_low = activated.astype(jnp.bfloat16)
    after_conv = after_attend + jnp.dot(
        activated_low, point_out_w, preferred_element_type=jnp.float32
    )
    after_rear, rear_saved = feed_forward(
        after_conv, gains_f[4], biases_f[4], rear_up_w, rear_down_w
    )
    final_out, final_pull = jax.vjp(layer_norm, after_rear, gains_f[5], biases_f[5])
    result = final_out.astype(jnp.bfloat16).reshape(row_count, frame_count, feature_count)
    grad_rear, gain_five, bias_five = final_pull(
        cotangent.astype(jnp.float32).reshape(token_count, feature_count)
    )
    grad_conv, gain_four, bias_four, rear_up_grad, rear_down_grad = feed_backward(
        grad_rear, rear_saved, rear_up_w, rear_down_w
    )
    conv_branch = grad_conv.astype(jnp.bfloat16)
    point_out_grad = jnp.einsum(
        "td,te->de", activated_low, conv_branch, preferred_element_type=jnp.float32
    )
    activated_grad = jnp.einsum(
        "te,de->td", conv_branch, point_out_w, preferred_element_type=jnp.float32
    )
    mixed_grad, gain_three, bias_three = activated_pull(activated_grad)
    mixed_low = mixed_grad.astype(jnp.bfloat16).reshape(row_count, frame_count, feature_count)
    grad_wide = padded(mixed_low, (("seq", 1),), half_k).astype(jnp.float32)
    mixed_back = mixed_low.astype(jnp.float32)
    depth_rows = [
        jnp.sum(
            jnp.where(
                same_list[offset], mixed_back * gated_wide[:, offset : offset + frame_count], 0.0
            ),
            axis=(0, 1),
        )
        for offset in range(kernel_len)
    ]
    depthwise_grad = jnp.stack(depth_rows)
    gated_grad = jnp.zeros((row_count, frame_count, feature_count), jnp.float32)
    for offset in range(kernel_len):
        mirror = 2 * half_k - offset
        gated_grad = gated_grad + jnp.where(
            same_list[mirror], depth_f[offset] * grad_wide[:, mirror : mirror + frame_count], 0.0
        )
    pre_grad = gate_pull(gated_grad.reshape(token_count, feature_count))[0].astype(jnp.bfloat16)
    point_in_grad = jnp.einsum("td,tc->dc", conv_low, pre_grad, preferred_element_type=jnp.float32)
    conv_normed_grad = jnp.einsum(
        "tc,dc->td", pre_grad, point_in_w, preferred_element_type=jnp.float32
    )
    conv_stream_grad, gain_two, bias_two = conv_pull(conv_normed_grad)
    grad_attend = grad_conv + conv_stream_grad
    attend_branch = grad_attend.astype(jnp.bfloat16)
    attend_out_grad = jnp.einsum(
        "td,te->de", attended_low, attend_branch, preferred_element_type=jnp.float32
    )
    attended_grad = jnp.einsum(
        "te,de->td", attend_branch, attend_out_w, preferred_element_type=jnp.float32
    )
    grad_heads = attended_grad.astype(jnp.bfloat16).reshape(
        row_count, frame_count, head_count, head_size
    )
    row_delta = jnp.sum(grad_heads.astype(jnp.float32) * attended, axis=-1)

    def query_terms(state, key_piece, value_piece, start, key_seg):
        query_grad, slope_grad = state
        row_prob, score_grad, score_low, log_distance, key_heads = prob_grads(
            query_heads,
            grad_heads,
            log_sum,
            row_delta,
            query_start,
            segments,
            key_piece,
            value_piece,
            start,
            key_seg,
            slopes,
        )
        query_grad = (
            query_grad
            + jnp.einsum(
                "rqhk,rkhd->rqhd", score_low, key_heads, preferred_element_type=jnp.float32
            )
            * score_scale
        )
        slope_grad = slope_grad - jnp.einsum("rqhk,qk->h", score_grad, log_distance)
        return (query_grad, slope_grad, row_prob, score_low)

    query_zero = jnp.zeros((row_count, frame_count, head_count, head_size), jnp.float32)
    slope_zero = jnp.zeros((head_count,), jnp.float32)
    local_zero = jnp.zeros((row_count, frame_count, feature_count), jnp.float32)

    def accumulate(step, query_grad, slope_grad, pair_kv, pair_acc):
        owner = (seq_index + step) % seq_size
        start = owner * frame_count
        key_seg = lax.dynamic_slice_in_dim(segment_row, start, frame_count, 1)
        grad_q = query_grad
        grad_s = slope_grad
        key_acc = pair_acc[0]
        value_acc = pair_acc[1]
        grad_q, grad_s, row_prob, score_low = query_terms(
            (grad_q, grad_s), pair_kv[0], pair_kv[1], start, key_seg
        )
        key_acc = key_acc + (
            jnp.einsum(
                "rqhk,rqhd->rkhd", score_low, query_heads, preferred_element_type=jnp.float32
            )
            * score_scale
        ).reshape(row_count, frame_count, feature_count)
        value_acc = value_acc + jnp.einsum(
            "rqhk,rqhd->rkhd",
            row_prob.astype(jnp.bfloat16),
            grad_heads,
            preferred_element_type=jnp.float32,
        ).reshape(row_count, frame_count, feature_count)
        query_grad, slope_grad, key_acc, value_acc = (grad_q, grad_s, key_acc, value_acc)
        pair_acc = shifted(jnp.stack([key_acc, value_acc]).astype(jnp.bfloat16), "seq", -1).astype(
            jnp.float32
        )
        return (query_grad, slope_grad, pair_acc)

    def cycle_step(step, carry):
        query_grad, slope_grad, pair_kv, pair_acc = carry
        next_kv = shifted(pair_kv, "seq", -1)
        query_grad, slope_grad, pair_acc = accumulate(
            step, query_grad, slope_grad, pair_kv, pair_acc
        )
        return (query_grad, slope_grad, next_kv, pair_acc)

    pair_start = jnp.stack([key_low, value_low])
    acc_start = jnp.stack([local_zero, local_zero])
    query_grad, slope_grad, pair_kv, pair_acc = lax.fori_loop(
        0, seq_size - 1, cycle_step, (query_zero, slope_zero, pair_start, acc_start)
    )
    query_grad, slope_grad, pair_acc = accumulate(
        seq_size - 1, query_grad, slope_grad, pair_kv, pair_acc
    )
    key_grad = pair_acc[0]
    value_grad = pair_acc[1]
    projected_grad = jnp.concatenate(
        [
            query_grad.reshape(token_count, feature_count),
            key_grad.reshape(token_count, feature_count),
            value_grad.reshape(token_count, feature_count),
        ],
        axis=1,
    ).astype(jnp.bfloat16)
    attend_in_grad = jnp.einsum(
        "td,tc->dc", attend_low, projected_grad, preferred_element_type=jnp.float32
    )
    attend_normed_grad = jnp.einsum(
        "tc,dc->td", projected_grad, attend_in_w, preferred_element_type=jnp.float32
    )
    attend_stream_grad, gain_one, bias_one = attend_pull(attend_normed_grad)
    grad_front = grad_attend + attend_stream_grad
    start_grad, gain_zero, bias_zero, front_up_grad, front_down_grad = feed_backward(
        grad_front, front_saved, front_up_w, front_down_w
    )
    frames_grad = start_grad.astype(jnp.bfloat16).reshape(row_count, frame_count, feature_count)
    gains_local = jnp.stack([gain_zero, gain_one, gain_two, gain_three, gain_four, gain_five])
    biases_local = jnp.stack([bias_zero, bias_one, bias_two, bias_three, bias_four, bias_five])
    slope_rows = jnp.broadcast_to(slope_grad[None, :], (seq_size, head_count))
    shares = (
        lax.psum_scatter(
            gains_local.astype(jnp.bfloat16), "seq", scatter_dimension=1, tiled=True
        ).astype(jnp.float32),
        lax.psum_scatter(
            biases_local.astype(jnp.bfloat16), "seq", scatter_dimension=1, tiled=True
        ).astype(jnp.float32),
        lax.psum_scatter(
            front_up_grad.astype(jnp.bfloat16), "seq", scatter_dimension=0, tiled=True
        ).astype(jnp.float32),
        lax.psum_scatter(
            front_down_grad.astype(jnp.bfloat16), "seq", scatter_dimension=0, tiled=True
        ).astype(jnp.float32),
        lax.psum_scatter(
            attend_in_grad.astype(jnp.bfloat16), "seq", scatter_dimension=0, tiled=True
        ).astype(jnp.float32),
        lax.psum_scatter(
            attend_out_grad.astype(jnp.bfloat16), "seq", scatter_dimension=0, tiled=True
        ).astype(jnp.float32),
        lax.psum_scatter(
            slope_rows.astype(jnp.bfloat16), "seq", scatter_dimension=0, tiled=True
        ).astype(jnp.float32),
        lax.psum_scatter(
            point_in_grad.astype(jnp.bfloat16), "seq", scatter_dimension=0, tiled=True
        ).astype(jnp.float32),
        lax.psum_scatter(
            depthwise_grad.astype(jnp.bfloat16), "seq", scatter_dimension=1, tiled=True
        ).astype(jnp.float32),
        lax.psum_scatter(
            point_out_grad.astype(jnp.bfloat16), "seq", scatter_dimension=0, tiled=True
        ).astype(jnp.float32),
        lax.psum_scatter(
            rear_up_grad.astype(jnp.bfloat16), "seq", scatter_dimension=0, tiled=True
        ).astype(jnp.float32),
        lax.psum_scatter(
            rear_down_grad.astype(jnp.bfloat16), "seq", scatter_dimension=0, tiled=True
        ).astype(jnp.float32),
    )
    totals = (
        lax.psum(shares[0].astype(jnp.bfloat16), "dp").astype(jnp.float32),
        lax.psum(shares[1].astype(jnp.bfloat16), "dp").astype(jnp.float32),
        lax.psum(shares[2].astype(jnp.bfloat16), "dp").astype(jnp.float32),
        lax.psum(shares[3].astype(jnp.bfloat16), "dp").astype(jnp.float32),
        lax.psum(shares[4].astype(jnp.bfloat16), "dp").astype(jnp.float32),
        lax.psum(shares[5].astype(jnp.bfloat16), "dp").astype(jnp.float32),
        lax.psum(shares[6].astype(jnp.bfloat16), "dp").astype(jnp.float32),
        lax.psum(shares[7].astype(jnp.bfloat16), "dp").astype(jnp.float32),
        lax.psum(shares[8].astype(jnp.bfloat16), "dp").astype(jnp.float32),
        lax.psum(shares[9].astype(jnp.bfloat16), "dp").astype(jnp.float32),
        lax.psum(shares[10].astype(jnp.bfloat16), "dp").astype(jnp.float32),
        lax.psum(shares[11].astype(jnp.bfloat16), "dp").astype(jnp.float32),
    )
    return (
        result,
        frames_grad,
        totals[0],
        totals[1],
        totals[2],
        totals[3],
        totals[4],
        totals[5],
        totals[6].reshape(head_count),
        totals[7],
        totals[8],
        totals[9],
        totals[10],
        totals[11],
    )


def grid_pairs(target):
    pairs = []
    for dp in range(4):
        for seq in range(8):
            there = target(dp // 2, dp % 2, seq // 2, seq % 2)
            if there is not None:
                y, x, z, core = there
                pairs.append((dp * 8 + seq, (y * 2 + x) * 8 + z * 2 + core))
    return pairs


OVER_X = grid_pairs(lambda y, x, z, core: (y, 1 - x, z, core))
OVER_Y = grid_pairs(lambda y, x, z, core: (1 - y, x, z, core))
OVER_CORE = grid_pairs(lambda y, x, z, core: (y, x, z, 1 - core))
OVER_PAIR = grid_pairs(lambda y, x, z, core: (y, x, z + 1 - 2 * (z % 2), core))
OVER_MIDDLE = grid_pairs(lambda y, x, z, core: (y, x, 3 - z, core) if z in (1, 2) else None)
OUTWARD = grid_pairs(lambda y, x, z, core: (y, x, z + (1 if z == 2 else -1), core) if z in (1, 2) else None)
ALONG_Z = [
    grid_pairs(lambda y, x, z, core, k=k: (y, x, (z + k) % 4, core)) for k in range(4)
]


def send(value, pairs):
    return lax.ppermute(value, ("dp", "seq"), pairs)


def place():
    dp, seq = lax.axis_index("dp"), lax.axis_index("seq")
    return dp // 2, dp % 2, seq // 2, seq % 2


def pick(value, index, axis):
    return lax.dynamic_index_in_dim(value, index, axis, keepdims=False)


MESH_ID = pl.DeviceIdType.MESH
PIECE = 32


def chunk_at(ref, lead, chunk, first, rows, tall):
    if tall:
        at = pl.ds(pl.multiple_of(128 * chunk + first, 16), rows)
        return ref.at[lead, at, :] if lead is not None else ref.at[at, :]
    at, cols = pl.ds(pl.multiple_of(first, 16), rows), pl.ds(1024 * chunk, 1024)
    return ref.at[lead, at, cols] if lead is not None else ref.at[at, cols]


def gather_kernel(*refs):
    up, down, inward, vectors, segments = refs[:5]
    up_all, down_all, in_all, vectors_all, segments_all = refs[5:10]
    sems = refs[10:]
    (z_sem, x_sem, y_sem, ax_sem, ay_sem, core_sem, own_sem, small_sem) = sems
    y, x, z, core = place()
    dp, seq = y * 2 + x, z * 2 + core
    over_x = (y * 2 + 1 - x, seq)
    over_y = ((1 - y) * 2 + x, seq)
    over_core = (dp, z * 2 + 1 - core)
    peers = [(dp, lax.rem(seq + k, 8)) for k in range(1, 8)]
    barrier = pltpu.get_barrier_semaphore()
    for there in peers + [over_x, over_y]:
        pl.semaphore_signal(barrier, inc=1, device_id=there, device_id_type=MESH_ID)
    pl.semaphore_wait(barrier, 9)

    def remote(src, dst, sem, at, there):
        copy = pltpu.make_async_remote_copy(
            src_ref=src,
            dst_ref=dst,
            send_sem=sem.at[(0,) + at],
            recv_sem=sem.at[(1,) + at],
            device_id=there,
            device_id_type=MESH_ID,
        )
        copy.start()
        return copy

    waits = []
    for k, there in enumerate(peers):
        waits.append(remote(vectors, vectors_all.at[seq], small_sem, (0, k), there))
        waits.append(remote(segments, segments_all.at[seq], small_sem, (1, k), there))
    chunks = [(up, up_all, j, False) for j in range(4)]
    chunks += [(down, down_all, j, True) for j in range(4)]
    chunks += [(inward, in_all, j, False) for j in range(3)]
    mine = PIECE * dp
    z_copies = {}
    for t, (shard, full, j, tall) in enumerate(chunks):
        for k in (1, 2, 3):
            there = (dp, lax.rem(z + k, 4) * 2 + core)
            z_copies[t, k] = remote(
                chunk_at(shard, None, j, mine, PIECE, tall),
                chunk_at(full, seq, j, mine, PIECE, tall),
                z_sem,
                (t, k - 1),
                there,
            )
    local = []
    for i, (shard, full) in enumerate(((up, up_all), (down, down_all), (inward, in_all))):
        waits.append(remote(shard, full.at[seq], own_sem, (i,), over_core))
        local.append(pltpu.make_async_copy(shard, full.at[seq], own_sem.at[2, i]))
    local.append(pltpu.make_async_copy(vectors, vectors_all.at[seq], own_sem.at[2, 3]))
    local.append(pltpu.make_async_copy(segments, segments_all.at[seq], own_sem.at[2, 4]))
    for copy in local:
        copy.start()

    x_copies, y_copies, ax_copies, ay_copies = {}, {}, {}, {}
    q_x, q_y = PIECE * (y * 2 + 1 - x), PIECE * ((1 - y) * 2 + x)

    def source(k):
        return lax.rem(z - k + 4, 4) * 2 + core

    def forward(copies, t, k, first, rows, sem, there):
        _, full, j, tall = chunks[t]
        where = chunk_at(full, source(k), j, first, rows, tall)
        copies[t, k] = remote(where, where, sem, (t, k - 1), there)

    count = len(chunks)
    for step in range(count + 2):
        for k in (1, 2, 3):
            if step < count:
                z_copies[step, k].wait_recv()
                forward(x_copies, step, k, mine, PIECE, x_sem, over_x)
                forward(y_copies, step, k, mine, PIECE, y_sem, over_y)
        for k in (1, 2, 3):
            t = step - 1
            if 0 <= t < count:
                y_copies[t, k].wait_recv()
                forward(ax_copies, t, k, q_y, PIECE // 2, ax_sem, over_x)
                x_copies[t, k].wait_recv()
                forward(ay_copies, t, k, q_x + PIECE // 2, PIECE // 2, ay_sem, over_y)
        for k in (1, 2, 3):
            t = step - 2
            if 0 <= t < count:
                ax_copies[t, k].wait_recv()
                ay_copies[t, k].wait_recv()
                _, full, j, tall = chunks[t]
                where = chunk_at(full, source(k), j, 0, 128, tall)
                waits.append(remote(where, where, core_sem, (t, k - 1), over_core))
    for copy in waits:
        copy.wait()
    for group in (z_copies, x_copies, y_copies, ax_copies, ay_copies):
        for copy in group.values():
            copy.wait_send()
    for copy in local:
        copy.wait()


def gather_front(front_up, front_down, attend_in, vectors, segments):
    args = (front_up, front_down, attend_in, vectors, segments)
    dma = pltpu.SemaphoreType.DMA
    return pl.pallas_call(
        gather_kernel,
        in_specs=[pl.BlockSpec(memory_space=pltpu.HBM)] * 5,
        out_specs=[pl.BlockSpec(memory_space=pltpu.HBM)] * 5,
        out_shape=[jax.ShapeDtypeStruct((8,) + a.shape, a.dtype) for a in args],
        scratch_shapes=[dma((2, 11, 3))] * 6 + [dma((3, 5)), dma((2, 2, 7))],
        compiler_params=pltpu.CompilerParams(collective_id=0, has_side_effects=True),
        name="gather_front",
    )(*args)


def place_kernel(where, shard, line, over_x, over_y, across_one, across_two, out):
    y, x, z = where[0], where[1], where[2]
    slot = lax.rem(z - pl.program_id(0) + 4, 4)
    half = across_one.shape[1]

    @pl.when(slot == 0)
    def _():
        out[0] = shard[...].reshape(out.shape[1:])

    @pl.when(slot != 0)
    def _():
        out[0, y * 2 + x] = line[0]
        out[0, y * 2 + 1 - x] = over_x[0]
        out[0, (1 - y) * 2 + x] = over_y[0]
        out[0, (1 - y) * 2 + 1 - x, :half] = across_one[0]
        out[0, (1 - y) * 2 + 1 - x, half:] = across_two[0]


def gather_halves(shard):
    y, x, z, core = place()
    rows, cols = shard.shape
    part = rows // 4
    own = lax.dynamic_slice_in_dim(shard, (y * 2 + x) * part, part, 0)
    line = jnp.stack([send(own, ALONG_Z[k]) for k in (1, 2, 3)])
    from_x = send(line, OVER_X)
    from_y = send(line, OVER_Y)
    across_one = send(from_y[:, : part // 2], OVER_X)
    across_two = send(from_x[:, part // 2 :], OVER_Y)

    def spec(height):
        return pl.BlockSpec(
            (1, height, cols),
            lambda i, w: (lax.rem(jnp.maximum(lax.rem(w[2] - i + 4, 4), 1) + 2, 3), 0, 0),
        )

    half = pl.pallas_call(
        place_kernel,
        grid_spec=pltpu.PrefetchScalarGridSpec(
            num_scalar_prefetch=1,
            grid=(4,),
            in_specs=[pl.BlockSpec((rows, cols), lambda i, w: (0, 0))]
            + [spec(part)] * 3
            + [spec(part // 2)] * 2,
            out_specs=pl.BlockSpec((1, 4, part, cols), lambda i, w: (i, 0, 0, 0)),
        ),
        out_shape=jax.ShapeDtypeStruct((4, 4, part, cols), shard.dtype),
        compiler_params=pltpu.CompilerParams(vmem_limit_bytes=32 * 2**20),
        cost_estimate=pl.CostEstimate(
            flops=0, bytes_accessed=rows * cols * 16, transcendentals=0
        ),
        name="place",
    )(jnp.stack([y, x, z]).astype(jnp.int32), shard, line, from_x, from_y, across_one, across_two)
    half = half.reshape(4 * rows, cols)
    return half, send(half, OVER_CORE)


def split_cols(value):
    core = lax.axis_index("seq") % 2
    width = value.shape[1] // 8
    blocks = [value[:, i * width : (i + 1) * width] for i in range(8)]
    first = jnp.concatenate(blocks[0::2], axis=1)
    second = jnp.concatenate(blocks[1::2], axis=1)
    is_first = core == 0
    return jnp.where(is_first, first, second), jnp.where(is_first, second, first)


def merge_cols(own, other):
    core = lax.axis_index("seq") % 2
    width = own.shape[1] // 4
    is_first = core == 0
    first = jnp.where(is_first, own, other)
    second = jnp.where(is_first, other, own)
    blocks = []
    for i in range(4):
        blocks += [first[:, i * width : (i + 1) * width], second[:, i * width : (i + 1) * width]]
    return jnp.concatenate(blocks, axis=1)


def mul(halves, weight):
    if not isinstance(weight, tuple):
        return jnp.dot(merge_cols(*halves), weight, preferred_element_type=jnp.float32)
    out = jnp.dot(halves[0], weight[0], preferred_element_type=jnp.float32)
    return out + jnp.dot(halves[1], weight[1], preferred_element_type=jnp.float32)


def mul_back(grad, weight):
    if not isinstance(weight, tuple):
        return jnp.einsum("tc,dc->td", grad, weight, preferred_element_type=jnp.float32)
    own = jnp.einsum("tc,dc->td", grad, weight[0], preferred_element_type=jnp.float32)
    other = jnp.einsum("tc,dc->td", grad, weight[1], preferred_element_type=jnp.float32)
    return merge_cols(own, other)


def plus(a, b):
    return (a.astype(jnp.float32) + b.astype(jnp.float32)).astype(jnp.bfloat16)


LAG = 1


def reduce_kernel(count, left, right, vec, out, vec_out, *scratch):
    (g_buf, h_buf, a_buf, b_buf, q_buf, core_in, a_in, b_in, a2_in, b2_in, z_in, o_buf) = scratch[:12]
    vec_in, vec_dp, sem, vec_sem = scratch[12:]
    step = pl.program_id(0)
    y, x, z, core = place()
    dp, seq = y * 2 + x, z * 2 + core
    over_x = (y * 2 + 1 - x, seq)
    over_y = ((1 - y) * 2 + x, seq)
    across = ((1 - y) * 2 + 1 - x, seq)
    over_core = (dp, z * 2 + 1 - core)
    peers = [(dp, lax.rem(seq + k, 8)) for k in range(1, 8)]
    dp_peers = [(lax.rem(dp + k, 4), seq) for k in range(1, 4)]

    @pl.when(step == 0)
    def _():
        barrier = pltpu.get_barrier_semaphore()
        for there in peers + dp_peers:
            pl.semaphore_signal(barrier, inc=1, device_id=there, device_id_type=MESH_ID)
        pl.semaphore_wait(barrier, 10)

    def remote(src, dst, t, slot, there):
        return pltpu.make_async_remote_copy(
            src_ref=src,
            dst_ref=dst,
            send_sem=sem.at[0, slot, t],
            recv_sem=sem.at[1, slot, t],
            device_id=there,
            device_id_type=MESH_ID,
        )

    def f32(value):
        return value.astype(jnp.float32)

    def low(value):
        return value.astype(jnp.bfloat16)

    def core_copies(t, slot):
        return [remote(g_buf.at[slot, 1], core_in.at[t], t, 0, over_core)]

    def first_copies(t, slot):
        return [
            remote(h_buf.at[slot, pl.ds(0, 2), :, 1 - x], a_in.at[t], t, 1, over_x),
            remote(h_buf.at[slot, pl.ds(2, 2), 1 - y], b_in.at[t], t, 2, over_y),
        ]

    def second_copies(t, slot):
        return [
            remote(a_buf.at[slot, :, 1 - y], a2_in.at[t], t, 3, over_y),
            remote(b_buf.at[slot, :, 1 - x], b2_in.at[t], t, 4, over_x),
        ]

    def line_copies(t, slot):
        copies = []
        for k in (1, 2, 3):
            to = lax.rem(z + k, 4)
            there = (dp, to * 2 + core)
            copies.append(remote(q_buf.at[slot, to], z_in.at[t, k - 1], t, 4 + k, there))
        return copies

    def share_copies(t, slot):
        where = o_buf.at[t, dp]
        return [remote(where, where, t, 8, over_x), remote(where, where, t, 9, over_y)]

    def across_copies(t, slot):
        one = o_buf.at[t, (1 - y) * 2 + x, pl.ds(0, PIECE // 2)]
        two = o_buf.at[t, y * 2 + 1 - x, pl.ds(PIECE // 2, PIECE // 2)]
        return [remote(one, one, t, 10, over_x), remote(two, two, t, 11, over_y)]

    def finish(copies):
        for copy in copies:
            copy.wait()

    def begin(copies):
        for copy in copies:
            copy.start()

    def write_out(t, slot):
        finish(across_copies(t, slot))
        out[0] = f32(o_buf[t].reshape(128, 1024))

    def pass_on(t, slot):
        finish(share_copies(t, slot))
        begin(across_copies(t, slot))

    def total_line(t, slot):
        finish(line_copies(t, slot))
        total = f32(q_buf[slot, z]) + f32(z_in[t, 0]) + f32(z_in[t, 1]) + f32(z_in[t, 2])
        o_buf[t, dp] = low(total)
        begin(share_copies(t, slot))

    def total_second(t, slot):
        finish(second_copies(t, slot))
        q_buf[slot, 0:2] = low(f32(a_buf[slot, :, y]) + f32(a2_in[t]))
        q_buf[slot, 2:4] = low(f32(b_buf[slot, :, x]) + f32(b2_in[t]))
        begin(line_copies(t, slot))

    def total_first(t, slot):
        finish(first_copies(t, slot))
        a_buf[slot] = low(f32(h_buf[slot, 0:2, :, x]) + f32(a_in[t]))
        b_buf[slot] = low(f32(h_buf[slot, 2:4, y]) + f32(b_in[t]))
        begin(second_copies(t, slot))

    def total_core(t, slot):
        finish(core_copies(t, slot))
        for i in range(4):
            total = low(f32(g_buf[slot, 0, i]) + f32(core_in[t, i]))
            h_buf[slot, i] = total.reshape(2, 2, PIECE, 1024)
        begin(first_copies(t, slot))

    def product(t, slot):
        rows = left[0]
        for i in range(8):
            part = lax.dot_general(
                rows[:, 128 * i : 128 * i + 128],
                right[0],
                (((0,), (0,)), ((), ())),
                preferred_element_type=jnp.float32,
            )
            g_buf[slot, lax.rem(core + i, 2), i // 2] = low(part)
        begin(core_copies(t, slot))

    stages = [product, total_core, total_first, total_second, total_line, pass_on, write_out]
    for depth in reversed(range(len(stages))):
        t = step - LAG * depth

        @pl.when((t >= 0) & (t < count))
        def _(t=t, depth=depth):
            stages[depth](t, lax.rem(t, LAG))

    def vec_copies():
        copies = []
        for k, there in enumerate(peers):
            copies.append(
                pltpu.make_async_remote_copy(
                    src_ref=vec.at[lax.rem(seq + k + 1, 8)],
                    dst_ref=vec_in.at[seq],
                    send_sem=vec_sem.at[0, k],
                    recv_sem=vec_sem.at[1, k],
                    device_id=there,
                    device_id_type=MESH_ID,
                )
            )
        return copies

    def vec_dp_copies():
        copies = []
        for k, there in enumerate(dp_peers):
            copies.append(
                pltpu.make_async_remote_copy(
                    src_ref=vec_dp.at[dp],
                    dst_ref=vec_dp.at[dp],
                    send_sem=vec_sem.at[0, 7 + k],
                    recv_sem=vec_sem.at[1, 7 + k],
                    device_id=there,
                    device_id_type=MESH_ID,
                )
            )
        return copies

    @pl.when(step == 0)
    def _():
        begin(vec_copies())
        vec_in[seq] = vec[seq]

    @pl.when(step == 2)
    def _():
        finish(vec_copies())
        total = vec_in[0]
        for i in range(1, 8):
            total = total + vec_in[i]
        vec_dp[dp] = total
        begin(vec_dp_copies())

    @pl.when(step == 4)
    def _():
        finish(vec_dp_copies())
        vec_out[...] = (vec_dp[0] + vec_dp[1]) + (vec_dp[2] + vec_dp[3])


def reduce_grads(left, right, vec):
    count, tokens, width = left.shape
    bf16 = jnp.bfloat16
    quarter = (PIECE, width)
    return pl.pallas_call(
        functools.partial(reduce_kernel, count),
        grid=(count + 6 * LAG,),
        in_specs=[
            pl.BlockSpec((1, tokens, width), lambda t: (lax.min(t, count - 1), 0, 0)),
            pl.BlockSpec((1, tokens, width), lambda t: (lax.min(t, count - 1), 0, 0)),
            pl.BlockSpec(vec.shape, lambda t: (0, 0, 0)),
        ],
        out_specs=[
            pl.BlockSpec((1, 128, width), lambda t: (lax.max(t - 6 * LAG, 0), 0, 0)),
            pl.BlockSpec(vec.shape[1:], lambda t: (0, 0)),
        ],
        out_shape=[
            jax.ShapeDtypeStruct((count, 128, width), jnp.float32),
            jax.ShapeDtypeStruct(vec.shape[1:], jnp.float32),
        ],
        scratch_shapes=[
            pltpu.VMEM((LAG, 2, 4, 128, width), bf16),
            pltpu.VMEM((LAG, 4, 2, 2) + quarter, bf16),
            pltpu.VMEM((LAG, 2, 2) + quarter, bf16),
            pltpu.VMEM((LAG, 2, 2) + quarter, bf16),
            pltpu.VMEM((LAG, 4) + quarter, bf16),
            pltpu.VMEM((count, 4, 128, width), bf16),
            pltpu.VMEM((count, 2, 2) + quarter, bf16),
            pltpu.VMEM((count, 2, 2) + quarter, bf16),
            pltpu.VMEM((count, 2) + quarter, bf16),
            pltpu.VMEM((count, 2) + quarter, bf16),
            pltpu.VMEM((count, 3) + quarter, bf16),
            pltpu.VMEM((count, 4) + quarter, bf16),
            pltpu.VMEM(vec.shape, jnp.float32),
            pltpu.VMEM((4,) + vec.shape[1:], jnp.float32),
            pltpu.SemaphoreType.DMA((2, 12, count)),
            pltpu.SemaphoreType.DMA((2, 10)),
        ],
        compiler_params=pltpu.CompilerParams(
            collective_id=1, has_side_effects=True, vmem_limit_bytes=56 * 2**20
        ),
        name="reduce_grads",
    )(left, right, vec)


def reduce_grad(halves, grad):
    y, x, z, core = place()
    cols = grad.shape[1]
    part = halves[0].shape[1] // 16
    away = jnp.einsum("td,tc->dc", halves[1], grad, preferred_element_type=jnp.float32)
    away = away.astype(jnp.bfloat16)
    keep = jnp.einsum("td,tc->dc", halves[0], grad, preferred_element_type=jnp.float32)
    keep = keep.astype(jnp.bfloat16)
    came = send(away, OVER_CORE)
    keep = keep.reshape(2, 2, 2, 2, part, cols)
    came = came.reshape(2, 2, 2, 2, part, cols)

    def take(value, index, axis):
        return pick(value, index, axis)

    one_away = plus(take(keep[0], 1 - x, 2), take(came[0], 1 - x, 2))
    two_away = plus(take(keep[1], 1 - y, 1), take(came[1], 1 - y, 1))
    one_came = send(one_away, OVER_X)
    two_came = send(two_away, OVER_Y)

    def sum_one(iy):
        total = take(take(keep[0], x, 2), iy, 1).astype(jnp.float32)
        total += take(take(came[0], x, 2), iy, 1).astype(jnp.float32)
        return (total + take(one_came, iy, 1).astype(jnp.float32)).astype(jnp.bfloat16)

    def sum_two(ix):
        total = take(take(keep[1], y, 1), ix, 1).astype(jnp.float32)
        total += take(take(came[1], y, 1), ix, 1).astype(jnp.float32)
        return (total + take(two_came, ix, 1).astype(jnp.float32)).astype(jnp.bfloat16)

    one_next = send(sum_one(1 - y), OVER_Y)
    two_next = send(sum_two(1 - x), OVER_X)
    line = jnp.concatenate([plus(sum_one(y), one_next), plus(sum_two(x), two_next)])
    total = pick(line, z, 0).astype(jnp.float32)
    for k in (1, 2, 3):
        total += send(pick(line, (z + k) % 4, 0), ALONG_Z[k]).astype(jnp.float32)
    own = total.astype(jnp.bfloat16)
    from_x = send(own, OVER_X)
    from_y = send(own, OVER_Y)
    across_one = send(from_y[: part // 2], OVER_X)
    across_two = send(from_x[part // 2 :], OVER_Y)
    across = jnp.concatenate([across_one, across_two])
    low_x, high_x = jnp.where(x == 0, own, from_x), jnp.where(x == 0, from_x, own)
    low_a, high_a = jnp.where(x == 0, from_y, across), jnp.where(x == 0, across, from_y)
    parts = [
        jnp.where(y == 0, low_x, low_a),
        jnp.where(y == 0, high_x, high_a),
        jnp.where(y == 0, low_a, low_x),
        jnp.where(y == 0, high_a, high_x),
    ]
    return jnp.concatenate(parts).astype(jnp.float32)


QUERIES = 256


def log_distance_block(length, start):
    keys = lax.broadcasted_iota(jnp.int32, (length, QUERIES), 0)
    queries = lax.broadcasted_iota(jnp.int32, (length, QUERIES), 1) + start
    return jnp.log(1.0 + jnp.abs(keys - queries).astype(jnp.float32))


def head_lanes(value, head, scale=1.0):
    lane = lax.broadcasted_iota(jnp.int32, value.shape, 1)
    mine = (lane >= 64 * head) & (lane < 64 * head + 64)
    return jnp.where(mine, value * jnp.asarray(scale, value.dtype), jnp.zeros_like(value))


def nt(a, b):
    return lax.dot_general(a, b, (((1,), (1,)), ((), ())), preferred_element_type=jnp.float32)


def attend_kernel(slopes, key_seg, query_seg, q_ref, k_ref, v_ref, out_ref):
    length = key_seg.shape[1]
    distance = log_distance_block(length, pl.program_id(1) * QUERIES)
    same = key_seg[0] == query_seg[0]
    q = q_ref[...].reshape(QUERIES, 128)
    k = k_ref[...].reshape(length, 128)
    value_t = v_ref[...].reshape(length, 128).T
    outs = []
    for head in range(2):
        logit = nt(k, head_lanes(q, head, 0.125)) - slopes[head] * distance
        logit = jnp.where(same, logit, -1e30)
        top = jnp.max(logit, axis=0, keepdims=True)
        power = jnp.exp(logit - top)
        total = jnp.sum(power, axis=0, keepdims=True)
        out = jnp.dot(value_t, power.astype(jnp.bfloat16), preferred_element_type=jnp.float32)
        outs.append(out[64 * head : 64 * head + 64] / total)
    out = jnp.concatenate(outs, axis=0).T
    out_ref[...] = out.astype(jnp.bfloat16).reshape(out_ref.shape)


def attend_back_kernel(
    slopes, key_seg, query_seg, q_ref, k_ref, v_ref, g_ref, out_ref, slope_ref, key_sum, value_sum
):
    length = key_seg.shape[1]
    step = pl.program_id(1)
    distance = log_distance_block(length, step * QUERIES)
    same = key_seg[0] == query_seg[0]
    q = q_ref[...].reshape(QUERIES, 128)
    k = k_ref[...].reshape(length, 128)
    v = v_ref[...].reshape(length, 128)
    g = g_ref[...].reshape(QUERIES, 128)
    key_t = k.T

    @pl.when(step == 0)
    def _():
        key_sum[...] = jnp.zeros_like(key_sum)
        value_sum[...] = jnp.zeros_like(value_sum)
        slope_ref[...] = jnp.zeros_like(slope_ref)

    outs = []
    for head in range(2):
        q_head = head_lanes(q, head, 0.125)
        g_head = head_lanes(g, head)
        logit = nt(k, q_head) - slopes[head] * distance
        logit = jnp.where(same, logit, -1e30)
        top = jnp.max(logit, axis=0, keepdims=True)
        power = jnp.exp(logit - top)
        prob = power * (1.0 / jnp.sum(power, axis=0, keepdims=True))
        prob_grad = nt(v, g_head)
        delta = jnp.sum(prob * prob_grad, axis=0, keepdims=True)
        logit_grad = prob * (prob_grad - delta)
        slope = jnp.sum(logit_grad * distance, axis=0, keepdims=True)
        slope_ref[0, head : head + 1, :] -= slope
        low = logit_grad.astype(jnp.bfloat16)
        key_sum[...] += jnp.dot(low, q_head, preferred_element_type=jnp.float32)
        value_sum[...] += jnp.dot(
            prob.astype(jnp.bfloat16), g_head, preferred_element_type=jnp.float32
        )
        query_t = jnp.dot(key_t, low, preferred_element_type=jnp.float32)
        outs.append(query_t[64 * head : 64 * head + 64] * 0.125)
    query = jnp.concatenate(outs, axis=0).T.astype(jnp.bfloat16)
    blocks = QUERIES // 128
    out_ref[pl.ds(step * blocks, blocks), 0, 0] = query.reshape(blocks, 128, 128)

    @pl.when(step == pl.num_programs(1) - 1)
    def _():
        out_ref[:, 1, 0] = key_sum[...].astype(jnp.bfloat16).reshape(length // 128, 128, 128)
        out_ref[:, 2, 0] = value_sum[...].astype(jnp.bfloat16).reshape(length // 128, 128, 128)


def attend_specs(peers, frames):
    length = peers * frames
    blocks = QUERIES // frames
    return [
        pl.BlockSpec(memory_space=pltpu.SMEM),
        pl.BlockSpec((1, length, 1), lambda r, i: (r, 0, 0)),
        pl.BlockSpec((1, 1, QUERIES), lambda r, i: (r, 0, i)),
        pl.BlockSpec((blocks, 1, 1, frames, 128), lambda r, i: (i, 0, r, 0, 0)),
        pl.BlockSpec((peers, 1, 1, frames, 128), lambda r, i: (0, 1, r, 0, 0)),
        pl.BlockSpec((peers, 1, 1, frames, 128), lambda r, i: (0, 2, r, 0, 0)),
    ]


def attend(slopes, segment_row, packed):
    peers, _, rows, frames, _ = packed.shape
    length = peers * frames
    blocks = QUERIES // frames
    pairs = rows * length * length * 2
    return pl.pallas_call(
        attend_kernel,
        grid=(rows, length // QUERIES),
        in_specs=attend_specs(peers, frames),
        out_specs=pl.BlockSpec((blocks, 1, frames, 128), lambda r, i: (i, r, 0, 0)),
        out_shape=jax.ShapeDtypeStruct((peers, rows, frames, 128), jnp.bfloat16),
        compiler_params=pltpu.CompilerParams(vmem_limit_bytes=48 * 2**20),
        cost_estimate=pl.CostEstimate(
            flops=pairs * 512, bytes_accessed=packed.size * 3, transcendentals=pairs
        ),
        name="attend",
    )(slopes, segment_row[:, :, None], segment_row[:, None, :], packed, packed, packed)


def attend_back(slopes, segment_row, packed, grads):
    peers, _, rows, frames, _ = packed.shape
    length = peers * frames
    blocks = QUERIES // frames
    pairs = rows * length * length * 2
    return pl.pallas_call(
        attend_back_kernel,
        grid=(rows, length // QUERIES),
        in_specs=attend_specs(peers, frames)
        + [pl.BlockSpec((blocks, 1, frames, 128), lambda r, i: (i, r, 0, 0))],
        out_specs=[
            pl.BlockSpec((peers, 3, 1, frames, 128), lambda r, i: (0, 0, r, 0, 0)),
            pl.BlockSpec((1, 2, QUERIES), lambda r, i: (r, 0, 0)),
        ],
        out_shape=[
            jax.ShapeDtypeStruct(packed.shape, jnp.bfloat16),
            jax.ShapeDtypeStruct((rows, 2, QUERIES), jnp.float32),
        ],
        scratch_shapes=[pltpu.VMEM((length, 128), jnp.float32)] * 2,
        compiler_params=pltpu.CompilerParams(vmem_limit_bytes=56 * 2**20),
        cost_estimate=pl.CostEstimate(
            flops=pairs * 1280, bytes_accessed=packed.size * 5, transcendentals=pairs
        ),
        name="attend_back",
    )(slopes, segment_row[:, :, None], segment_row[:, None, :], packed, packed, packed, grads)


def to_heads(value, count, rows, frames):
    peers = lax.axis_size("seq")
    value = value.reshape(rows, frames, count, peers, 128).transpose(3, 2, 0, 1, 4)
    return lax.all_to_all(value, "seq", 0, 0, tiled=True)


def from_heads(value):
    peers, count, rows, frames, _ = value.shape
    value = lax.all_to_all(value, "seq", 0, 0, tiled=True)
    return value.transpose(2, 3, 1, 0, 4).reshape(rows * frames, count * peers * 128)


def silu_back(pre, grad):
    gate = jax.nn.sigmoid(pre)
    return grad * gate * (1.0 + pre * (1.0 - gate))


def half_layer(stream, gain, bias, up, down):
    normed, pull = jax.vjp(layer_norm, stream, gain, bias)
    normed = split_cols(normed.astype(jnp.bfloat16))
    pre = mul(normed, up)
    hidden = split_cols(jax.nn.silu(pre).astype(jnp.bfloat16))
    return stream + 0.5 * mul(hidden, down), (pull, normed, pre, hidden)


def half_layer_back(grad, saved, up, down):
    pull, normed, pre, hidden = saved
    branch = (0.5 * grad).astype(jnp.bfloat16)
    hidden_grad = mul_back(branch, down)
    pre_grad = silu_back(pre, hidden_grad).astype(jnp.bfloat16)
    stream_grad, gain_grad, bias_grad = pull(mul_back(pre_grad, up))
    return grad + stream_grad, gain_grad, bias_grad, (normed, pre_grad), (hidden, branch)


def body_staged(
    frames,
    segments,
    cotangent,
    norm_gains,
    norm_biases,
    front_up,
    front_down,
    attend_in,
    attend_out,
    slopes,
    point_in,
    depthwise,
    point_out,
    rear_up,
    rear_down,
):
    row_count, frame_count, width = frames.shape
    token_count = row_count * frame_count
    seq = lax.axis_index("seq")
    query_start = seq * frame_count
    taps = depthwise.shape[0]
    half_k = taps // 2

    vector_shard = jnp.concatenate([norm_gains, norm_biases, depthwise])
    vector_shard = jnp.pad(vector_shard, ((0, 48 - vector_shard.shape[0]), (0, 0)))
    segment_shard = jnp.pad(segments, ((0, 8 - row_count), (0, 0)))
    front_up_w, front_down_w, attend_in_w, vectors, segment_row = gather_front(
        front_up, front_down, attend_in, vector_shard, segment_shard
    )
    vectors = vectors.transpose(1, 0, 2).reshape(48, width).astype(jnp.float32)
    gains, biases, depth = vectors[:6], vectors[6:12], vectors[12 : 12 + taps]
    segment_row = segment_row[:, :row_count].transpose(1, 0, 2).reshape(row_count, -1)
    front_up_w = front_up_w.reshape(width, -1)
    front_down_w = front_down_w.reshape(-1, width)
    attend_in_w = attend_in_w.reshape(width, -1)

    middle = jnp.concatenate([attend_out, point_in, point_out], axis=1)
    middle, rear_up, rear_down, front_up_w, front_down_w, attend_in_w = lax.optimization_barrier(
        (middle, rear_up, rear_down, front_up_w, front_down_w, attend_in_w)
    )
    middle_w = gather_halves(middle)
    attend_out_w = tuple(w[:, :width] for w in middle_w)
    point_in_w = tuple(w[:, width : 3 * width] for w in middle_w)
    point_out_w = tuple(w[:, 3 * width :] for w in middle_w)
    rear_up_w = gather_halves(rear_up)
    rear_down_w = gather_halves(rear_down)

    stream = frames.astype(jnp.float32).reshape(token_count, width)
    after_front, front_saved = half_layer(stream, gains[0], biases[0], front_up_w, front_down_w)

    attend_norm, attend_pull = jax.vjp(layer_norm, after_front, gains[1], biases[1])
    attend_norm = split_cols(attend_norm.astype(jnp.bfloat16))
    projected = mul(attend_norm, attend_in_w).astype(jnp.bfloat16)
    packed = to_heads(projected, 3, row_count, frame_count)
    my_slopes = lax.dynamic_slice_in_dim(slopes, seq * 2, 2, 0)
    heads_out = attend(my_slopes, segment_row, packed)
    attended = split_cols(from_heads(heads_out[:, None]))
    after_attend = after_front + mul(attended, attend_out_w)

    conv_norm, conv_pull = jax.vjp(layer_norm, after_attend, gains[2], biases[2])
    conv_norm = split_cols(conv_norm.astype(jnp.bfloat16))
    conv_pre = mul(conv_norm, point_in_w)

    def gate_unit(inner_act):
        return inner_act[:, :width] * jax.nn.sigmoid(inner_act[:, width:])

    gated, gate_pull = jax.vjp(gate_unit, conv_pre)
    gated_low = gated.astype(jnp.bfloat16).reshape(row_count, frame_count, width)
    gated_wide = padded(gated_low, (("seq", 1),), half_k).astype(jnp.float32)
    padded_seg = jnp.pad(segment_row, ((0, 0), (half_k, half_k)), constant_values=-1)
    seg_window = lax.dynamic_slice_in_dim(padded_seg, query_start, frame_count + 2 * half_k, 1)
    same_list = [
        (seg_window[:, offset : offset + frame_count] == segments)[..., None]
        for offset in range(taps)
    ]
    mixed = jnp.zeros((row_count, frame_count, width), jnp.float32)
    for offset in range(taps):
        mixed = mixed + jnp.where(
            same_list[offset], depth[offset] * gated_wide[:, offset : offset + frame_count], 0.0
        )

    def norm_silu(stream, norm_gain, norm_bias):
        return jax.nn.silu(layer_norm(stream, norm_gain, norm_bias))

    activated, activated_pull = jax.vjp(
        norm_silu, mixed.reshape(token_count, width), gains[3], biases[3]
    )
    activated = split_cols(activated.astype(jnp.bfloat16))
    after_conv = after_attend + mul(activated, point_out_w)
    after_rear, rear_saved = half_layer(after_conv, gains[4], biases[4], rear_up_w, rear_down_w)
    final_out, final_pull = jax.vjp(layer_norm, after_rear, gains[5], biases[5])
    result = final_out.astype(jnp.bfloat16).reshape(row_count, frame_count, width)

    grad_rear, gain_five, bias_five = final_pull(
        cotangent.astype(jnp.float32).reshape(token_count, width)
    )
    grad_conv, gain_four, bias_four, rear_up_terms, rear_down_terms = half_layer_back(
        grad_rear, rear_saved, rear_up_w, rear_down_w
    )
    rear_down_grad = reduce_grad(*rear_down_terms)
    rear_up_grad = reduce_grad(*rear_up_terms)
    conv_branch = grad_conv.astype(jnp.bfloat16)
    mixed_grad, gain_three, bias_three = activated_pull(mul_back(conv_branch, point_out_w))
    mixed_low = mixed_grad.astype(jnp.bfloat16).reshape(row_count, frame_count, width)
    grad_wide = padded(mixed_low, (("seq", 1),), half_k).astype(jnp.float32)
    mixed_back = mixed_low.astype(jnp.float32)
    depth_grad = jnp.stack(
        [
            jnp.sum(
                jnp.where(
                    same_list[offset],
                    mixed_back * gated_wide[:, offset : offset + frame_count],
                    0.0,
                ),
                axis=(0, 1),
            )
            for offset in range(taps)
        ]
    )
    gated_grad = jnp.zeros((row_count, frame_count, width), jnp.float32)
    for offset in range(taps):
        mirror = 2 * half_k - offset
        gated_grad = gated_grad + jnp.where(
            same_list[mirror], depth[offset] * grad_wide[:, mirror : mirror + frame_count], 0.0
        )
    pre_grad = gate_pull(gated_grad.reshape(token_count, width))[0].astype(jnp.bfloat16)
    conv_stream_grad, gain_two, bias_two = conv_pull(mul_back(pre_grad, point_in_w))
    grad_attend = grad_conv + conv_stream_grad

    attend_branch = grad_attend.astype(jnp.bfloat16)
    attended_grad = mul_back(attend_branch, attend_out_w).astype(jnp.bfloat16)
    head_grads = to_heads(attended_grad, 1, row_count, frame_count)[:, 0]
    packed_grad, slope_parts = attend_back(my_slopes, segment_row, packed, head_grads)
    projected_grad = from_heads(packed_grad)
    attend_stream_grad, gain_one, bias_one = attend_pull(mul_back(projected_grad, attend_in_w))
    grad_front = grad_attend + attend_stream_grad
    start_grad, gain_zero, bias_zero, front_up_terms, front_down_terms = half_layer_back(
        grad_front, front_saved, front_up_w, front_down_w
    )
    frames_grad = start_grad.astype(jnp.bfloat16).reshape(row_count, frame_count, width)

    small = jnp.concatenate(
        [
            jnp.stack([gain_zero, gain_one, gain_two, gain_three, gain_four, gain_five]),
            jnp.stack([bias_zero, bias_one, bias_two, bias_three, bias_four, bias_five]),
            depth_grad,
            jnp.zeros((48 - 12 - taps, width), jnp.float32),
        ]
    )
    peers = lax.axis_size("seq")
    small = small.reshape(48, peers, width // peers).transpose(1, 0, 2)
    my_slope_grad = jnp.sum(slope_parts, axis=(0, 2))
    slope_row = jnp.zeros((peers, 1, width // peers), jnp.float32)
    slope_row = lax.dynamic_update_slice(
        slope_row, jnp.broadcast_to(my_slope_grad, (peers, 1, 2)), (0, 0, seq * 2)
    )
    small = lax.dynamic_update_slice(small, slope_row, (0, 12 + taps, 0))

    def wide(terms):
        left, right = merge_cols(*terms[0]), terms[1]
        blocks = right.shape[1] // width
        return [(left, right[:, i * width : (i + 1) * width]) for i in range(blocks)]

    def tall(terms):
        left, right = merge_cols(*terms[0]), terms[1]
        blocks = left.shape[1] // width
        left = left.reshape(token_count, peers, blocks, width // peers)
        return [(left[:, :, i].reshape(token_count, width), right) for i in range(blocks)]

    jobs = wide((attended, attend_branch)) + wide((conv_norm, pre_grad))
    jobs += wide((activated, conv_branch)) + wide((attend_norm, projected_grad))
    jobs += tall(front_down_terms) + wide(front_up_terms)
    shares, share = reduce_grads(
        jnp.stack([job[0] for job in jobs]), jnp.stack([job[1] for job in jobs]), small
    )

    def beside(first, count):
        return jnp.concatenate([shares[first + i] for i in range(count)], axis=1)

    attend_out_grad, point_in_grad, point_out_grad = shares[0], beside(1, 2), shares[3]
    attend_in_grad = beside(4, 3)
    front_down_grad = shares[7:11].reshape(-1, width)
    front_up_grad = beside(11, 4)
    return (
        result,
        frames_grad,
        share[:6],
        share[6:12],
        front_up_grad,
        front_down_grad,
        attend_in_grad,
        attend_out_grad,
        share[12 + taps, : slopes.shape[0]],
        point_in_grad,
        share[12 : 12 + taps],
        point_out_grad,
        rear_up_grad,
        rear_down_grad,
    )


def solution(mesh):
    placed = (
        P("dp", "seq", None),
        P("dp", "seq"),
        P("dp", "seq", None),
        P(None, "seq"),
        P(None, "seq"),
        P("seq", None),
        P("seq", None),
        P("seq", None),
        P("seq", None),
        P(),
        P("seq", None),
        P(None, "seq"),
        P("seq", None),
        P("seq", None),
        P("seq", None),
    )
    sizes = mesh.shape
    staged = sizes["dp"] == 4 and sizes["seq"] == 8
    return jax.shard_map(
        body_staged if staged else body,
        mesh=mesh,
        in_specs=placed,
        out_specs=(
            P("dp", "seq", None),
            P("dp", "seq", None),
            P(None, "seq"),
            P(None, "seq"),
            P("seq", None),
            P("seq", None),
            P("seq", None),
            P("seq", None),
            P(),
            P("seq", None),
            P(None, "seq"),
            P("seq", None),
            P("seq", None),
            P("seq", None),
        ),
        check_vma=False,
    )
```

```python
import jax
import jax.numpy as jnp
from jax import lax
from jax.experimental import pallas as pl
from jax.experimental.pallas import tpu as pltpu
from jax.sharding import PartitionSpec as P


def padded(value, sides, width):
    for axis, dim in sides:
        peers, length = (lax.axis_size(axis), value.shape[dim])
        up = [(i, (i + 1) % peers) for i in range(peers - 1)]
        down = [(j, i) for i, j in up]
        last = lax.slice_in_dim(value, length - width, length, axis=dim)
        leading = lax.slice_in_dim(value, 0, width, axis=dim)
        before = lax.ppermute(last, axis, up)
        after = lax.ppermute(leading, axis, down)
        value = jnp.concatenate([before, value, after], axis=dim)
    return value


def shifted(block, axis, distance):
    devices = range(lax.axis_size(axis))
    route = [((i - distance) % len(devices), i) for i in devices]
    return lax.ppermute(block, axis, route)


def layer_norm(stream, norm_gain, norm_bias):
    average = jnp.mean(stream, axis=-1, keepdims=True)
    centred = stream - average
    spread = jnp.mean(centred * centred, axis=-1, keepdims=True)
    return centred * lax.rsqrt(spread + 1e-05) * norm_gain + norm_bias


def feed_forward(stream, norm_gain, norm_bias, weight_up, weight_down):
    normed, norm_pull = jax.vjp(layer_norm, stream, norm_gain, norm_bias)
    normed_low = normed.astype(jnp.bfloat16)
    inner_act = jnp.dot(normed_low, weight_up, preferred_element_type=jnp.float32)
    hidden, act_pull = jax.vjp(jax.nn.silu, inner_act)
    hidden_low = hidden.astype(jnp.bfloat16)
    branch = jnp.dot(hidden_low, weight_down, preferred_element_type=jnp.float32)
    return (stream + 0.5 * branch, (norm_pull, normed_low, act_pull, hidden_low))


def feed_backward(grad_in, saved_state, weight_up, weight_down):
    norm_pull, normed_low, act_pull, hidden_low = saved_state
    branch_low = (0.5 * grad_in).astype(jnp.bfloat16)
    down_grad = jnp.einsum("tf,td->fd", hidden_low, branch_low, preferred_element_type=jnp.float32)
    hidden_grad = jnp.einsum(
        "td,fd->tf", branch_low, weight_down, preferred_element_type=jnp.float32
    )
    inner_grad = act_pull(hidden_grad)[0].astype(jnp.bfloat16)
    up_grad = jnp.einsum("td,tf->df", normed_low, inner_grad, preferred_element_type=jnp.float32)
    normed_grad = jnp.einsum("tf,df->td", inner_grad, weight_up, preferred_element_type=jnp.float32)
    stream_grad, gain_grad, bias_grad = norm_pull(normed_grad)
    return (grad_in + stream_grad, gain_grad, bias_grad, up_grad, down_grad)


def score_block(query_heads, key_piece, query_start, key_start, query_seg, key_seg, slopes):
    row_count, key_count, feature_count = key_piece.shape
    head_count = query_heads.shape[2]
    head_size = query_heads.shape[3]
    key_heads = key_piece.reshape(row_count, key_count, head_count, head_size)
    raw_score = jnp.einsum(
        "rqhd,rkhd->rqhk", query_heads, key_heads, preferred_element_type=jnp.float32
    ) * head_size ** (-0.5)
    query_place = query_start + jnp.arange(query_heads.shape[1], dtype=jnp.int32)
    key_place = key_start + jnp.arange(key_count, dtype=jnp.int32)
    log_distance = jnp.log1p(jnp.abs(query_place[:, None] - key_place[None, :]).astype(jnp.float32))
    is_live = (query_seg[:, :, None] == key_seg[:, None, :])[:, :, None, :]
    logits = jnp.where(
        is_live, raw_score - slopes[None, None, :, None] * log_distance[None, :, None, :], -1e30
    )
    return (logits, is_live, log_distance, key_heads)


def prob_grads(
    query_heads,
    grad_heads,
    log_sum,
    row_delta,
    query_start,
    query_seg,
    key_piece,
    value_piece,
    key_start,
    key_seg,
    slopes,
):
    logits, is_live, log_distance, key_heads = score_block(
        query_heads, key_piece, query_start, key_start, query_seg, key_seg, slopes
    )
    row_prob = jnp.where(is_live, jnp.exp(logits - log_sum[..., None]), 0.0)
    value_heads = value_piece.reshape(key_heads.shape)
    prob_grad = jnp.einsum(
        "rqhd,rkhd->rqhk", grad_heads, value_heads, preferred_element_type=jnp.float32
    )
    score_grad = row_prob * (prob_grad - row_delta[..., None])
    return (row_prob, score_grad, score_grad.astype(jnp.bfloat16), log_distance, key_heads)


def body(
    frames,
    segments,
    cotangent,
    norm_gains,
    norm_biases,
    front_up,
    front_down,
    attend_in,
    attend_out,
    slopes,
    point_in,
    depthwise,
    point_out,
    rear_up,
    rear_down,
):
    row_count, frame_count, feature_count = frames.shape
    head_count = slopes.shape[0]
    head_size = feature_count // head_count
    token_count = row_count * frame_count
    seq_size = lax.axis_size("seq")
    seq_index = lax.axis_index("seq")
    query_start = seq_index * frame_count
    score_scale = head_size ** (-0.5)
    (
        gains_w,
        biases_w,
        front_up_w,
        front_down_w,
        attend_in_w,
        attend_out_w,
        point_in_w,
        depth_w,
        point_out_w,
        rear_up_w,
        rear_down_w,
    ) = (
        lax.all_gather(norm_gains, "seq", axis=1, tiled=True),
        lax.all_gather(norm_biases, "seq", axis=1, tiled=True),
        lax.all_gather(front_up, "seq", axis=0, tiled=True),
        lax.all_gather(front_down, "seq", axis=0, tiled=True),
        lax.all_gather(attend_in, "seq", axis=0, tiled=True),
        lax.all_gather(attend_out, "seq", axis=0, tiled=True),
        lax.all_gather(point_in, "seq", axis=0, tiled=True),
        lax.all_gather(depthwise, "seq", axis=1, tiled=True),
        lax.all_gather(point_out, "seq", axis=0, tiled=True),
        lax.all_gather(rear_up, "seq", axis=0, tiled=True),
        lax.all_gather(rear_down, "seq", axis=0, tiled=True),
    )
    gains_f = gains_w.astype(jnp.float32)
    biases_f = biases_w.astype(jnp.float32)
    depth_f = depth_w.astype(jnp.float32)
    kernel_len = depth_f.shape[0]
    half_k = kernel_len // 2
    segment_row = lax.all_gather(segments, "seq", axis=1, tiled=True)
    start_stream = frames.astype(jnp.float32).reshape(token_count, feature_count)
    after_front, front_saved = feed_forward(
        start_stream, gains_f[0], biases_f[0], front_up_w, front_down_w
    )
    attend_normed, attend_pull = jax.vjp(layer_norm, after_front, gains_f[1], biases_f[1])
    attend_low = attend_normed.astype(jnp.bfloat16)
    projected = jnp.dot(attend_low, attend_in_w, preferred_element_type=jnp.float32).astype(
        jnp.bfloat16
    )
    query_heads = projected[:, :feature_count].reshape(
        row_count, frame_count, head_count, head_size
    )
    key_low = projected[:, feature_count : 2 * feature_count].reshape(
        row_count, frame_count, feature_count
    )
    value_low = projected[:, 2 * feature_count :].reshape(row_count, frame_count, feature_count)
    stat_shape = (row_count, frame_count, head_count)
    start = jnp.int32(0)
    key_piece = lax.all_gather(key_low, "seq", axis=1, tiled=True)
    value_piece = lax.all_gather(value_low, "seq", axis=1, tiled=True)
    key_seg = segment_row
    row_top = jnp.full(stat_shape, -1e30, jnp.float32)
    logits, is_live, log_distance, key_heads = score_block(
        query_heads, key_piece, query_start, start, segments, key_seg, slopes
    )
    new_top = jnp.maximum(row_top, jnp.max(logits, axis=-1))
    row_exp = jnp.where(is_live, jnp.exp(logits - new_top[..., None]), 0.0)
    value_heads = value_piece.reshape(key_heads.shape)
    accum = jnp.einsum(
        "rqhk,rkhd->rqhd",
        row_exp.astype(jnp.bfloat16),
        value_heads,
        preferred_element_type=jnp.float32,
    )
    row_top, row_total, accum = (new_top, jnp.sum(row_exp, axis=-1), accum)
    attended = accum / row_total[..., None]
    log_sum = row_top + jnp.log(row_total)
    attended_low = attended.reshape(token_count, feature_count).astype(jnp.bfloat16)
    after_attend = after_front + jnp.dot(
        attended_low, attend_out_w, preferred_element_type=jnp.float32
    )
    conv_normed, conv_pull = jax.vjp(layer_norm, after_attend, gains_f[2], biases_f[2])
    conv_low = conv_normed.astype(jnp.bfloat16)
    conv_pre = jnp.dot(conv_low, point_in_w, preferred_element_type=jnp.float32)

    def gate_unit(inner_act):
        return inner_act[:, :feature_count] * jax.nn.sigmoid(inner_act[:, feature_count:])

    gated, gate_pull = jax.vjp(gate_unit, conv_pre)
    gated_low = gated.astype(jnp.bfloat16).reshape(row_count, frame_count, feature_count)
    gated_wide = padded(gated_low, (("seq", 1),), half_k).astype(jnp.float32)
    padded_seg = jnp.pad(segment_row, ((0, 0), (half_k, half_k)), constant_values=-1)
    seg_window = lax.dynamic_slice_in_dim(padded_seg, query_start, frame_count + 2 * half_k, 1)
    same_list = [
        (seg_window[:, offset : offset + frame_count] == segments)[..., None]
        for offset in range(kernel_len)
    ]
    mixed_conv = jnp.zeros((row_count, frame_count, feature_count), jnp.float32)
    for offset in range(kernel_len):
        mixed_conv = mixed_conv + jnp.where(
            same_list[offset], depth_f[offset] * gated_wide[:, offset : offset + frame_count], 0.0
        )

    def norm_silu(stream, norm_gain, norm_bias):
        return jax.nn.silu(layer_norm(stream, norm_gain, norm_bias))

    activated, activated_pull = jax.vjp(
        norm_silu, mixed_conv.reshape(token_count, feature_count), gains_f[3], biases_f[3]
    )
    activated_low = activated.astype(jnp.bfloat16)
    after_conv = after_attend + jnp.dot(
        activated_low, point_out_w, preferred_element_type=jnp.float32
    )
    after_rear, rear_saved = feed_forward(
        after_conv, gains_f[4], biases_f[4], rear_up_w, rear_down_w
    )
    final_out, final_pull = jax.vjp(layer_norm, after_rear, gains_f[5], biases_f[5])
    result = final_out.astype(jnp.bfloat16).reshape(row_count, frame_count, feature_count)
    grad_rear, gain_five, bias_five = final_pull(
        cotangent.astype(jnp.float32).reshape(token_count, feature_count)
    )
    grad_conv, gain_four, bias_four, rear_up_grad, rear_down_grad = feed_backward(
        grad_rear, rear_saved, rear_up_w, rear_down_w
    )
    conv_branch = grad_conv.astype(jnp.bfloat16)
    point_out_grad = jnp.einsum(
        "td,te->de", activated_low, conv_branch, preferred_element_type=jnp.float32
    )
    activated_grad = jnp.einsum(
        "te,de->td", conv_branch, point_out_w, preferred_element_type=jnp.float32
    )
    mixed_grad, gain_three, bias_three = activated_pull(activated_grad)
    mixed_low = mixed_grad.astype(jnp.bfloat16).reshape(row_count, frame_count, feature_count)
    grad_wide = padded(mixed_low, (("seq", 1),), half_k).astype(jnp.float32)
    mixed_back = mixed_low.astype(jnp.float32)
    depth_rows = [
        jnp.sum(
            jnp.where(
                same_list[offset], mixed_back * gated_wide[:, offset : offset + frame_count], 0.0
            ),
            axis=(0, 1),
        )
        for offset in range(kernel_len)
    ]
    depthwise_grad = jnp.stack(depth_rows)
    gated_grad = jnp.zeros((row_count, frame_count, feature_count), jnp.float32)
    for offset in range(kernel_len):
        mirror = 2 * half_k - offset
        gated_grad = gated_grad + jnp.where(
            same_list[mirror], depth_f[offset] * grad_wide[:, mirror : mirror + frame_count], 0.0
        )
    pre_grad = gate_pull(gated_grad.reshape(token_count, feature_count))[0].astype(jnp.bfloat16)
    point_in_grad = jnp.einsum("td,tc->dc", conv_low, pre_grad, preferred_element_type=jnp.float32)
    conv_normed_grad = jnp.einsum(
        "tc,dc->td", pre_grad, point_in_w, preferred_element_type=jnp.float32
    )
    conv_stream_grad, gain_two, bias_two = conv_pull(conv_normed_grad)
    grad_attend = grad_conv + conv_stream_grad
    attend_branch = grad_attend.astype(jnp.bfloat16)
    attend_out_grad = jnp.einsum(
        "td,te->de", attended_low, attend_branch, preferred_element_type=jnp.float32
    )
    attended_grad = jnp.einsum(
        "te,de->td", attend_branch, attend_out_w, preferred_element_type=jnp.float32
    )
    grad_heads = attended_grad.astype(jnp.bfloat16).reshape(
        row_count, frame_count, head_count, head_size
    )
    row_delta = jnp.sum(grad_heads.astype(jnp.float32) * attended, axis=-1)

    def query_terms(state, key_piece, value_piece, start, key_seg):
        query_grad, slope_grad = state
        row_prob, score_grad, score_low, log_distance, key_heads = prob_grads(
            query_heads,
            grad_heads,
            log_sum,
            row_delta,
            query_start,
            segments,
            key_piece,
            value_piece,
            start,
            key_seg,
            slopes,
        )
        query_grad = (
            query_grad
            + jnp.einsum(
                "rqhk,rkhd->rqhd", score_low, key_heads, preferred_element_type=jnp.float32
            )
            * score_scale
        )
        slope_grad = slope_grad - jnp.einsum("rqhk,qk->h", score_grad, log_distance)
        return (query_grad, slope_grad, row_prob, score_low)

    query_zero = jnp.zeros((row_count, frame_count, head_count, head_size), jnp.float32)
    slope_zero = jnp.zeros((head_count,), jnp.float32)
    local_zero = jnp.zeros((row_count, frame_count, feature_count), jnp.float32)

    def accumulate(step, query_grad, slope_grad, pair_kv, pair_acc):
        owner = (seq_index + step) % seq_size
        start = owner * frame_count
        key_seg = lax.dynamic_slice_in_dim(segment_row, start, frame_count, 1)
        grad_q = query_grad
        grad_s = slope_grad
        key_acc = pair_acc[0]
        value_acc = pair_acc[1]
        grad_q, grad_s, row_prob, score_low = query_terms(
            (grad_q, grad_s), pair_kv[0], pair_kv[1], start, key_seg
        )
        key_acc = key_acc + (
            jnp.einsum(
                "rqhk,rqhd->rkhd", score_low, query_heads, preferred_element_type=jnp.float32
            )
            * score_scale
        ).reshape(row_count, frame_count, feature_count)
        value_acc = value_acc + jnp.einsum(
            "rqhk,rqhd->rkhd",
            row_prob.astype(jnp.bfloat16),
            grad_heads,
            preferred_element_type=jnp.float32,
        ).reshape(row_count, frame_count, feature_count)
        query_grad, slope_grad, key_acc, value_acc = (grad_q, grad_s, key_acc, value_acc)
        pair_acc = shifted(jnp.stack([key_acc, value_acc]).astype(jnp.bfloat16), "seq", -1).astype(
            jnp.float32
        )
        return (query_grad, slope_grad, pair_acc)

    def cycle_step(step, carry):
        query_grad, slope_grad, pair_kv, pair_acc = carry
        next_kv = shifted(pair_kv, "seq", -1)
        query_grad, slope_grad, pair_acc = accumulate(
            step, query_grad, slope_grad, pair_kv, pair_acc
        )
        return (query_grad, slope_grad, next_kv, pair_acc)

    pair_start = jnp.stack([key_low, value_low])
    acc_start = jnp.stack([local_zero, local_zero])
    query_grad, slope_grad, pair_kv, pair_acc = lax.fori_loop(
        0, seq_size - 1, cycle_step, (query_zero, slope_zero, pair_start, acc_start)
    )
    query_grad, slope_grad, pair_acc = accumulate(
        seq_size - 1, query_grad, slope_grad, pair_kv, pair_acc
    )
    key_grad = pair_acc[0]
    value_grad = pair_acc[1]
    projected_grad = jnp.concatenate(
        [
            query_grad.reshape(token_count, feature_count),
            key_grad.reshape(token_count, feature_count),
            value_grad.reshape(token_count, feature_count),
        ],
        axis=1,
    ).astype(jnp.bfloat16)
    attend_in_grad = jnp.einsum(
        "td,tc->dc", attend_low, projected_grad, preferred_element_type=jnp.float32
    )
    attend_normed_grad = jnp.einsum(
        "tc,dc->td", projected_grad, attend_in_w, preferred_element_type=jnp.float32
    )
    attend_stream_grad, gain_one, bias_one = attend_pull(attend_normed_grad)
    grad_front = grad_attend + attend_stream_grad
    start_grad, gain_zero, bias_zero, front_up_grad, front_down_grad = feed_backward(
        grad_front, front_saved, front_up_w, front_down_w
    )
    frames_grad = start_grad.astype(jnp.bfloat16).reshape(row_count, frame_count, feature_count)
    gains_local = jnp.stack([gain_zero, gain_one, gain_two, gain_three, gain_four, gain_five])
    biases_local = jnp.stack([bias_zero, bias_one, bias_two, bias_three, bias_four, bias_five])
    slope_rows = jnp.broadcast_to(slope_grad[None, :], (seq_size, head_count))
    shares = (
        lax.psum_scatter(
            gains_local.astype(jnp.bfloat16), "seq", scatter_dimension=1, tiled=True
        ).astype(jnp.float32),
        lax.psum_scatter(
            biases_local.astype(jnp.bfloat16), "seq", scatter_dimension=1, tiled=True
        ).astype(jnp.float32),
        lax.psum_scatter(
            front_up_grad.astype(jnp.bfloat16), "seq", scatter_dimension=0, tiled=True
        ).astype(jnp.float32),
        lax.psum_scatter(
            front_down_grad.astype(jnp.bfloat16), "seq", scatter_dimension=0, tiled=True
        ).astype(jnp.float32),
        lax.psum_scatter(
            attend_in_grad.astype(jnp.bfloat16), "seq", scatter_dimension=0, tiled=True
        ).astype(jnp.float32),
        lax.psum_scatter(
            attend_out_grad.astype(jnp.bfloat16), "seq", scatter_dimension=0, tiled=True
        ).astype(jnp.float32),
        lax.psum_scatter(
            slope_rows.astype(jnp.bfloat16), "seq", scatter_dimension=0, tiled=True
        ).astype(jnp.float32),
        lax.psum_scatter(
            point_in_grad.astype(jnp.bfloat16), "seq", scatter_dimension=0, tiled=True
        ).astype(jnp.float32),
        lax.psum_scatter(
            depthwise_grad.astype(jnp.bfloat16), "seq", scatter_dimension=1, tiled=True
        ).astype(jnp.float32),
        lax.psum_scatter(
            point_out_grad.astype(jnp.bfloat16), "seq", scatter_dimension=0, tiled=True
        ).astype(jnp.float32),
        lax.psum_scatter(
            rear_up_grad.astype(jnp.bfloat16), "seq", scatter_dimension=0, tiled=True
        ).astype(jnp.float32),
        lax.psum_scatter(
            rear_down_grad.astype(jnp.bfloat16), "seq", scatter_dimension=0, tiled=True
        ).astype(jnp.float32),
    )
    totals = (
        lax.psum(shares[0].astype(jnp.bfloat16), "dp").astype(jnp.float32),
        lax.psum(shares[1].astype(jnp.bfloat16), "dp").astype(jnp.float32),
        lax.psum(shares[2].astype(jnp.bfloat16), "dp").astype(jnp.float32),
        lax.psum(shares[3].astype(jnp.bfloat16), "dp").astype(jnp.float32),
        lax.psum(shares[4].astype(jnp.bfloat16), "dp").astype(jnp.float32),
        lax.psum(shares[5].astype(jnp.bfloat16), "dp").astype(jnp.float32),
        lax.psum(shares[6].astype(jnp.bfloat16), "dp").astype(jnp.float32),
        lax.psum(shares[7].astype(jnp.bfloat16), "dp").astype(jnp.float32),
        lax.psum(shares[8].astype(jnp.bfloat16), "dp").astype(jnp.float32),
        lax.psum(shares[9].astype(jnp.bfloat16), "dp").astype(jnp.float32),
        lax.psum(shares[10].astype(jnp.bfloat16), "dp").astype(jnp.float32),
        lax.psum(shares[11].astype(jnp.bfloat16), "dp").astype(jnp.float32),
    )
    return (
        result,
        frames_grad,
        totals[0],
        totals[1],
        totals[2],
        totals[3],
        totals[4],
        totals[5],
        totals[6].reshape(head_count),
        totals[7],
        totals[8],
        totals[9],
        totals[10],
        totals[11],
    )


def place():
    dp, seq = lax.axis_index("dp"), lax.axis_index("seq")
    return dp // 2, dp % 2, seq // 2, seq % 2


QUERIES = 256


def log_distance_block(length, start):
    keys = lax.broadcasted_iota(jnp.int32, (length, QUERIES), 0)
    queries = lax.broadcasted_iota(jnp.int32, (length, QUERIES), 1) + start
    return jnp.log(1.0 + jnp.abs(keys - queries).astype(jnp.float32))


def head_lanes(value, head, scale=1.0):
    lane = lax.broadcasted_iota(jnp.int32, value.shape, 1)
    mine = (lane >= 64 * head) & (lane < 64 * head + 64)
    return jnp.where(mine, value * jnp.asarray(scale, value.dtype), jnp.zeros_like(value))


def nt(a, b):
    return lax.dot_general(a, b, (((1,), (1,)), ((), ())), preferred_element_type=jnp.float32)


MESH_ID = pl.DeviceIdType.MESH
PIECE = 32
HALO = 16
UP, DOWN, PROJECT, ATTEND_OUT, POINT_IN, POINT_OUT, REAR_UP, REAR_DOWN = 0, 4, 8, 11, 12, 14, 15, 19
CHUNKS = 23
LEAD = 3
STAGE = 1
STEP = 4 * STAGE
VECTORS = 48


def low(value):
    return value.astype(jnp.bfloat16)


def f32(value):
    return value.astype(jnp.float32)


def dot(a, b):
    return jnp.dot(a, b, preferred_element_type=jnp.float32)


def norm_rows(v, gain, bias):
    centred = v - jnp.mean(v, axis=-1, keepdims=True)
    spread = jnp.mean(centred * centred, axis=-1, keepdims=True)
    return centred * lax.rsqrt(spread + 1e-05) * gain + bias


def logistic(v):
    return 1.0 / (1.0 + jnp.exp(-v))


def remote_copy(src, dst, send_sem, recv_sem, there):
    return pltpu.make_async_remote_copy(
        src_ref=src,
        dst_ref=dst,
        send_sem=send_sem,
        recv_sem=recv_sem,
        device_id=there,
        device_id_type=MESH_ID,
    )


def attend_block(packed, slopes, seg_cols, seg_rows, row, block, length):
    distance = log_distance_block(length, block * QUERIES)
    same = seg_cols == seg_rows
    q = packed[pl.ds(block * 2, 2), 0, row].reshape(QUERIES, 128)
    k = packed[:, 1, row].reshape(length, 128)
    value_t = packed[:, 2, row].reshape(length, 128).T
    outs = []
    for head in range(2):
        logit = nt(k, head_lanes(q, head, 0.125)) - slopes[head] * distance
        logit = jnp.where(same, logit, -1e30)
        top = jnp.max(logit, axis=0, keepdims=True)
        power = jnp.exp(logit - top)
        total = jnp.sum(power, axis=0, keepdims=True)
        out = dot(value_t, low(power))
        outs.append(out[64 * head : 64 * head + 64] / total)
    return low(jnp.concatenate(outs, axis=0).T)


def forward_kernel(*refs):
    shards, vec, seg, frames, slopes = refs[:5]
    (full, vec_all, seg_all, norm0, pre_f, hid_f, after_front, norm1, packed, attended, after_attend) = refs[5:16]
    (norm2, conv_pre, gated, mixed, act, after_conv, norm4, pre_r, hid_r, after_rear) = refs[16:26]
    (wbuf, vectors, pk_out, att_out, att_in, gated_f, seg_plane, seg_cols, seg_rows, acc) = refs[26:36]
    (gather_sem, own_sem, small_sem, pk_sem, att_sem, halo_sem, load_sem) = refs[36:]
    y, x, z, core = place()
    dp, seq = y * 2 + x, z * 2 + core
    rows, width = 2, 1024
    frame_count = 128
    length = 8 * frame_count
    over_x = (y * 2 + 1 - x, seq)
    over_y = ((1 - y) * 2 + x, seq)
    over_core = (dp, z * 2 + 1 - core)

    def peer(k):
        return lax.rem(seq + k, 8)

    barrier = pltpu.get_barrier_semaphore()
    for there in [(dp, peer(k)) for k in range(1, 8)] + [over_x, over_y]:
        pl.semaphore_signal(barrier, inc=1, device_id=there, device_id_type=MESH_ID)
    pl.semaphore_wait(barrier, 9)

    q_own, q_x, q_y = PIECE * dp, PIECE * (y * 2 + 1 - x), PIECE * ((1 - y) * 2 + x)

    def travel(kind, t, k, first, rows_, there, src=None):
        source = seq if src is not None else lax.rem(z - k + 4, 4) * 2 + core
        where = full.at[t, source, pl.ds(pl.multiple_of(first, 16), rows_)]
        return remote_copy(
            where if src is None else src,
            where,
            gather_sem.at[0, kind, t, k - 1],
            gather_sem.at[1, kind, t, k - 1],
            there,
        )

    def line(t, k):
        src = shards.at[t, pl.ds(pl.multiple_of(q_own, 16), PIECE)]
        return travel(0, t, k, q_own, PIECE, (dp, lax.rem(z + k, 4) * 2 + core), src)

    def to_x(t, k):
        return travel(1, t, k, q_own, PIECE, over_x)

    def to_y(t, k):
        return travel(2, t, k, q_own, PIECE, over_y)

    def on_x(t, k):
        return travel(3, t, k, q_y, PIECE // 2, over_x)

    def on_y(t, k):
        return travel(4, t, k, q_x + PIECE // 2, PIECE // 2, over_y)

    def to_core(t, k):
        return travel(5, t, k, 0, 4 * PIECE, over_core)

    def own_to_core():
        return remote_copy(shards, full.at[:, seq], own_sem.at[0], own_sem.at[1], over_core)

    def own_to_full():
        return pltpu.make_async_copy(shards, full.at[:, seq], own_sem.at[2])

    def small_copies():
        copies = []
        for k in range(1, 8):
            for i, (src, dst) in enumerate(((vec, vec_all), (seg, seg_all))):
                copies.append(
                    remote_copy(
                        src,
                        dst.at[seq],
                        small_sem.at[0, i, k - 1],
                        small_sem.at[1, i, k - 1],
                        (dp, peer(k)),
                    )
                )
        return copies

    for copy in small_copies():
        copy.start()
    own_to_core().start()
    own_to_full().start()
    vec_all[seq] = vec[...]
    seg_all[seq] = seg[...]
    def relay(t):
        where = full.at[t, lax.rem(z + 2, 4) * 2 + core, pl.ds(pl.multiple_of(q_own, 16), PIECE)]
        return remote_copy(
            where,
            where,
            gather_sem.at[0, 6, t, 0],
            gather_sem.at[1, 0, t, 2 * z - 2],
            (dp, 3 * (z - 1) * 2 + core),
        )

    def direct(k):
        return {1: z != 3, 2: z >= 0, 3: z != 0}[k]

    def in_time(k):
        return {1: z != 0, 2: z >= 0, 3: z != 3}[k]

    relays = (z == 1) | (z == 2)

    def start_line(t):
        for k in (1, 2, 3):

            @pl.when(direct(k))
            def _():
                line(t, k).start()

    def arrived(t, k):
        line(t, k).wait_recv()
        to_x(t, k).start()
        to_y(t, k).start()

    for t in range(LEAD):
        start_line(t)

    def gather_step(step):
        @pl.when(step + LEAD < CHUNKS)
        def _():
            start_line(step + LEAD)

        @pl.when(step < CHUNKS)
        def _():
            for k in (2, 1, 3):

                @pl.when(in_time(k))
                def _():
                    arrived(step, k)

                if k == 2:

                    @pl.when(relays)
                    def _():
                        relay(step).start()

        late = step - STAGE

        @pl.when((late >= 0) & (late < CHUNKS))
        def _():
            for k in (1, 3):

                @pl.when(jnp.logical_not(in_time(k)))
                def _():
                    arrived(late, k)

        second, third, last = step - 2 * STAGE, step - 3 * STAGE, step - 4 * STAGE

        @pl.when((second >= 0) & (second < CHUNKS))
        def _():
            for k in (1, 2, 3):
                to_y(second, k).wait_recv()
                on_x(second, k).start()
                to_x(second, k).wait_recv()
                on_y(second, k).start()

        @pl.when((third >= 0) & (third < CHUNKS))
        def _():
            for k in (1, 2, 3):
                on_x(third, k).wait_recv()
                on_y(third, k).wait_recv()
                to_core(third, k).start()

        @pl.when((last >= 0) & (last < CHUNKS))
        def _():
            for k in (1, 2, 3):
                to_core(last, k).wait_recv()

    def load(u):
        return pltpu.make_async_copy(full.at[u], wbuf.at[lax.rem(u, 2)], load_sem.at[lax.rem(u, 2)])

    def weight(u):
        load(u).wait()
        return wbuf[lax.rem(u, 2)].reshape(width, width)

    def vector(i):
        return vectors[i : i + 1, :]

    def norm(v, i):
        return low(norm_rows(v, vector(i), vector(6 + i)))

    def prepare():
        own_to_full().wait()
        own_to_core().wait()
        for copy in small_copies():
            copy.wait()
        for s in range(8):
            vectors[:, s * 128 : s * 128 + 128] = f32(vec_all[s])
            columns = f32(seg_all[s]).T
            for r in range(rows):
                seg_cols[r, s * 128 : s * 128 + 128, :] = columns[:, r : r + 1]
                seg_rows[r : r + 1, s * 128 : s * 128 + 128] = f32(seg_all[s, r : r + 1, :])
        before = jnp.where(seq > 0, f32(seg_all[lax.max(seq - 1, 0)]), -1.0).T
        middle = f32(seg_all[seq]).T
        after = jnp.where(seq < 7, f32(seg_all[lax.min(seq + 1, 7)]), -1.0).T
        for r in range(rows):
            for first, col in (
                (0, before[frame_count - HALO :, r : r + 1]),
                (HALO, middle[:, r : r + 1]),
                (HALO + frame_count, after[:HALO, r : r + 1]),
            ):
                seg_plane[r, first : first + col.shape[0], :] = jnp.broadcast_to(col, (col.shape[0], 128))
        gated[:, :HALO] = jnp.zeros((rows, HALO, width), jnp.bfloat16)
        gated[:, HALO + frame_count :] = jnp.zeros((rows, HALO, width), jnp.bfloat16)
        norm0[...] = norm(f32(frames[...]), 0)

    def up(u, j, source, pre, hid):
        value = dot(source[...], weight(u))
        pre[j] = low(value)
        hid[j] = low(value * logistic(value))

    def down(u, j, stream, hid, target):
        value = dot(hid[j], weight(u))

        @pl.when(j == 0)
        def _():
            acc[...] = value

        @pl.when(j > 0)
        def _():
            acc[...] += value

        @pl.when(j == 3)
        def _():
            target[...] = f32(stream[...]) + 0.5 * acc[...]

    def pk_copy(c, k, recv=False):
        there = peer(k)
        return remote_copy(
            pk_out.at[there, c],
            packed.at[there if recv else seq, c],
            pk_sem.at[0, there, c],
            pk_sem.at[1, there if recv else seq, c],
            (dp, there),
        )

    def project(u, c):
        value = low(dot(norm1[...], weight(u)))
        for s in range(8):
            pk_out[s, c] = value[:, s * 128 : s * 128 + 128].reshape(rows, frame_count, 128)
        packed[seq, c] = pk_out[seq, c]
        for k in range(1, 8):
            pk_copy(c, k).start()

    def att_copy(b, r, recv=False):
        return remote_copy(
            att_out.at[b, r],
            att_in.at[b if recv else seq, r],
            att_sem.at[0, b, r],
            att_sem.at[1, b if recv else seq, r],
            (dp, b),
        )

    def attend_step(i):
        row, block = i // 4, lax.rem(i, 4)
        cols = seg_cols[row]
        first = pl.multiple_of(block * QUERIES, QUERIES)
        out = attend_block(
            packed, slopes, cols, seg_rows[pl.ds(row, 1), pl.ds(first, QUERIES)], row, block, length
        )
        for half in range(2):
            b = block * 2 + half
            att_out[b, row] = out[half * 128 : half * 128 + 128]

            @pl.when(b != seq)
            def _():
                att_copy(b, row).start()

            @pl.when(b == seq)
            def _():
                att_in[b, row] = out[half * 128 : half * 128 + 128]

    def halo_copy(side):
        if side == 0:
            src, dst, there = gated.at[:, pl.ds(HALO, HALO)], gated.at[:, pl.ds(HALO + frame_count, HALO)], lax.rem(seq + 7, 8)
        else:
            src, dst, there = gated.at[:, pl.ds(frame_count, HALO)], gated.at[:, pl.ds(0, HALO)], lax.rem(seq + 1, 8)
        return remote_copy(src, dst, halo_sem.at[0, side], halo_sem.at[1, side], (dp, there))

    def convolve():
        @pl.when(seq > 0)
        def _():
            halo_copy(0).wait_send()
            halo_copy(1).wait_recv()

        @pl.when(seq < 7)
        def _():
            halo_copy(1).wait_send()
            halo_copy(0).wait_recv()

        gated_f[...] = f32(gated[...])

        def lanes(i, _):
            at = pl.ds(pl.multiple_of(i * 128, 128), 128)
            for r in range(rows):
                own = seg_plane[r, HALO : HALO + frame_count, :]
                total = jnp.zeros((frame_count, 128), jnp.float32)
                for tap in range(31):
                    first = tap + HALO - 15
                    same = seg_plane[r, first : first + frame_count, :] == own
                    term = gated_f[r, first : first + frame_count, at] * vectors[12 + tap : 13 + tap, at]
                    total = total + jnp.where(same, term, 0.0)
                mixed[r * frame_count : (r + 1) * frame_count, at] = total
            return 0

        lax.fori_loop(0, width // 128, lanes, 0)

    def step_work(step, _):
        gather_step(step)

        now = step - STEP

        def at(first, count=1):
            return pl.when((now >= first) & (now < first + count))

        @at(0)
        def _():
            prepare()

        @at(1, 4)
        def _():
            up(now - 1, now - 1, norm0, pre_f, hid_f)

        @at(5, 4)
        def _():
            down(now - 1, now - 5, frames, hid_f, after_front)

        @at(9, 3)
        def _():
            @pl.when(now == 9)
            def _():
                norm1[...] = norm(after_front[...], 1)

            project(now - 1, now - 9)

        @at(13)
        def _():
            for c in range(3):
                for k in range(1, 8):
                    pk_copy(c, k, True).wait_recv()

        @at(13, 4)
        def _():
            attend_step((now - 13) * 2)
            attend_step((now - 13) * 2 + 1)

        @at(17)
        def _():
            for r in range(rows):
                for k in range(1, 8):
                    att_copy(peer(k), r, True).wait_recv()
            for s in range(8):
                attended[:, s * 128 : s * 128 + 128] = att_in[s].reshape(rows * frame_count, 128)
            after_attend[...] = after_front[...] + dot(attended[...], weight(ATTEND_OUT))
            norm2[...] = norm(after_attend[...], 2)

        @at(18)
        def _():
            acc[...] = dot(norm2[...], weight(POINT_IN))
            conv_pre[0] = low(acc[...])

        @at(19)
        def _():
            gate = dot(norm2[...], weight(POINT_IN + 1))
            conv_pre[1] = low(gate)
            value = low(acc[...] * logistic(gate))
            gated[:, HALO : HALO + frame_count] = value.reshape(rows, frame_count, width)

            @pl.when(seq > 0)
            def _():
                halo_copy(0).start()

            @pl.when(seq < 7)
            def _():
                halo_copy(1).start()

        @at(20)
        def _():
            convolve()
            value = norm_rows(mixed[...], vector(3), vector(9))
            act[...] = low(value * logistic(value))
            after_conv[...] = after_attend[...] + dot(act[...], weight(POINT_OUT))
            norm4[...] = norm(after_conv[...], 4)

        @at(21, 4)
        def _():
            up(now - 21 + REAR_UP, now - 21, norm4, pre_r, hid_r)

        @at(25, 4)
        def _():
            down(now - 25 + REAR_DOWN, now - 25, after_conv, hid_r, after_rear)

        @at(0, 11)
        def _():
            load(now - 0).start()

        @at(16, 12)
        def _():
            load(now - 5).start()

        return 0

    lax.fori_loop(0, STEP + 29, step_work, 0)

    def drain(t, _):
        for kind in (to_x, to_y, on_x, on_y, to_core):
            for k in (1, 2, 3):
                kind(t, k).wait_send()
        for k in (1, 2, 3):

            @pl.when(direct(k))
            def _():
                line(t, k).wait_send()

        @pl.when(relays)
        def _():
            relay(t).wait_send()

        return 0

    lax.fori_loop(0, CHUNKS, drain, 0)
    for c in range(3):
        for k in range(1, 8):
            pk_copy(c, k).wait_send()
    for r in range(rows):
        for k in range(1, 8):
            att_copy(peer(k), r).wait_send()


def forward_layer(shards, vec, seg, frames, slopes):
    bf16, tokens, width = jnp.bfloat16, frames.shape[0], frames.shape[1]
    dma = pltpu.SemaphoreType.DMA

    def shape(kind, *sizes):
        return jax.ShapeDtypeStruct(sizes, kind)

    plain, single = shape(bf16, tokens, width), shape(jnp.float32, tokens, width)
    four = shape(bf16, 4, tokens, width)
    outs = [
        shape(bf16, CHUNKS, 8, 128, width),
        shape(bf16, 8, VECTORS, 128),
        shape(jnp.int32, 8, 8, 128),
        plain,
        four,
        four,
        single,
        plain,
        shape(bf16, 8, 3, 2, 128, 128),
        plain,
        single,
        plain,
        shape(bf16, 2, tokens, width),
        shape(bf16, 2, 128 + 2 * HALO, width),
        single,
        plain,
        single,
        plain,
        four,
        four,
        single,
    ]
    vmem, hbm = pl.BlockSpec(memory_space=pltpu.VMEM), pl.BlockSpec(memory_space=pltpu.HBM)
    return pl.pallas_call(
        forward_kernel,
        in_specs=[vmem, vmem, vmem, vmem, pl.BlockSpec(memory_space=pltpu.SMEM)],
        out_specs=[hbm] + [vmem] * (len(outs) - 1),
        out_shape=outs,
        scratch_shapes=[
            pltpu.VMEM((2, 8, 128, width), bf16),
            pltpu.VMEM((VECTORS, width), jnp.float32),
            pltpu.VMEM((8, 3, 2, 128, 128), bf16),
            pltpu.VMEM((8, 2, 128, 128), bf16),
            pltpu.VMEM((8, 2, 128, 128), bf16),
            pltpu.VMEM((2, 128 + 2 * HALO, width), jnp.float32),
            pltpu.VMEM((2, 128 + 2 * HALO, 128), jnp.float32),
            pltpu.VMEM((2, 1024, 1), jnp.float32),
            pltpu.VMEM((8, 1024), jnp.float32),
            pltpu.VMEM((tokens, width), jnp.float32),
            dma((2, 7, CHUNKS, 3)),
            dma((3,)),
            dma((2, 2, 7)),
            dma((2, 8, 3)),
            dma((2, 8, 2)),
            dma((2, 2)),
            dma((2,)),
        ],
        compiler_params=pltpu.CompilerParams(
            collective_id=0, has_side_effects=True, vmem_limit_bytes=60 * 2**20
        ),
        name="forward_layer",
    )(shards, vec, seg, frames, slopes)


JOB_RU, JOB_PO, JOB_PI, JOB_AO, JOB_P, JOB_FD, JOB_FU, JOBS = 4, 8, 9, 11, 12, 15, 19, 23
RING = 4
OUT_LAG = 6


def silu_slope(pre, grad):
    gate = logistic(pre)
    return grad * gate * (1.0 + pre * (1.0 - gate))


def tn(a, b):
    return lax.dot_general(a, b, (((0,), (0,)), ((), ())), preferred_element_type=jnp.float32)


def backward_kernel(*refs):
    (full, vec_all, seg_all, norm0, pre_f, hid_f, after_front, norm1, packed, attended, after_attend) = refs[:11]
    (norm2, conv_pre, gated, mixed, act, after_conv, norm4, pre_r, hid_r, after_rear) = refs[11:21]
    (frames, cotangent, slopes) = refs[21:24]
    (result, frames_grad, shares, vec_out) = refs[24:28]
    (wbuf, pre_buf, hid_buf, v_buf, vectors, small, left, right) = refs[28:36]
    (branch, pre_grads, conv_branch, gate_grads, attend_branch, parts) = refs[36:42]
    (grad, total, gated_f, mixed_w, mixed_f, seg_plane, seg_cols, seg_rows) = refs[42:50]
    (g_out, g_in, p_out, p_in, key_sum, value_sum, slope_sum, out_buf) = refs[50:58]
    (g_buf, h_buf, a_buf, b_buf, q_buf, core_in, a_in, b_in, a2_in, b2_in, z_in, o_buf) = refs[58:70]
    (vec_send, vec_in, vec_dp) = refs[70:73]
    (sem, vec_sem, load_sem, pre_sem, hid_sem, v_sem, ga_sem, pk_sem, halo_sem, out_sem) = refs[73:]
    y, x, z, core = place()
    dp, seq = y * 2 + x, z * 2 + core
    rows, width, frame_count = 2, 1024, 128
    length = 8 * frame_count
    over_x = (y * 2 + 1 - x, seq)
    over_y = ((1 - y) * 2 + x, seq)
    over_core = (dp, z * 2 + 1 - core)

    def peer(k):
        return lax.rem(seq + k, 8)

    def dp_peer(k):
        return (lax.rem(dp + k, 4), seq)

    mixed_w[:, :HALO] = jnp.zeros((rows, HALO, width), jnp.bfloat16)
    mixed_w[:, HALO + frame_count :] = jnp.zeros((rows, HALO, width), jnp.bfloat16)
    barrier = pltpu.get_barrier_semaphore()
    for there in [(dp, peer(k)) for k in range(1, 8)] + [dp_peer(k) for k in range(1, 4)]:
        pl.semaphore_signal(barrier, inc=1, device_id=there, device_id_type=MESH_ID)
    pl.semaphore_wait(barrier, 10)

    def remote(src, dst, t, slot, there):
        return remote_copy(
            src, dst, sem.at[0, slot, lax.rem(t, RING)], sem.at[1, slot, lax.rem(t, RING)], there
        )

    def core_copies(t, r):
        return [remote(g_buf.at[1], core_in.at[r], t, 0, over_core)]

    def first_copies(t, r):
        return [
            remote(h_buf.at[pl.ds(0, 2), :, 1 - x], a_in.at[r], t, 1, over_x),
            remote(h_buf.at[pl.ds(2, 2), 1 - y], b_in.at[r], t, 2, over_y),
        ]

    def second_copies(t, r):
        return [
            remote(a_buf.at[:, 1 - y], a2_in.at[r], t, 3, over_y),
            remote(b_buf.at[:, 1 - x], b2_in.at[r], t, 4, over_x),
        ]

    def line_copies(t, r):
        copies = []
        for k in (1, 2, 3):
            to = lax.rem(z + k, 4)
            copies.append(remote(q_buf.at[to], z_in.at[r, k - 1], t, 4 + k, (dp, to * 2 + core)))
        return copies

    def share_copies(t, r):
        where = o_buf.at[r, dp]
        return [remote(where, where, t, 8, over_x), remote(where, where, t, 9, over_y)]

    def across_copies(t, r):
        one = o_buf.at[r, (1 - y) * 2 + x, pl.ds(0, PIECE // 2)]
        two = o_buf.at[r, y * 2 + 1 - x, pl.ds(PIECE // 2, PIECE // 2)]
        return [remote(one, one, t, 10, over_x), remote(two, two, t, 11, over_y)]

    def out_copy(t):
        slot = lax.rem(t, 2)
        return pltpu.make_async_copy(out_buf.at[slot], shares.at[t], out_sem.at[slot])

    def finish(copies):
        for copy in copies:
            copy.wait()

    def begin(copies):
        for copy in copies:
            copy.start()

    def write_out(t, r):
        finish(across_copies(t, r))

        @pl.when(t >= 2)
        def _():
            out_copy(t - 2).wait()

        out_buf[lax.rem(t, 2)] = f32(o_buf[r].reshape(128, width))
        out_copy(t).start()

    def pass_on(t, r):
        finish(share_copies(t, r))
        begin(across_copies(t, r))

    def total_line(t, r):
        finish(line_copies(t, r))
        value = f32(q_buf[z]) + f32(z_in[r, 0]) + f32(z_in[r, 1]) + f32(z_in[r, 2])
        o_buf[r, dp] = low(value)
        begin(share_copies(t, r))

    def total_second(t, r):
        finish(second_copies(t, r))
        q_buf[0:2] = low(f32(a_buf[:, y]) + f32(a2_in[r]))
        q_buf[2:4] = low(f32(b_buf[:, x]) + f32(b2_in[r]))
        begin(line_copies(t, r))

    def total_first(t, r):
        finish(first_copies(t, r))
        a_buf[...] = low(f32(h_buf[0:2, :, x]) + f32(a_in[r]))
        b_buf[...] = low(f32(h_buf[2:4, y]) + f32(b_in[r]))
        begin(second_copies(t, r))

    def total_core(t, r):
        finish(core_copies(t, r))
        for i in range(4):
            value = low(f32(g_buf[0, i]) + f32(core_in[r, i]))
            h_buf[i] = value.reshape(2, 2, PIECE, width)
        begin(first_copies(t, r))

    def product(t, r):
        for i in range(8):
            part = tn(left[:, 128 * i : 128 * i + 128], right[...])
            g_buf[lax.rem(core + i, 2), i // 2] = low(part)
        begin(core_copies(t, r))

    sums = [total_core, total_first, total_second, total_line, pass_on, write_out]

    def sum_step(step):
        for depth in reversed(range(1, 7)):
            t = step - depth

            @pl.when((t >= 0) & (t < JOBS))
            def _(t=t, depth=depth):
                sums[depth - 1](t, lax.rem(t, RING))

    def load(i, u):
        return pltpu.make_async_copy(full.at[u], wbuf.at[i], load_sem.at[i])

    def weight(i, u):
        load(i, u).wait()
        return wbuf[i].reshape(width, width)

    def fetch_pre(source, j):
        return pltpu.make_async_copy(source.at[j], pre_buf, pre_sem.at[0])

    def fetch_hid(source, j):
        return pltpu.make_async_copy(source.at[j], hid_buf, hid_sem.at[0])

    def fetch(source):
        return pltpu.make_async_copy(source, v_buf, v_sem.at[0])

    def vector(i):
        return vectors[i : i + 1, :]

    def norm_back(v, i, dy):
        centred = v - jnp.mean(v, axis=-1, keepdims=True)
        rstd = lax.rsqrt(jnp.mean(centred * centred, axis=-1, keepdims=True) + 1e-05)
        n = centred * rstd
        small[i : i + 1, :] = jnp.sum(dy * n, axis=0, keepdims=True)
        small[6 + i : 7 + i, :] = jnp.sum(dy, axis=0, keepdims=True)
        dn = dy * vector(i)
        first = jnp.mean(dn, axis=-1, keepdims=True)
        second = jnp.mean(dn * n, axis=-1, keepdims=True)
        return rstd * (dn - first - n * second)

    def half_back(j, pre, up, down):
        hidden_grad = nt(branch[...], weight(0, down + j))
        fetch_pre(pre, j).wait()
        pre_grads[j] = low(silu_slope(f32(pre_buf[...]), hidden_grad))
        value = nt(pre_grads[j], weight(1, up + j))

        @pl.when(j == 0)
        def _():
            total[...] = value

        @pl.when(j > 0)
        def _():
            total[...] += value

    def prepare():
        small[...] = jnp.zeros_like(small)
        slope_sum[...] = jnp.zeros_like(slope_sum)
        for s in range(8):
            vectors[:, s * 128 : s * 128 + 128] = f32(vec_all[s])
            columns = f32(seg_all[s]).T
            for r in range(rows):
                seg_cols[r, s * 128 : s * 128 + 128, :] = columns[:, r : r + 1]
                seg_rows[r : r + 1, s * 128 : s * 128 + 128] = f32(seg_all[s, r : r + 1, :])
        before = jnp.where(seq > 0, f32(seg_all[lax.max(seq - 1, 0)]), -1.0).T
        middle = f32(seg_all[seq]).T
        after = jnp.where(seq < 7, f32(seg_all[lax.min(seq + 1, 7)]), -1.0).T
        for r in range(rows):
            for first, col in (
                (0, before[frame_count - HALO :, r : r + 1]),
                (HALO, middle[:, r : r + 1]),
                (HALO + frame_count, after[:HALO, r : r + 1]),
            ):
                seg_plane[r, first : first + col.shape[0], :] = jnp.broadcast_to(
                    col, (col.shape[0], 128)
                )
        gated_f[...] = f32(gated[...])

    def halo_copy(side):
        if side == 0:
            src, dst = pl.ds(HALO, HALO), pl.ds(HALO + frame_count, HALO)
            there = lax.rem(seq + 7, 8)
        else:
            src, dst = pl.ds(frame_count, HALO), pl.ds(0, HALO)
            there = lax.rem(seq + 1, 8)
        return remote_copy(
            mixed_w.at[:, src],
            mixed_w.at[:, dst],
            halo_sem.at[0, side],
            halo_sem.at[1, side],
            (dp, there),
        )

    def convolve_back(r):
        def lanes(i, _):
            at = pl.ds(pl.multiple_of(i * 128, 128), 128)
            own = seg_plane[r, HALO : HALO + frame_count, :]
            mine = mixed_f[r, HALO : HALO + frame_count, at]
            value = jnp.zeros((frame_count, 128), jnp.float32)
            for tap in range(31):
                first = tap + HALO - 15
                same = seg_plane[r, first : first + frame_count, :] == own
                near = jnp.where(same, gated_f[r, first : first + frame_count, at], 0.0)
                small[12 + tap : 13 + tap, at] += jnp.sum(near * mine, axis=0, keepdims=True)
                came = jnp.where(same, mixed_f[r, first : first + frame_count, at], 0.0)
                value = value + came * vectors[12 + 30 - tap : 13 + 30 - tap, at]
            total[r * frame_count : (r + 1) * frame_count, at] = value
            return 0

        lax.fori_loop(0, width // 128, lanes, 0)

    def ga_copy(k, recv=False):
        there = peer(k)
        return remote_copy(
            g_out.at[there],
            g_in.at[there if recv else seq],
            ga_sem.at[0, there],
            ga_sem.at[1, there if recv else seq],
            (dp, there),
        )

    def pk_copy(there, c, r, recv=False):
        return remote_copy(
            p_out.at[there, c, r],
            p_in.at[there if recv else seq, c, r],
            pk_sem.at[0, there, c, r],
            pk_sem.at[1, there if recv else seq, c, r],
            (dp, there),
        )

    def attend_back_step(i):
        row, block = i // 4, lax.rem(i, 4)
        first = pl.multiple_of(block * QUERIES, QUERIES)
        distance = log_distance_block(length, block * QUERIES)
        same = seg_cols[row] == seg_rows[pl.ds(row, 1), pl.ds(first, QUERIES)]
        q = packed[pl.ds(block * 2, 2), 0, row].reshape(QUERIES, 128)
        k = packed[:, 1, row].reshape(length, 128)
        v = packed[:, 2, row].reshape(length, 128)
        g = g_in[pl.ds(block * 2, 2), row].reshape(QUERIES, 128)
        key_t = k.T

        @pl.when(block == 0)
        def _():
            key_sum[...] = jnp.zeros_like(key_sum)
            value_sum[...] = jnp.zeros_like(value_sum)

        outs = []
        for head in range(2):
            q_head = head_lanes(q, head, 0.125)
            g_head = head_lanes(g, head)
            logit = nt(k, q_head) - slopes[head] * distance
            logit = jnp.where(same, logit, -1e30)
            top = jnp.max(logit, axis=0, keepdims=True)
            power = jnp.exp(logit - top)
            prob = power * (1.0 / jnp.sum(power, axis=0, keepdims=True))
            prob_grad = nt(v, g_head)
            delta = jnp.sum(prob * prob_grad, axis=0, keepdims=True)
            logit_grad = prob * (prob_grad - delta)
            slope = jnp.sum(logit_grad * distance, axis=0, keepdims=True)
            slope_sum[head : head + 1, :] -= slope
            score = low(logit_grad)
            key_sum[...] += dot(score, q_head)
            value_sum[...] += dot(low(prob), g_head)
            query_t = dot(key_t, score)
            outs.append(query_t[64 * head : 64 * head + 64] * 0.125)
        query = low(jnp.concatenate(outs, axis=0).T)

        def deliver(b, c, value):
            p_out[b, c, row] = value

            @pl.when(b != seq)
            def _():
                pk_copy(b, c, row).start()

            @pl.when(b == seq)
            def _():
                p_in[b, c, row] = value

        for half in range(2):
            deliver(block * 2 + half, 0, query[half * 128 : half * 128 + 128])

        @pl.when(block == 3)
        def _():
            for b in range(8):
                at = slice(b * 128, b * 128 + 128)
                deliver(b, 1, low(key_sum[at, :]))
                deliver(b, 2, low(value_sum[at, :]))

    def vec_copies():
        copies = []
        for k in range(1, 8):
            copies.append(
                remote_copy(
                    vec_send.at[peer(k)],
                    vec_in.at[seq],
                    vec_sem.at[0, k - 1],
                    vec_sem.at[1, k - 1],
                    (dp, peer(k)),
                )
            )
        return copies

    def vec_dp_copies():
        where = vec_dp.at[dp]
        return [
            remote_copy(where, where, vec_sem.at[0, 6 + k], vec_sem.at[1, 6 + k], dp_peer(k))
            for k in (1, 2, 3)
        ]

    def send_vectors():
        lane = lax.broadcasted_iota(jnp.int32, (1, 128), 1)
        mine = jnp.zeros((1, 128), jnp.float32)
        for head in range(2):
            value = jnp.sum(slope_sum[head : head + 1, :], axis=-1, keepdims=True)
            mine = mine + jnp.where(lane == seq * 2 + head, value, 0.0)
        for s in range(8):
            vec_send[s] = small[:, s * 128 : s * 128 + 128]
            vec_send[s, 43:44, :] = mine
        vec_in[seq] = vec_send[seq]
        begin(vec_copies())

    def sum_vectors():
        finish(vec_copies())
        value = vec_in[0]
        for i in range(1, 8):
            value = value + vec_in[i]
        vec_dp[dp] = value
        begin(vec_dp_copies())

    def finish_vectors():
        finish(vec_dp_copies())
        vec_out[...] = (vec_dp[0] + vec_dp[1]) + (vec_dp[2] + vec_dp[3])

    def stage(first, second):
        left[...] = first
        right[...] = second

    def strided(b):
        blocks = []
        for e in range(2):
            at = pl.ds(pl.multiple_of((b * 2 + e) * 128, 128), 128)
            blocks += [pre_grads[j, :, at] for j in range(4)]
        return jnp.concatenate(blocks, axis=1)

    def step_work(step, _):
        sum_step(step)

        def at(first, count=1):
            return pl.when((step >= first) & (step < first + count))

        @at(0)
        def _():
            load(0, REAR_DOWN).start()
            load(1, REAR_UP).start()
            fetch_pre(pre_r, 0).start()
            fetch(after_rear).start()
            prepare()
            fetch(after_rear).wait()
            result[...] = low(norm_rows(v_buf[...], vector(5), vector(11)))
            grad[...] = norm_back(v_buf[...], 5, f32(cotangent[...]))
            branch[...] = low(0.5 * grad[...])
            fetch(after_conv).start()

        @at(0, 2)
        def _():
            for e in range(2):
                j = step * 2 + e
                half_back(j, pre_r, REAR_UP, REAR_DOWN)

                @pl.when(j < 3)
                def _():
                    load(0, REAR_DOWN + j + 1).start()
                    load(1, REAR_UP + j + 1).start()
                    fetch_pre(pre_r, j + 1).start()

        @at(1)
        def _():
            fetch(after_conv).wait()
            grad[...] += norm_back(v_buf[...], 4, total[...])
            conv_branch[...] = low(grad[...])
            fetch(mixed).start()
            load(0, POINT_OUT).start()

        @at(2)
        def _():
            act_grad = nt(conv_branch[...], weight(0, POINT_OUT))
            fetch(mixed).wait()
            act_grad = silu_slope(norm_rows(v_buf[...], vector(3), vector(9)), act_grad)
            value = low(norm_back(v_buf[...], 3, act_grad))
            mixed_w[:, HALO : HALO + frame_count] = value.reshape(rows, frame_count, width)

            @pl.when(seq > 0)
            def _():
                halo_copy(0).start()

            @pl.when(seq < 7)
            def _():
                halo_copy(1).start()

            fetch(after_attend).start()
            load(0, POINT_IN).start()
            load(1, POINT_IN + 1).start()

        @at(3)
        def _():
            @pl.when(seq > 0)
            def _():
                halo_copy(0).wait_send()
                halo_copy(1).wait_recv()

            @pl.when(seq < 7)
            def _():
                halo_copy(1).wait_send()
                halo_copy(0).wait_recv()

            mixed_f[...] = f32(mixed_w[...])
            convolve_back(0)

        @at(4)
        def _():
            convolve_back(1)

        @at(5)
        def _():
            gate = logistic(f32(conv_pre[1]))
            gate_grads[0] = low(total[...] * gate)
            gate_grads[1] = low(total[...] * f32(conv_pre[0]) * gate * (1.0 - gate))
            norm_grad = nt(gate_grads[0], weight(0, POINT_IN))
            load(0, ATTEND_OUT).start()
            norm_grad = norm_grad + nt(gate_grads[1], weight(1, POINT_IN + 1))
            fetch(after_attend).wait()
            grad[...] += norm_back(v_buf[...], 2, norm_grad)
            attend_branch[...] = low(grad[...])
            fetch(after_front).start()
            value = low(nt(attend_branch[...], weight(0, ATTEND_OUT)))
            for s in range(8):
                g_out[s] = value[:, s * 128 : s * 128 + 128].reshape(rows, frame_count, 128)
            g_in[seq] = g_out[seq]
            for k in range(1, 8):
                ga_copy(k).start()
            load(0, PROJECT).start()
            load(1, PROJECT + 1).start()

        @at(7)
        def _():
            for k in range(1, 8):
                ga_copy(k, True).wait_recv()
                ga_copy(k).wait_send()

        @at(7, 4)
        def _():
            attend_back_step((step - 7) * 2)
            attend_back_step((step - 7) * 2 + 1)

        @at(12)
        def _():
            for c in range(3):
                for r in range(rows):
                    for k in range(1, 8):
                        pk_copy(peer(k), c, r, True).wait_recv()
                        pk_copy(peer(k), c, r).wait_send()
                for s in range(8):
                    parts[c, :, s * 128 : s * 128 + 128] = p_in[s, c].reshape(
                        rows * frame_count, 128
                    )
            norm_grad = nt(parts[0], weight(0, PROJECT))
            load(0, PROJECT + 2).start()
            norm_grad = norm_grad + nt(parts[1], weight(1, PROJECT + 1))
            load(1, UP).start()
            fetch_pre(pre_f, 0).start()
            norm_grad = norm_grad + nt(parts[2], weight(0, PROJECT + 2))
            load(0, DOWN).start()
            fetch(after_front).wait()
            grad[...] += norm_back(v_buf[...], 1, norm_grad)
            branch[...] = low(0.5 * grad[...])

        @at(13, 4)
        def _():
            j = step - 13
            half_back(j, pre_f, UP, DOWN)

            @pl.when(j < 3)
            def _():
                load(0, DOWN + j + 1).start()
                load(1, UP + j + 1).start()
                fetch_pre(pre_f, j + 1).start()

        @at(17)
        def _():
            frames_grad[...] = low(
                grad[...] + norm_back(f32(frames[...]), 0, total[...])
            )
            send_vectors()

        @at(19)
        def _():
            sum_vectors()

        @at(21)
        def _():
            finish_vectors()

        @at(0)
        def _():
            fetch_hid(hid_r, 0).start()

        @at(0, JOB_RU)
        def _():
            fetch_hid(hid_r, step).wait()
            stage(hid_buf[...], branch[...])

            @pl.when(step < 3)
            def _():
                fetch_hid(hid_r, step + 1).start()

        @at(JOB_RU, 4)
        def _():
            stage(norm4[...], strided(step - JOB_RU))

        @at(JOB_PO)
        def _():
            stage(act[...], conv_branch[...])

        @at(JOB_PI, 2)
        def _():
            stage(norm2[...], gate_grads[step - JOB_PI])

        @at(JOB_AO)
        def _():
            stage(attended[...], attend_branch[...])

        @at(JOB_P, 3)
        def _():
            stage(norm1[...], parts[step - JOB_P])

        @at(JOB_FD - 1)
        def _():
            fetch_hid(hid_f, 0).start()

        @at(JOB_FD, 4)
        def _():
            fetch_hid(hid_f, step - JOB_FD).wait()
            stage(hid_buf[...], branch[...])

            @pl.when(step < JOB_FD + 3)
            def _():
                fetch_hid(hid_f, step - JOB_FD + 1).start()

        @at(JOB_FU, 4)
        def _():
            stage(norm0[...], strided(step - JOB_FU))

        @at(0, JOBS)
        def _():
            product(step, lax.rem(step, RING))

        return 0

    lax.fori_loop(0, JOBS + OUT_LAG, step_work, 0)
    out_copy(JOBS - 2).wait()
    out_copy(JOBS - 1).wait()


def backward_layer(saved, frames, cotangent, slopes):
    bf16, single = jnp.bfloat16, jnp.float32
    tokens, width = frames.shape
    dma = pltpu.SemaphoreType.DMA
    vmem, hbm = pl.BlockSpec(memory_space=pltpu.VMEM), pl.BlockSpec(memory_space=pltpu.HBM)
    kept = (0, 4, 5, 6, 10, 14, 16, 18, 19, 20)

    def buf(kind, *sizes):
        return pltpu.VMEM(sizes, kind)

    low_buf, wide_buf = buf(bf16, tokens, width), buf(single, tokens, width)
    frame_count = 128
    tall = frame_count + 2 * HALO
    return pl.pallas_call(
        backward_kernel,
        in_specs=[hbm if i in kept else vmem for i in range(21)]
        + [vmem, vmem, pl.BlockSpec(memory_space=pltpu.SMEM)],
        out_specs=[vmem, vmem, hbm, vmem],
        out_shape=[
            jax.ShapeDtypeStruct((tokens, width), bf16),
            jax.ShapeDtypeStruct((tokens, width), bf16),
            jax.ShapeDtypeStruct((JOBS, 128, width), single),
            jax.ShapeDtypeStruct((VECTORS, 128), single),
        ],
        scratch_shapes=[
            buf(bf16, 2, 8, 128, width),
            low_buf,
            low_buf,
            wide_buf,
            buf(single, VECTORS, width),
            buf(single, VECTORS, width),
            low_buf,
            low_buf,
            low_buf,
            buf(bf16, 4, tokens, width),
            low_buf,
            buf(bf16, 2, tokens, width),
            low_buf,
            buf(bf16, 3, tokens, width),
            wide_buf,
            wide_buf,
            buf(single, 2, tall, width),
            buf(bf16, 2, tall, width),
            buf(single, 2, tall, width),
            buf(single, 2, tall, 128),
            buf(single, 2, 1024, 1),
            buf(single, 8, 1024),
            buf(bf16, 8, 2, 128, 128),
            buf(bf16, 8, 2, 128, 128),
            buf(bf16, 8, 3, 2, 128, 128),
            buf(bf16, 8, 3, 2, 128, 128),
            buf(single, 1024, 128),
            buf(single, 1024, 128),
            buf(single, 8, QUERIES),
            buf(single, 2, 128, width),
            buf(bf16, 2, 4, 128, width),
            buf(bf16, 4, 2, 2, PIECE, width),
            buf(bf16, 2, 2, PIECE, width),
            buf(bf16, 2, 2, PIECE, width),
            buf(bf16, 4, PIECE, width),
            buf(bf16, RING, 4, 128, width),
            buf(bf16, RING, 2, 2, PIECE, width),
            buf(bf16, RING, 2, 2, PIECE, width),
            buf(bf16, RING, 2, PIECE, width),
            buf(bf16, RING, 2, PIECE, width),
            buf(bf16, RING, 3, PIECE, width),
            buf(bf16, RING, 4, PIECE, width),
            buf(single, 8, VECTORS, 128),
            buf(single, 8, VECTORS, 128),
            buf(single, 4, VECTORS, 128),
            dma((2, 12, RING)),
            dma((2, 10)),
            dma((2,)),
            dma((1,)),
            dma((1,)),
            dma((1,)),
            dma((2, 8)),
            dma((2, 8, 3, 2)),
            dma((2, 2)),
            dma((2,)),
        ],
        compiler_params=pltpu.CompilerParams(
            collective_id=1, has_side_effects=True, vmem_limit_bytes=62 * 2**20
        ),
        name="backward_layer",
    )(*saved, frames, cotangent, slopes)


def body_staged(
    frames,
    segments,
    cotangent,
    norm_gains,
    norm_biases,
    front_up,
    front_down,
    attend_in,
    attend_out,
    slopes,
    point_in,
    depthwise,
    point_out,
    rear_up,
    rear_down,
):
    row_count, frame_count, width = frames.shape
    token_count = row_count * frame_count
    seq = lax.axis_index("seq")
    taps = depthwise.shape[0]

    def wide(shard):
        return shard.reshape(128, -1, width).transpose(1, 0, 2)

    def dealt(shard):
        return shard.reshape(128, 8, 4, 128).transpose(2, 0, 1, 3).reshape(4, 128, width)

    shards = jnp.concatenate(
        [
            dealt(front_up),
            front_down.reshape(4, 128, width),
            wide(attend_in),
            wide(attend_out),
            wide(point_in),
            wide(point_out),
            dealt(rear_up),
            rear_down.reshape(4, 128, width),
        ]
    )
    vector_shard = jnp.concatenate([norm_gains, norm_biases, depthwise])
    vector_shard = jnp.pad(vector_shard, ((0, VECTORS - vector_shard.shape[0]), (0, 0)))
    segment_shard = jnp.pad(segments, ((0, 8 - row_count), (0, 0)))
    my_slopes = lax.dynamic_slice_in_dim(slopes, seq * 2, 2, 0)
    tokens = frames.reshape(token_count, width)
    saved = forward_layer(shards, vector_shard, segment_shard, tokens, my_slopes)
    result, frames_grad, shares, vectors = backward_layer(
        saved, tokens, cotangent.reshape(token_count, width), my_slopes
    )

    def beside(first, count):
        return jnp.concatenate([shares[first + i] for i in range(count)], axis=1)

    def below(first):
        return shares[first : first + 4].reshape(-1, width)

    return (
        result.reshape(frames.shape),
        frames_grad.reshape(frames.shape),
        vectors[:6],
        vectors[6:12],
        beside(JOB_FU, 4),
        below(JOB_FD),
        beside(JOB_P, 3),
        shares[JOB_AO],
        vectors[12 + taps, : slopes.shape[0]],
        beside(JOB_PI, 2),
        vectors[12 : 12 + taps],
        shares[JOB_PO],
        beside(JOB_RU, 4),
        below(0),
    )


def solution(mesh):
    placed = (
        P("dp", "seq", None),
        P("dp", "seq"),
        P("dp", "seq", None),
        P(None, "seq"),
        P(None, "seq"),
        P("seq", None),
        P("seq", None),
        P("seq", None),
        P("seq", None),
        P(),
        P("seq", None),
        P(None, "seq"),
        P("seq", None),
        P("seq", None),
        P("seq", None),
    )
    sizes = mesh.shape
    staged = sizes["dp"] == 4 and sizes["seq"] == 8
    return jax.shard_map(
        body_staged if staged else body,
        mesh=mesh,
        in_specs=placed,
        out_specs=(
            P("dp", "seq", None),
            P("dp", "seq", None),
            P(None, "seq"),
            P(None, "seq"),
            P("seq", None),
            P("seq", None),
            P("seq", None),
            P("seq", None),
            P(),
            P("seq", None),
            P(None, "seq"),
            P("seq", None),
            P("seq", None),
            P("seq", None),
        ),
        check_vma=False,
    )
```

```python
import jax
import jax.numpy as jnp
from jax import lax
from jax.experimental import pallas as pl
from jax.experimental.pallas import tpu as pltpu
from jax.sharding import PartitionSpec as P


def padded(value, sides, width):
    for axis, dim in sides:
        peers, length = (lax.axis_size(axis), value.shape[dim])
        up = [(i, (i + 1) % peers) for i in range(peers - 1)]
        down = [(j, i) for i, j in up]
        last = lax.slice_in_dim(value, length - width, length, axis=dim)
        leading = lax.slice_in_dim(value, 0, width, axis=dim)
        before = lax.ppermute(last, axis, up)
        after = lax.ppermute(leading, axis, down)
        value = jnp.concatenate([before, value, after], axis=dim)
    return value


def shifted(block, axis, distance):
    devices = range(lax.axis_size(axis))
    route = [((i - distance) % len(devices), i) for i in devices]
    return lax.ppermute(block, axis, route)


def layer_norm(stream, norm_gain, norm_bias):
    average = jnp.mean(stream, axis=-1, keepdims=True)
    centred = stream - average
    spread = jnp.mean(centred * centred, axis=-1, keepdims=True)
    return centred * lax.rsqrt(spread + 1e-05) * norm_gain + norm_bias


def feed_forward(stream, norm_gain, norm_bias, weight_up, weight_down):
    normed, norm_pull = jax.vjp(layer_norm, stream, norm_gain, norm_bias)
    normed_low = normed.astype(jnp.bfloat16)
    inner_act = jnp.dot(normed_low, weight_up, preferred_element_type=jnp.float32)
    hidden, act_pull = jax.vjp(jax.nn.silu, inner_act)
    hidden_low = hidden.astype(jnp.bfloat16)
    branch = jnp.dot(hidden_low, weight_down, preferred_element_type=jnp.float32)
    return (stream + 0.5 * branch, (norm_pull, normed_low, act_pull, hidden_low))


def feed_backward(grad_in, saved_state, weight_up, weight_down):
    norm_pull, normed_low, act_pull, hidden_low = saved_state
    branch_low = (0.5 * grad_in).astype(jnp.bfloat16)
    down_grad = jnp.einsum("tf,td->fd", hidden_low, branch_low, preferred_element_type=jnp.float32)
    hidden_grad = jnp.einsum(
        "td,fd->tf", branch_low, weight_down, preferred_element_type=jnp.float32
    )
    inner_grad = act_pull(hidden_grad)[0].astype(jnp.bfloat16)
    up_grad = jnp.einsum("td,tf->df", normed_low, inner_grad, preferred_element_type=jnp.float32)
    normed_grad = jnp.einsum("tf,df->td", inner_grad, weight_up, preferred_element_type=jnp.float32)
    stream_grad, gain_grad, bias_grad = norm_pull(normed_grad)
    return (grad_in + stream_grad, gain_grad, bias_grad, up_grad, down_grad)


def score_block(query_heads, key_piece, query_start, key_start, query_seg, key_seg, slopes):
    row_count, key_count, feature_count = key_piece.shape
    head_count = query_heads.shape[2]
    head_size = query_heads.shape[3]
    key_heads = key_piece.reshape(row_count, key_count, head_count, head_size)
    raw_score = jnp.einsum(
        "rqhd,rkhd->rqhk", query_heads, key_heads, preferred_element_type=jnp.float32
    ) * head_size ** (-0.5)
    query_place = query_start + jnp.arange(query_heads.shape[1], dtype=jnp.int32)
    key_place = key_start + jnp.arange(key_count, dtype=jnp.int32)
    log_distance = jnp.log1p(jnp.abs(query_place[:, None] - key_place[None, :]).astype(jnp.float32))
    is_live = (query_seg[:, :, None] == key_seg[:, None, :])[:, :, None, :]
    logits = jnp.where(
        is_live, raw_score - slopes[None, None, :, None] * log_distance[None, :, None, :], -1e30
    )
    return (logits, is_live, log_distance, key_heads)


def prob_grads(
    query_heads,
    grad_heads,
    log_sum,
    row_delta,
    query_start,
    query_seg,
    key_piece,
    value_piece,
    key_start,
    key_seg,
    slopes,
):
    logits, is_live, log_distance, key_heads = score_block(
        query_heads, key_piece, query_start, key_start, query_seg, key_seg, slopes
    )
    row_prob = jnp.where(is_live, jnp.exp(logits - log_sum[..., None]), 0.0)
    value_heads = value_piece.reshape(key_heads.shape)
    prob_grad = jnp.einsum(
        "rqhd,rkhd->rqhk", grad_heads, value_heads, preferred_element_type=jnp.float32
    )
    score_grad = row_prob * (prob_grad - row_delta[..., None])
    return (row_prob, score_grad, score_grad.astype(jnp.bfloat16), log_distance, key_heads)


def body(
    frames,
    segments,
    cotangent,
    norm_gains,
    norm_biases,
    front_up,
    front_down,
    attend_in,
    attend_out,
    slopes,
    point_in,
    depthwise,
    point_out,
    rear_up,
    rear_down,
):
    row_count, frame_count, feature_count = frames.shape
    head_count = slopes.shape[0]
    head_size = feature_count // head_count
    token_count = row_count * frame_count
    seq_size = lax.axis_size("seq")
    seq_index = lax.axis_index("seq")
    query_start = seq_index * frame_count
    score_scale = head_size ** (-0.5)
    (
        gains_w,
        biases_w,
        front_up_w,
        front_down_w,
        attend_in_w,
        attend_out_w,
        point_in_w,
        depth_w,
        point_out_w,
        rear_up_w,
        rear_down_w,
    ) = (
        lax.all_gather(norm_gains, "seq", axis=1, tiled=True),
        lax.all_gather(norm_biases, "seq", axis=1, tiled=True),
        lax.all_gather(front_up, "seq", axis=0, tiled=True),
        lax.all_gather(front_down, "seq", axis=0, tiled=True),
        lax.all_gather(attend_in, "seq", axis=0, tiled=True),
        lax.all_gather(attend_out, "seq", axis=0, tiled=True),
        lax.all_gather(point_in, "seq", axis=0, tiled=True),
        lax.all_gather(depthwise, "seq", axis=1, tiled=True),
        lax.all_gather(point_out, "seq", axis=0, tiled=True),
        lax.all_gather(rear_up, "seq", axis=0, tiled=True),
        lax.all_gather(rear_down, "seq", axis=0, tiled=True),
    )
    gains_f = gains_w.astype(jnp.float32)
    biases_f = biases_w.astype(jnp.float32)
    depth_f = depth_w.astype(jnp.float32)
    kernel_len = depth_f.shape[0]
    half_k = kernel_len // 2
    segment_row = lax.all_gather(segments, "seq", axis=1, tiled=True)
    start_stream = frames.astype(jnp.float32).reshape(token_count, feature_count)
    after_front, front_saved = feed_forward(
        start_stream, gains_f[0], biases_f[0], front_up_w, front_down_w
    )
    attend_normed, attend_pull = jax.vjp(layer_norm, after_front, gains_f[1], biases_f[1])
    attend_low = attend_normed.astype(jnp.bfloat16)
    projected = jnp.dot(attend_low, attend_in_w, preferred_element_type=jnp.float32).astype(
        jnp.bfloat16
    )
    query_heads = projected[:, :feature_count].reshape(
        row_count, frame_count, head_count, head_size
    )
    key_low = projected[:, feature_count : 2 * feature_count].reshape(
        row_count, frame_count, feature_count
    )
    value_low = projected[:, 2 * feature_count :].reshape(row_count, frame_count, feature_count)
    stat_shape = (row_count, frame_count, head_count)
    start = jnp.int32(0)
    key_piece = lax.all_gather(key_low, "seq", axis=1, tiled=True)
    value_piece = lax.all_gather(value_low, "seq", axis=1, tiled=True)
    key_seg = segment_row
    row_top = jnp.full(stat_shape, -1e30, jnp.float32)
    logits, is_live, log_distance, key_heads = score_block(
        query_heads, key_piece, query_start, start, segments, key_seg, slopes
    )
    new_top = jnp.maximum(row_top, jnp.max(logits, axis=-1))
    row_exp = jnp.where(is_live, jnp.exp(logits - new_top[..., None]), 0.0)
    value_heads = value_piece.reshape(key_heads.shape)
    accum = jnp.einsum(
        "rqhk,rkhd->rqhd",
        row_exp.astype(jnp.bfloat16),
        value_heads,
        preferred_element_type=jnp.float32,
    )
    row_top, row_total, accum = (new_top, jnp.sum(row_exp, axis=-1), accum)
    attended = accum / row_total[..., None]
    log_sum = row_top + jnp.log(row_total)
    attended_low = attended.reshape(token_count, feature_count).astype(jnp.bfloat16)
    after_attend = after_front + jnp.dot(
        attended_low, attend_out_w, preferred_element_type=jnp.float32
    )
    conv_normed, conv_pull = jax.vjp(layer_norm, after_attend, gains_f[2], biases_f[2])
    conv_low = conv_normed.astype(jnp.bfloat16)
    conv_pre = jnp.dot(conv_low, point_in_w, preferred_element_type=jnp.float32)

    def gate_unit(inner_act):
        return inner_act[:, :feature_count] * jax.nn.sigmoid(inner_act[:, feature_count:])

    gated, gate_pull = jax.vjp(gate_unit, conv_pre)
    gated_low = gated.astype(jnp.bfloat16).reshape(row_count, frame_count, feature_count)
    gated_wide = padded(gated_low, (("seq", 1),), half_k).astype(jnp.float32)
    padded_seg = jnp.pad(segment_row, ((0, 0), (half_k, half_k)), constant_values=-1)
    seg_window = lax.dynamic_slice_in_dim(padded_seg, query_start, frame_count + 2 * half_k, 1)
    same_list = [
        (seg_window[:, offset : offset + frame_count] == segments)[..., None]
        for offset in range(kernel_len)
    ]
    mixed_conv = jnp.zeros((row_count, frame_count, feature_count), jnp.float32)
    for offset in range(kernel_len):
        mixed_conv = mixed_conv + jnp.where(
            same_list[offset], depth_f[offset] * gated_wide[:, offset : offset + frame_count], 0.0
        )

    def norm_silu(stream, norm_gain, norm_bias):
        return jax.nn.silu(layer_norm(stream, norm_gain, norm_bias))

    activated, activated_pull = jax.vjp(
        norm_silu, mixed_conv.reshape(token_count, feature_count), gains_f[3], biases_f[3]
    )
    activated_low = activated.astype(jnp.bfloat16)
    after_conv = after_attend + jnp.dot(
        activated_low, point_out_w, preferred_element_type=jnp.float32
    )
    after_rear, rear_saved = feed_forward(
        after_conv, gains_f[4], biases_f[4], rear_up_w, rear_down_w
    )
    final_out, final_pull = jax.vjp(layer_norm, after_rear, gains_f[5], biases_f[5])
    result = final_out.astype(jnp.bfloat16).reshape(row_count, frame_count, feature_count)
    grad_rear, gain_five, bias_five = final_pull(
        cotangent.astype(jnp.float32).reshape(token_count, feature_count)
    )
    grad_conv, gain_four, bias_four, rear_up_grad, rear_down_grad = feed_backward(
        grad_rear, rear_saved, rear_up_w, rear_down_w
    )
    conv_branch = grad_conv.astype(jnp.bfloat16)
    point_out_grad = jnp.einsum(
        "td,te->de", activated_low, conv_branch, preferred_element_type=jnp.float32
    )
    activated_grad = jnp.einsum(
        "te,de->td", conv_branch, point_out_w, preferred_element_type=jnp.float32
    )
    mixed_grad, gain_three, bias_three = activated_pull(activated_grad)
    mixed_low = mixed_grad.astype(jnp.bfloat16).reshape(row_count, frame_count, feature_count)
    grad_wide = padded(mixed_low, (("seq", 1),), half_k).astype(jnp.float32)
    mixed_back = mixed_low.astype(jnp.float32)
    depth_rows = [
        jnp.sum(
            jnp.where(
                same_list[offset], mixed_back * gated_wide[:, offset : offset + frame_count], 0.0
            ),
            axis=(0, 1),
        )
        for offset in range(kernel_len)
    ]
    depthwise_grad = jnp.stack(depth_rows)
    gated_grad = jnp.zeros((row_count, frame_count, feature_count), jnp.float32)
    for offset in range(kernel_len):
        mirror = 2 * half_k - offset
        gated_grad = gated_grad + jnp.where(
            same_list[mirror], depth_f[offset] * grad_wide[:, mirror : mirror + frame_count], 0.0
        )
    pre_grad = gate_pull(gated_grad.reshape(token_count, feature_count))[0].astype(jnp.bfloat16)
    point_in_grad = jnp.einsum("td,tc->dc", conv_low, pre_grad, preferred_element_type=jnp.float32)
    conv_normed_grad = jnp.einsum(
        "tc,dc->td", pre_grad, point_in_w, preferred_element_type=jnp.float32
    )
    conv_stream_grad, gain_two, bias_two = conv_pull(conv_normed_grad)
    grad_attend = grad_conv + conv_stream_grad
    attend_branch = grad_attend.astype(jnp.bfloat16)
    attend_out_grad = jnp.einsum(
        "td,te->de", attended_low, attend_branch, preferred_element_type=jnp.float32
    )
    attended_grad = jnp.einsum(
        "te,de->td", attend_branch, attend_out_w, preferred_element_type=jnp.float32
    )
    grad_heads = attended_grad.astype(jnp.bfloat16).reshape(
        row_count, frame_count, head_count, head_size
    )
    row_delta = jnp.sum(grad_heads.astype(jnp.float32) * attended, axis=-1)

    def query_terms(state, key_piece, value_piece, start, key_seg):
        query_grad, slope_grad = state
        row_prob, score_grad, score_low, log_distance, key_heads = prob_grads(
            query_heads,
            grad_heads,
            log_sum,
            row_delta,
            query_start,
            segments,
            key_piece,
            value_piece,
            start,
            key_seg,
            slopes,
        )
        query_grad = (
            query_grad
            + jnp.einsum(
                "rqhk,rkhd->rqhd", score_low, key_heads, preferred_element_type=jnp.float32
            )
            * score_scale
        )
        slope_grad = slope_grad - jnp.einsum("rqhk,qk->h", score_grad, log_distance)
        return (query_grad, slope_grad, row_prob, score_low)

    query_zero = jnp.zeros((row_count, frame_count, head_count, head_size), jnp.float32)
    slope_zero = jnp.zeros((head_count,), jnp.float32)
    local_zero = jnp.zeros((row_count, frame_count, feature_count), jnp.float32)

    def accumulate(step, query_grad, slope_grad, pair_kv, pair_acc):
        owner = (seq_index + step) % seq_size
        start = owner * frame_count
        key_seg = lax.dynamic_slice_in_dim(segment_row, start, frame_count, 1)
        grad_q = query_grad
        grad_s = slope_grad
        key_acc = pair_acc[0]
        value_acc = pair_acc[1]
        grad_q, grad_s, row_prob, score_low = query_terms(
            (grad_q, grad_s), pair_kv[0], pair_kv[1], start, key_seg
        )
        key_acc = key_acc + (
            jnp.einsum(
                "rqhk,rqhd->rkhd", score_low, query_heads, preferred_element_type=jnp.float32
            )
            * score_scale
        ).reshape(row_count, frame_count, feature_count)
        value_acc = value_acc + jnp.einsum(
            "rqhk,rqhd->rkhd",
            row_prob.astype(jnp.bfloat16),
            grad_heads,
            preferred_element_type=jnp.float32,
        ).reshape(row_count, frame_count, feature_count)
        query_grad, slope_grad, key_acc, value_acc = (grad_q, grad_s, key_acc, value_acc)
        pair_acc = shifted(jnp.stack([key_acc, value_acc]).astype(jnp.bfloat16), "seq", -1).astype(
            jnp.float32
        )
        return (query_grad, slope_grad, pair_acc)

    def cycle_step(step, carry):
        query_grad, slope_grad, pair_kv, pair_acc = carry
        next_kv = shifted(pair_kv, "seq", -1)
        query_grad, slope_grad, pair_acc = accumulate(
            step, query_grad, slope_grad, pair_kv, pair_acc
        )
        return (query_grad, slope_grad, next_kv, pair_acc)

    pair_start = jnp.stack([key_low, value_low])
    acc_start = jnp.stack([local_zero, local_zero])
    query_grad, slope_grad, pair_kv, pair_acc = lax.fori_loop(
        0, seq_size - 1, cycle_step, (query_zero, slope_zero, pair_start, acc_start)
    )
    query_grad, slope_grad, pair_acc = accumulate(
        seq_size - 1, query_grad, slope_grad, pair_kv, pair_acc
    )
    key_grad = pair_acc[0]
    value_grad = pair_acc[1]
    projected_grad = jnp.concatenate(
        [
            query_grad.reshape(token_count, feature_count),
            key_grad.reshape(token_count, feature_count),
            value_grad.reshape(token_count, feature_count),
        ],
        axis=1,
    ).astype(jnp.bfloat16)
    attend_in_grad = jnp.einsum(
        "td,tc->dc", attend_low, projected_grad, preferred_element_type=jnp.float32
    )
    attend_normed_grad = jnp.einsum(
        "tc,dc->td", projected_grad, attend_in_w, preferred_element_type=jnp.float32
    )
    attend_stream_grad, gain_one, bias_one = attend_pull(attend_normed_grad)
    grad_front = grad_attend + attend_stream_grad
    start_grad, gain_zero, bias_zero, front_up_grad, front_down_grad = feed_backward(
        grad_front, front_saved, front_up_w, front_down_w
    )
    frames_grad = start_grad.astype(jnp.bfloat16).reshape(row_count, frame_count, feature_count)
    gains_local = jnp.stack([gain_zero, gain_one, gain_two, gain_three, gain_four, gain_five])
    biases_local = jnp.stack([bias_zero, bias_one, bias_two, bias_three, bias_four, bias_five])
    slope_rows = jnp.broadcast_to(slope_grad[None, :], (seq_size, head_count))
    shares = (
        lax.psum_scatter(
            gains_local.astype(jnp.bfloat16), "seq", scatter_dimension=1, tiled=True
        ).astype(jnp.float32),
        lax.psum_scatter(
            biases_local.astype(jnp.bfloat16), "seq", scatter_dimension=1, tiled=True
        ).astype(jnp.float32),
        lax.psum_scatter(
            front_up_grad.astype(jnp.bfloat16), "seq", scatter_dimension=0, tiled=True
        ).astype(jnp.float32),
        lax.psum_scatter(
            front_down_grad.astype(jnp.bfloat16), "seq", scatter_dimension=0, tiled=True
        ).astype(jnp.float32),
        lax.psum_scatter(
            attend_in_grad.astype(jnp.bfloat16), "seq", scatter_dimension=0, tiled=True
        ).astype(jnp.float32),
        lax.psum_scatter(
            attend_out_grad.astype(jnp.bfloat16), "seq", scatter_dimension=0, tiled=True
        ).astype(jnp.float32),
        lax.psum_scatter(
            slope_rows.astype(jnp.bfloat16), "seq", scatter_dimension=0, tiled=True
        ).astype(jnp.float32),
        lax.psum_scatter(
            point_in_grad.astype(jnp.bfloat16), "seq", scatter_dimension=0, tiled=True
        ).astype(jnp.float32),
        lax.psum_scatter(
            depthwise_grad.astype(jnp.bfloat16), "seq", scatter_dimension=1, tiled=True
        ).astype(jnp.float32),
        lax.psum_scatter(
            point_out_grad.astype(jnp.bfloat16), "seq", scatter_dimension=0, tiled=True
        ).astype(jnp.float32),
        lax.psum_scatter(
            rear_up_grad.astype(jnp.bfloat16), "seq", scatter_dimension=0, tiled=True
        ).astype(jnp.float32),
        lax.psum_scatter(
            rear_down_grad.astype(jnp.bfloat16), "seq", scatter_dimension=0, tiled=True
        ).astype(jnp.float32),
    )
    totals = (
        lax.psum(shares[0].astype(jnp.bfloat16), "dp").astype(jnp.float32),
        lax.psum(shares[1].astype(jnp.bfloat16), "dp").astype(jnp.float32),
        lax.psum(shares[2].astype(jnp.bfloat16), "dp").astype(jnp.float32),
        lax.psum(shares[3].astype(jnp.bfloat16), "dp").astype(jnp.float32),
        lax.psum(shares[4].astype(jnp.bfloat16), "dp").astype(jnp.float32),
        lax.psum(shares[5].astype(jnp.bfloat16), "dp").astype(jnp.float32),
        lax.psum(shares[6].astype(jnp.bfloat16), "dp").astype(jnp.float32),
        lax.psum(shares[7].astype(jnp.bfloat16), "dp").astype(jnp.float32),
        lax.psum(shares[8].astype(jnp.bfloat16), "dp").astype(jnp.float32),
        lax.psum(shares[9].astype(jnp.bfloat16), "dp").astype(jnp.float32),
        lax.psum(shares[10].astype(jnp.bfloat16), "dp").astype(jnp.float32),
        lax.psum(shares[11].astype(jnp.bfloat16), "dp").astype(jnp.float32),
    )
    return (
        result,
        frames_grad,
        totals[0],
        totals[1],
        totals[2],
        totals[3],
        totals[4],
        totals[5],
        totals[6].reshape(head_count),
        totals[7],
        totals[8],
        totals[9],
        totals[10],
        totals[11],
    )


def place():
    dp, seq = lax.axis_index("dp"), lax.axis_index("seq")
    return dp // 2, dp % 2, seq // 2, seq % 2


QUERIES = 256


def head_lanes(value, head, scale=1.0):
    lane = lax.broadcasted_iota(jnp.int32, value.shape, 1)
    mine = (lane >= 64 * head) & (lane < 64 * head + 64)
    return jnp.where(mine, value * jnp.asarray(scale, value.dtype), jnp.zeros_like(value))


def nt(a, b):
    return lax.dot_general(a, b, (((1,), (1,)), ((), ())), preferred_element_type=jnp.float32)


MESH_ID = pl.DeviceIdType.MESH
PIECE = 32
HALO = 16
TILE, TILES = 128, 8
UP, DOWN, PROJECT, ATTEND_OUT, POINT_IN, POINT_OUT, REAR_UP, REAR_DOWN = 0, 4, 8, 11, 12, 14, 15, 19
CHUNKS = 23
TALL = (False, True, False, False, False, False, False, True)
LEAD = 12
VMEM_LIMIT = 63 * 2**20
STAGE = 1
STEP = 4 * STAGE
VECTORS = 48


def low(value):
    return value.astype(jnp.bfloat16)


def f32(value):
    return value.astype(jnp.float32)


def dot(a, b):
    return jnp.dot(a, b, preferred_element_type=jnp.float32)


def norm_rows(v, gain, bias):
    centred = v - jnp.mean(v, axis=-1, keepdims=True)
    spread = jnp.mean(centred * centred, axis=-1, keepdims=True)
    return centred * lax.rsqrt(spread + 1e-05) * gain + bias


def logistic(v):
    return 1.0 / (1.0 + jnp.exp(-v))


def remote_copy(src, dst, send_sem, recv_sem, there):
    return pltpu.make_async_remote_copy(
        src_ref=src,
        dst_ref=dst,
        send_sem=send_sem,
        recv_sem=recv_sem,
        device_id=there,
        device_id_type=MESH_ID,
    )


def attend_block(e, first_head, row, block):
    q = e.packed[pl.ds(block * 2, 2), 0, row].reshape(QUERIES, 128)
    value_t = e.packed[:, 2, row].reshape(TILES * TILE, 128).T
    first = pl.multiple_of(block * QUERIES, QUERIES)
    query_seg = e.seg_rows[pl.ds(row, 1), pl.ds(first, QUERIES)]
    outs = []
    for head in range(2):
        q_head = head_lanes(q, head, 0.125)
        slope = e.slopes[first_head + head]
        top = jnp.full((1, QUERIES), -1e30, jnp.float32)
        for kb in range(TILES):
            logit = logit_tile(e, q_head, slope, query_seg, row, block, kb)[0]
            e.logits[kb] = logit
            top = jnp.maximum(top, jnp.max(logit, axis=0, keepdims=True))
        total = jnp.zeros((1, QUERIES), jnp.float32)
        for kb in range(TILES):
            power = jnp.exp(e.logits[kb] - top)
            total = total + jnp.sum(power, axis=0, keepdims=True)
            e.scores[kb * TILE : kb * TILE + TILE, :] = low(power)
        e.log_sum[row, head, :, pl.ds(first, QUERIES)] = top + jnp.log(total)
        out = dot(value_t, e.scores[...])
        outs.append(out[64 * head : 64 * head + 64] / total)
    return jnp.concatenate(outs, axis=0).T


def logit_tile(e, q_head, slope, query_seg, row, block, kb):
    logit = nt(e.packed[kb, 1, row], q_head)
    distance = jnp.concatenate(
        [e.distances[kb - 2 * block + TILES - 1], e.distances[kb - 2 * block + TILES - 2]], axis=1
    )
    same = e.seg_cols[row, kb * TILE : kb * TILE + TILE, :] == query_seg
    return jnp.where(same, logit - slope * distance, -1e30), distance


def forward_part(e):
    sources, gains, biases, depth, segments, frames = (
        e.sources,
        e.gains,
        e.biases,
        e.depth,
        e.segments,
        e.frames,
    )
    full, vec_all, seg_all, packed, gated, mixed, act = (
        e.full,
        e.vec_all,
        e.seg_all,
        e.packed,
        e.gated,
        e.mixed,
        e.act,
    )
    norm0, norm1, norm2, norm4, attended, conv_pre = (
        e.norm0,
        e.norm1,
        e.norm2,
        e.norm4,
        e.attended,
        e.conv_pre,
    )
    after_front, after_attend, after_conv, after_rear = (
        e.after_front,
        e.after_attend,
        e.after_conv,
        e.after_rear,
    )
    pre, hid, wbuf, vectors, shards, acc = e.pre, e.hid, e.wbuf, e.vectors, e.pool, e.total
    pk_out, att_out, att_in, gated_f = e.pk_out, e.att_out, e.att_in, e.gated_f
    seg_plane, seg_cols, seg_rows = e.seg_plane, e.seg_cols, e.seg_rows
    vec_wide, vec, seg = e.vec_wide, e.vec, e.seg
    gather_sem, own_sem, small_sem, pk_sem, att_sem, halo_sem, load_sem, keep_sem = e.forward_sems
    y, x, z, core = place()
    dp, seq = y * 2 + x, z * 2 + core
    rows, width = 2, 1024
    frame_count = 128
    length = 8 * frame_count
    over_x = (y * 2 + 1 - x, seq)
    over_y = ((1 - y) * 2 + x, seq)
    over_core = (dp, z * 2 + 1 - core)

    def peer(k):
        return lax.rem(seq + k, 8)

    def read(t):
        first = 0
        for source, tall in zip(sources, TALL):
            count = source.shape[0] // 128 if tall else source.shape[1] // width
            if t < first + count:
                at = pl.ds((t - first) * (128 if tall else width), 128 if tall else width)
                where = source.at[at, :] if tall else source.at[:, at]
                return pltpu.make_async_copy(where, shards.at[t], own_sem.at[3, t])
            first += count

    def read_done(t):
        pltpu.make_async_copy(shards.at[t], shards.at[t], own_sem.at[3, t]).wait()

    for t in range(CHUNKS):
        read(t).start()
    vec_wide[...] = jnp.zeros_like(vec_wide)
    vec_wide[0:6, :] = f32(gains[...])
    vec_wide[6:12, :] = f32(biases[...])
    vec_wide[12:43, :] = f32(depth[...])
    vec[...] = low(vec_wide[...])
    seg[...] = jnp.zeros_like(seg)
    seg[0:rows, :] = segments[...]

    barrier = pltpu.get_barrier_semaphore()
    for there in [(dp, peer(k)) for k in range(1, 8)] + [(lax.rem(dp + k, 4), seq) for k in (1, 2, 3)]:
        pl.semaphore_signal(barrier, inc=1, device_id=there, device_id_type=MESH_ID)
    pl.semaphore_wait(barrier, 10)

    q_own, q_x, q_y = PIECE * dp, PIECE * (y * 2 + 1 - x), PIECE * ((1 - y) * 2 + x)

    def travel(kind, t, k, first, rows_, there, src=None):
        source = seq if src is not None else lax.rem(z - k + 4, 4) * 2 + core
        where = full.at[t, source, pl.ds(pl.multiple_of(first, 16), rows_)]
        return remote_copy(
            where if src is None else src,
            where,
            gather_sem.at[0, kind, t, k - 1],
            gather_sem.at[1, kind, t, k - 1],
            there,
        )

    def line(t, k):
        src = shards.at[t, pl.ds(pl.multiple_of(q_own, 16), PIECE)]
        return travel(0, t, k, q_own, PIECE, (dp, lax.rem(z + k, 4) * 2 + core), src)

    def to_x(t, k):
        return travel(1, t, k, q_own, PIECE, over_x)

    def to_y(t, k):
        return travel(2, t, k, q_own, PIECE, over_y)

    def on_x(t, k):
        return travel(3, t, k, q_y, PIECE // 2, over_x)

    def on_y(t, k):
        return travel(4, t, k, q_x + PIECE // 2, PIECE // 2, over_y)

    def to_core(t, k):
        return travel(5, t, k, 0, 4 * PIECE, over_core)

    def own_to_core(t):
        return remote_copy(
            shards.at[t], full.at[t, seq], own_sem.at[0, t], own_sem.at[1, t], over_core
        )

    def own_to_full(t):
        return pltpu.make_async_copy(shards.at[t], full.at[t, seq], own_sem.at[2, t])

    def small_copies():
        copies = []
        for k in range(1, 8):
            for i, (src, dst) in enumerate(((vec, vec_all), (seg, seg_all))):
                copies.append(
                    remote_copy(
                        src,
                        dst.at[seq],
                        small_sem.at[0, i, k - 1],
                        small_sem.at[1, i, k - 1],
                        (dp, peer(k)),
                    )
                )
        return copies

    for copy in small_copies():
        copy.start()
    vec_all[seq] = vec[...]
    seg_all[seq] = seg[...]
    def relay(t):
        where = full.at[t, lax.rem(z + 2, 4) * 2 + core, pl.ds(pl.multiple_of(q_own, 16), PIECE)]
        return remote_copy(
            where,
            where,
            gather_sem.at[0, 6, t, 0],
            gather_sem.at[1, 0, t, 2 * z - 2],
            (dp, 3 * (z - 1) * 2 + core),
        )

    def direct(k):
        return {1: z != 3, 2: z >= 0, 3: z != 0}[k]

    def in_time(k):
        return {1: z != 0, 2: z >= 0, 3: z != 3}[k]

    relays = (z == 1) | (z == 2)

    def start_line(t):
        read_done(t)
        own_to_core(t).start()
        own_to_full(t).start()
        for k in (1, 2, 3):

            @pl.when(direct(k))
            def _():
                line(t, k).start()

    def arrived(t, k):
        line(t, k).wait_recv()
        to_x(t, k).start()
        to_y(t, k).start()

    for t in range(LEAD):
        start_line(t)

    def gather_step(step):
        @pl.when(step + LEAD < CHUNKS)
        def _():
            start_line(step + LEAD)

        @pl.when(step < CHUNKS)
        def _():
            for k in (2, 1, 3):

                @pl.when(in_time(k))
                def _():
                    arrived(step, k)

                if k == 2:

                    @pl.when(relays)
                    def _():
                        relay(step).start()

        late = step - STAGE

        @pl.when((late >= 0) & (late < CHUNKS))
        def _():
            for k in (1, 3):

                @pl.when(jnp.logical_not(in_time(k)))
                def _():
                    arrived(late, k)

        second, third, last = step - 2 * STAGE, step - 3 * STAGE, step - 4 * STAGE

        @pl.when((second >= 0) & (second < CHUNKS))
        def _():
            for k in (1, 2, 3):
                to_y(second, k).wait_recv()
                on_x(second, k).start()
                to_x(second, k).wait_recv()
                on_y(second, k).start()

        @pl.when((third >= 0) & (third < CHUNKS))
        def _():
            for k in (1, 2, 3):
                on_x(third, k).wait_recv()
                on_y(third, k).wait_recv()
                to_core(third, k).start()

        @pl.when((last >= 0) & (last < CHUNKS))
        def _():
            for k in (1, 2, 3):
                to_core(last, k).wait_recv()
            own_to_core(last).wait_recv()
            own_to_full(last).wait()

    def load(u):
        return pltpu.make_async_copy(full.at[u], wbuf.at[lax.rem(u, 3)], load_sem.at[lax.rem(u, 3)])

    def weight(u):
        load(u).wait()
        return wbuf[lax.rem(u, 3)].reshape(width, width)

    def vector(i):
        return vectors[i : i + 1, :]

    def norm(v, i):
        return low(norm_rows(v, vector(i), vector(6 + i)))

    def prepare():
        for copy in small_copies():
            copy.wait()
        for s in range(8):
            vectors[:, s * 128 : s * 128 + 128] = f32(vec_all[s])
            columns = f32(seg_all[s]).T
            for r in range(rows):
                seg_cols[r, s * 128 : s * 128 + 128, :] = columns[:, r : r + 1]
                seg_rows[r : r + 1, s * 128 : s * 128 + 128] = f32(seg_all[s, r : r + 1, :])
        before = jnp.where(seq > 0, f32(seg_all[lax.max(seq - 1, 0)]), -1.0).T
        middle = f32(seg_all[seq]).T
        after = jnp.where(seq < 7, f32(seg_all[lax.min(seq + 1, 7)]), -1.0).T
        for r in range(rows):
            for first, col in (
                (0, before[frame_count - HALO :, r : r + 1]),
                (HALO, middle[:, r : r + 1]),
                (HALO + frame_count, after[:HALO, r : r + 1]),
            ):
                seg_plane[r, first : first + col.shape[0], :] = jnp.broadcast_to(col, (col.shape[0], 128))
        keys = lax.broadcasted_iota(jnp.int32, (TILE, TILE), 0)
        queries = lax.broadcasted_iota(jnp.int32, (TILE, TILE), 1)
        for i in range(2 * TILES - 1):
            apart = jnp.abs(keys - queries + TILE * (i - TILES + 1))
            e.distances[i] = jnp.log(1.0 + apart.astype(jnp.float32))
        norm0[...] = norm(f32(frames[...]), 0)

    def up(u, j, source):
        value = dot(source[...], weight(u))
        active = low(value * logistic(value))
        value = low(value)
        for half in range(2):
            to = pl.ds(pl.multiple_of((j * 2 + half) * 128, 128), 128)
            for i in range(4):
                first = half * 512 + i * 128
                pre[i, :, to] = value[:, first : first + 128]
                hid[i, :, to] = active[:, first : first + 128]

    def down(u, j, stream, target):
        value = dot(hid[j], weight(u))

        @pl.when(j == 0)
        def _():
            acc[...] = value

        @pl.when(j > 0)
        def _():
            acc[...] += value

        @pl.when(j == 3)
        def _():
            target[...] = f32(stream[...]) + 0.5 * acc[...]

    def keep_copies():
        return [
            pltpu.make_async_copy(pre, e.pre_keep, keep_sem.at[0]),
            pltpu.make_async_copy(hid, e.hid_keep, keep_sem.at[1]),
        ]

    def pk_copy(c, k, recv=False):
        there = peer(k)
        return remote_copy(
            pk_out.at[there, c],
            packed.at[there if recv else seq, c],
            pk_sem.at[0, there, c],
            pk_sem.at[1, there if recv else seq, c],
            (dp, there),
        )

    def project(u, c):
        value = low(dot(norm1[...], weight(u)))
        for s in range(8):
            pk_out[s, c] = value[:, s * 128 : s * 128 + 128].reshape(rows, frame_count, 128)
        packed[seq, c] = pk_out[seq, c]
        for k in range(1, 8):
            pk_copy(c, k).start()

    def att_copy(b, r, recv=False):
        return remote_copy(
            att_out.at[b, r],
            att_in.at[b if recv else seq, r],
            att_sem.at[0, b, r],
            att_sem.at[1, b if recv else seq, r],
            (dp, b),
        )

    def attend_step(i):
        row, block = i // 4, lax.rem(i, 4)
        out = attend_block(e, seq * 2, row, block)
        e.att_keep[row, pl.ds(pl.multiple_of(block * QUERIES, QUERIES), QUERIES), :] = out
        out = low(out)
        for half in range(2):
            b = block * 2 + half
            att_out[b, row] = out[half * 128 : half * 128 + 128]

            @pl.when(b != seq)
            def _():
                att_copy(b, row).start()

            @pl.when(b == seq)
            def _():
                att_in[b, row] = out[half * 128 : half * 128 + 128]

    def halo_copy(side):
        if side == 0:
            src, dst, there = gated.at[:, pl.ds(HALO, HALO)], gated.at[:, pl.ds(HALO + frame_count, HALO)], lax.rem(seq + 7, 8)
        else:
            src, dst, there = gated.at[:, pl.ds(frame_count, HALO)], gated.at[:, pl.ds(0, HALO)], lax.rem(seq + 1, 8)
        return remote_copy(src, dst, halo_sem.at[0, side], halo_sem.at[1, side], (dp, there))

    def convolve():
        @pl.when(seq > 0)
        def _():
            halo_copy(0).wait_send()
            halo_copy(1).wait_recv()

        @pl.when(seq < 7)
        def _():
            halo_copy(1).wait_send()
            halo_copy(0).wait_recv()

        gated_f[...] = f32(gated[...])

        def lanes(i, _):
            at = pl.ds(pl.multiple_of(i * 128, 128), 128)
            for r in range(rows):
                own = seg_plane[r, HALO : HALO + frame_count, :]
                total = jnp.zeros((frame_count, 128), jnp.float32)
                for shift in range(8):
                    near = gated_f[r, shift : shift + frame_count + 24, at]
                    seg_near = seg_plane[r, shift : shift + frame_count + 24, :]
                    for first in range(0, 32, 8):
                        tap = shift + first - 1
                        if 0 <= tap < 31:
                            same = seg_near[first : first + frame_count] == own
                            term = near[first : first + frame_count] * vectors[12 + tap : 13 + tap, at]
                            total = total + jnp.where(same, term, 0.0)
                mixed[r * frame_count : (r + 1) * frame_count, at] = total
            return 0

        lax.fori_loop(0, width // 128, lanes, 0)

    def step_work(step, _):
        gather_step(step)

        now = step - STEP

        def at(first, count=1):
            return pl.when((now >= first) & (now < first + count))

        @at(0)
        def _():
            prepare()

        @at(1, 4)
        def _():
            up(now - 1, now - 1, norm0)

        @at(5, 4)
        def _():
            down(now - 1, now - 5, frames, after_front)

        @at(9, 3)
        def _():
            @pl.when(now == 9)
            def _():
                norm1[...] = norm(after_front[...], 1)
                for copy in keep_copies():
                    copy.start()

            project(now - 1, now - 9)

        @at(13)
        def _():
            for c in range(3):
                for k in range(1, 8):
                    pk_copy(c, k, True).wait_recv()

        @at(13, 4)
        def _():
            def one(i, _):
                attend_step((now - 13) * 2 + i)
                return 0

            lax.fori_loop(0, 2, one, 0)

        @at(17)
        def _():
            for r in range(rows):
                for k in range(1, 8):
                    att_copy(peer(k), r, True).wait_recv()
            for s in range(8):
                attended[:, s * 128 : s * 128 + 128] = att_in[s].reshape(rows * frame_count, 128)
            after_attend[...] = after_front[...] + dot(attended[...], weight(ATTEND_OUT))
            norm2[...] = norm(after_attend[...], 2)

        @at(18)
        def _():
            acc[...] = dot(norm2[...], weight(POINT_IN))
            conv_pre[0] = low(acc[...])
            gate = dot(norm2[...], weight(POINT_IN + 1))
            conv_pre[1] = low(gate)
            value = low(acc[...] * logistic(gate))
            gated[:, HALO : HALO + frame_count] = value.reshape(rows, frame_count, width)

            @pl.when(seq > 0)
            def _():
                halo_copy(0).start()

            @pl.when(seq < 7)
            def _():
                halo_copy(1).start()

        @at(19)
        def _():
            convolve()
            value = norm_rows(mixed[...], vector(3), vector(9))
            act[...] = low(value * logistic(value))
            after_conv[...] = after_attend[...] + dot(act[...], weight(POINT_OUT))
            norm4[...] = norm(after_conv[...], 4)

        @at(20, 2)
        def _():
            @pl.when(now == 20)
            def _():
                for copy in keep_copies():
                    copy.wait()

            for i in range(2):
                j = (now - 20) * 2 + i
                up(j + REAR_UP, j, norm4)

        @at(22, 2)
        def _():
            for i in range(2):
                j = (now - 22) * 2 + i
                down(j + REAR_DOWN, j, after_conv, after_rear)

        @at(0, 14)
        def _():
            load(now).start()

        for when, chunks in ((17, (14,)), (18, (15, 16)), (19, (17,)), (20, (18, 19)), (21, (20, 21)), (22, (22,))):

            @at(when)
            def _(chunks=chunks):
                for u in chunks:
                    load(u).start()

        return 0

    lax.fori_loop(0, STEP + 24, step_work, 0)

    def drain(t, _):
        for kind in (to_x, to_y, on_x, on_y, to_core):
            for k in (1, 2, 3):
                kind(t, k).wait_send()
        for k in (1, 2, 3):

            @pl.when(direct(k))
            def _():
                line(t, k).wait_send()

        @pl.when(relays)
        def _():
            relay(t).wait_send()

        own_to_core(t).wait_send()
        return 0

    lax.fori_loop(0, CHUNKS, drain, 0)
    for c in range(3):
        for k in range(1, 8):
            pk_copy(c, k).wait_send()
    for r in range(rows):
        for k in range(1, 8):
            att_copy(peer(k), r).wait_send()


JOB_RU, JOB_PO, JOB_PI, JOB_AO, JOB_P, JOB_FD, JOB_FU, JOBS = 4, 8, 9, 11, 12, 15, 19, 23
RING = 4
GRADS = ((7, True), (6, False), (5, False), (4, False), (3, False), (2, False), (1, True), (0, False))
OUT_LAG = 6


def silu_slope(pre, grad):
    gate = logistic(pre)
    return grad * gate * (1.0 + pre * (1.0 - gate))


def tn(a, b):
    return lax.dot_general(a, b, (((0,), (0,)), ((), ())), preferred_element_type=jnp.float32)


def backward_part(e):
    full, gated, mixed, act, packed = e.full, e.gated, e.mixed, e.act, e.packed
    norm0, norm1, norm2, norm4, attended, conv_pre = (
        e.norm0,
        e.norm1,
        e.norm2,
        e.norm4,
        e.attended,
        e.conv_pre,
    )
    after_front, after_attend, after_conv, after_rear = (
        e.after_front,
        e.after_attend,
        e.after_conv,
        e.after_rear,
    )
    frames, cotangent, slopes = e.frames, e.cotangent, e.slopes
    result, frames_grad, vec_out, grads = e.result, e.frames_grad, e.vec_out, e.grads
    pre_grads, hid, wbuf, vectors, pool = e.pre, e.hid, e.wbuf, e.vectors, e.pool
    small, left, right, branch, conv_branch = e.small, e.left, e.right, e.branch, e.conv_branch
    gate_grads, attend_branch, parts = e.gate_grads, e.attend_branch, e.parts
    grad, total, gated_f, mixed_w, mixed_f = e.grad, e.total, e.gated_f, e.mixed_w, e.mixed_f
    seg_plane, seg_rows = e.seg_plane, e.seg_rows
    g_out, g_in, p_out, p_in = e.att_out, e.g_in, e.pk_out, e.p_in
    key_sum, value_sum, slope_sum, out_buf = e.key_sum, e.value_sum, e.slope_sum, e.out_buf
    h_buf, a_buf, b_buf, q_buf = e.h_buf, e.a_buf, e.b_buf, e.q_buf
    a_in, b_in, a2_in, b2_in, z_in, o_buf = e.a_in, e.b_in, e.a2_in, e.b2_in, e.z_in, e.o_buf
    vec_send, vec_in, vec_dp = e.vec_send, e.vec_in, e.vec_dp
    sem, vec_sem, load_sem, keep_sem, ga_sem, pk_sem, halo_sem, out_sem, sync = e.backward_sems
    y, x, z, core = place()
    dp, seq = y * 2 + x, z * 2 + core
    rows, width, frame_count = 2, 1024, 128
    length = 8 * frame_count
    over_x = (y * 2 + 1 - x, seq)
    over_y = ((1 - y) * 2 + x, seq)
    over_core = (dp, z * 2 + 1 - core)

    def peer(k):
        return lax.rem(seq + k, 8)

    def dp_peer(k):
        return (lax.rem(dp + k, 4), seq)

    pl.semaphore_signal(sync, inc=1, device_id=over_core, device_id_type=MESH_ID)
    pl.semaphore_wait(sync, 1)
    mine = 4 * RING

    def remote(src, dst, t, slot, there):
        return remote_copy(
            src, dst, sem.at[0, slot, lax.rem(t, RING)], sem.at[1, slot, lax.rem(t, RING)], there
        )

    def core_copies(t, r):
        return [
            remote(pool.at[pl.ds(mine + 4, 4)], pool.at[pl.ds(4 * r, 4)], t, 0, over_core)
        ]

    def first_copies(t, r):
        return [
            remote(h_buf.at[pl.ds(0, 2), :, 1 - x], a_in.at[r], t, 1, over_x),
            remote(h_buf.at[pl.ds(2, 2), 1 - y], b_in.at[r], t, 2, over_y),
        ]

    def second_copies(t, r):
        return [
            remote(a_buf.at[:, 1 - y], a2_in.at[r], t, 3, over_y),
            remote(b_buf.at[:, 1 - x], b2_in.at[r], t, 4, over_x),
        ]

    def line_copies(t, r):
        copies = []
        for k in (1, 2, 3):
            to = lax.rem(z + k, 4)
            copies.append(remote(q_buf.at[to], z_in.at[r, k - 1], t, 4 + k, (dp, to * 2 + core)))
        return copies

    def share_copies(t, r):
        where = o_buf.at[r, dp]
        return [remote(where, where, t, 8, over_x), remote(where, where, t, 9, over_y)]

    def across_copies(t, r):
        one = o_buf.at[r, (1 - y) * 2 + x, pl.ds(0, PIECE // 2)]
        two = o_buf.at[r, y * 2 + 1 - x, pl.ds(PIECE // 2, PIECE // 2)]
        return [remote(one, one, t, 10, over_x), remote(two, two, t, 11, over_y)]

    def out_start(t):
        slot = lax.rem(t, 2)
        first = 0
        for out, tall in GRADS:
            ref = grads[out]
            size = 128 if tall else width
            count = ref.shape[0] // size if tall else ref.shape[1] // size

            @pl.when((t >= first) & (t < first + count))
            def _(ref=ref, tall=tall, size=size, first=first):
                at = pl.ds(pl.multiple_of((t - first) * size, size), size)
                where = ref.at[at, :] if tall else ref.at[:, at]
                pltpu.make_async_copy(out_buf.at[slot], where, out_sem.at[slot]).start()

            first += count

    def out_done(t):
        slot = lax.rem(t, 2)
        pltpu.make_async_copy(out_buf.at[slot], out_buf.at[slot], out_sem.at[slot]).wait()

    def finish(copies):
        for copy in copies:
            copy.wait()

    def begin(copies):
        for copy in copies:
            copy.start()

    def write_out(t, r):
        finish(across_copies(t, r))

        @pl.when(t >= 2)
        def _():
            out_done(t - 2)

        out_buf[lax.rem(t, 2)] = f32(o_buf[r].reshape(128, width))
        out_start(t)

    def pass_on(t, r):
        finish(share_copies(t, r))
        begin(across_copies(t, r))

    def total_line(t, r):
        finish(line_copies(t, r))
        value = f32(q_buf[z]) + f32(z_in[r, 0]) + f32(z_in[r, 1]) + f32(z_in[r, 2])
        o_buf[r, dp] = low(value)
        begin(share_copies(t, r))

    def total_second(t, r):
        finish(second_copies(t, r))
        q_buf[0:2] = low(f32(a_buf[:, y]) + f32(a2_in[r]))
        q_buf[2:4] = low(f32(b_buf[:, x]) + f32(b2_in[r]))
        begin(line_copies(t, r))

    def total_first(t, r):
        finish(first_copies(t, r))
        a_buf[...] = low(f32(h_buf[0:2, :, x]) + f32(a_in[r]))
        b_buf[...] = low(f32(h_buf[2:4, y]) + f32(b_in[r]))
        begin(second_copies(t, r))

    def total_core(t, r):
        finish(core_copies(t, r))
        for i in range(4):
            value = low(f32(pool[mine + i]) + f32(pool[4 * r + i]))
            h_buf[i] = value.reshape(2, 2, PIECE, width)
        begin(first_copies(t, r))

    def product(t, r):
        for i in range(8):
            part = tn(left[:, 128 * i : 128 * i + 128], right[...])
            pool[mine + 4 * lax.rem(core + i, 2) + i // 2] = low(part)
        begin(core_copies(t, r))

    sums = [total_core, total_first, total_second, total_line, pass_on, write_out]

    def sum_step(step):
        for depth in reversed(range(1, 7)):
            t = step - depth

            @pl.when((t >= 0) & (t < JOBS))
            def _(t=t, depth=depth):
                sums[depth - 1](t, lax.rem(t, RING))

    def load(i, u):
        return pltpu.make_async_copy(full.at[u], wbuf.at[i], load_sem.at[i])

    def weight(i, u):
        load(i, u).wait()
        return wbuf[i].reshape(width, width)

    def keep_copies():
        return [
            pltpu.make_async_copy(e.pre_keep, pre_grads, keep_sem.at[0]),
            pltpu.make_async_copy(e.hid_keep, hid, keep_sem.at[1]),
        ]

    def vector(i):
        return vectors[i : i + 1, :]

    def norm_back(v, i, dy):
        centred = v - jnp.mean(v, axis=-1, keepdims=True)
        rstd = lax.rsqrt(jnp.mean(centred * centred, axis=-1, keepdims=True) + 1e-05)
        n = centred * rstd
        small[i : i + 1, :] = jnp.sum(dy * n, axis=0, keepdims=True)
        small[6 + i : 7 + i, :] = jnp.sum(dy, axis=0, keepdims=True)
        dn = dy * vector(i)
        first = jnp.mean(dn, axis=-1, keepdims=True)
        second = jnp.mean(dn * n, axis=-1, keepdims=True)
        return rstd * (dn - first - n * second)

    def strided(b):
        blocks = []
        for half in range(2):
            at = pl.ds(pl.multiple_of((b * 2 + half) * 128, 128), 128)
            blocks += [pre_grads[j, :, at] for j in range(4)]
        return jnp.concatenate(blocks, axis=1)

    def down_back(j, down):
        hidden_grad = nt(branch[...], weight(lax.rem(j, 2), down + j))
        pre_grads[j] = low(silu_slope(f32(pre_grads[j]), hidden_grad))

    def up_back(b, up):
        value = nt(strided(b), weight(lax.rem(b, 2), up + b))

        @pl.when(b == 0)
        def _():
            total[...] = value

        @pl.when(b > 0)
        def _():
            total[...] += value

    def prepare():
        small[...] = jnp.zeros_like(small)
        slope_sum[...] = jnp.zeros_like(slope_sum)

    def halo_copy(side):
        if side == 0:
            src, dst = pl.ds(HALO, HALO), pl.ds(HALO + frame_count, HALO)
            there = lax.rem(seq + 7, 8)
        else:
            src, dst = pl.ds(frame_count, HALO), pl.ds(0, HALO)
            there = lax.rem(seq + 1, 8)
        return remote_copy(
            mixed_w.at[:, src],
            mixed_w.at[:, dst],
            halo_sem.at[0, side],
            halo_sem.at[1, side],
            (dp, there),
        )

    def convolve_back(r):
        def lanes(i, _):
            at = pl.ds(pl.multiple_of(i * 128, 128), 128)
            own = seg_plane[r, HALO : HALO + frame_count, :]
            mine = mixed_f[r, HALO : HALO + frame_count, at]
            value = jnp.zeros((frame_count, 128), jnp.float32)
            for shift in range(8):
                window = slice(shift, shift + frame_count + 24)
                seg_near = seg_plane[r, window, :]
                gated_near = gated_f[r, window, at]
                mixed_near = mixed_f[r, window, at]
                for first in range(0, 32, 8):
                    tap = shift + first - 1
                    if 0 <= tap < 31:
                        here = slice(first, first + frame_count)
                        same = seg_near[here] == own
                        near = jnp.where(same, gated_near[here], 0.0)
                        small[12 + tap : 13 + tap, at] += jnp.sum(near * mine, axis=0, keepdims=True)
                        came = jnp.where(same, mixed_near[here], 0.0)
                        value = value + came * vectors[12 + 30 - tap : 13 + 30 - tap, at]
            total[r * frame_count : (r + 1) * frame_count, at] = value
            return 0

        lax.fori_loop(0, width // 128, lanes, 0)

    def ga_copy(k, recv=False):
        there = peer(k)
        return remote_copy(
            g_out.at[there],
            g_in.at[there if recv else seq],
            ga_sem.at[0, there],
            ga_sem.at[1, there if recv else seq],
            (dp, there),
        )

    def pk_copy(there, c, r, recv=False):
        return remote_copy(
            p_out.at[there, c, r],
            p_in.at[there if recv else seq, c, r],
            pk_sem.at[0, there, c, r],
            pk_sem.at[1, there if recv else seq, c, r],
            (dp, there),
        )

    def attend_back_step(i):
        row, block = i // 4, lax.rem(i, 4)
        first = pl.multiple_of(block * QUERIES, QUERIES)
        query_seg = seg_rows[pl.ds(row, 1), pl.ds(first, QUERIES)]
        q = packed[pl.ds(block * 2, 2), 0, row].reshape(QUERIES, 128)
        g = g_in[pl.ds(block * 2, 2), row].reshape(QUERIES, 128)
        key_t = packed[:, 1, row].reshape(length, 128).T
        deltas = (f32(g) * e.att_keep[row, pl.ds(first, QUERIES), :]).T

        @pl.when(block == 0)
        def _():
            key_sum[...] = jnp.zeros_like(key_sum)
            value_sum[...] = jnp.zeros_like(value_sum)

        outs = []
        for head in range(2):
            q_head = head_lanes(q, head, 0.125)
            g_head = head_lanes(g, head)
            slope = slopes[seq * 2 + head]
            log_sum = e.log_sum[row, head, :, pl.ds(first, QUERIES)]
            delta = jnp.sum(deltas[64 * head : 64 * head + 64], axis=0, keepdims=True)
            slope_total = jnp.zeros((8, QUERIES), jnp.float32)
            for kb in range(TILES):
                at = slice(kb * TILE, kb * TILE + TILE)
                logit, distance = logit_tile(e, q_head, slope, query_seg, row, block, kb)
                prob = jnp.exp(logit - log_sum)
                prob_grad = nt(packed[kb, 2, row], g_head)
                value_sum[at, :] += dot(low(prob), g_head)
                logit_grad = prob * (prob_grad - delta)
                slope_total = slope_total + jnp.sum(
                    (logit_grad * distance).reshape(TILE // 8, 8, QUERIES), axis=0
                )
                score = low(logit_grad)
                e.scores[at, :] = score
                key_sum[at, :] += dot(score, q_head)
            slope_sum[head] -= slope_total
            query_t = dot(key_t, e.scores[...])
            outs.append(query_t[64 * head : 64 * head + 64] * 0.125)
        query = low(jnp.concatenate(outs, axis=0).T)

        def deliver(b, c, value):
            p_out[b, c, row] = value

            @pl.when(b != seq)
            def _():
                pk_copy(b, c, row).start()

            @pl.when(b == seq)
            def _():
                p_in[b, c, row] = value

        for half in range(2):
            deliver(block * 2 + half, 0, query[half * 128 : half * 128 + 128])

        @pl.when(block == 3)
        def _():
            for b in range(8):
                at = slice(b * 128, b * 128 + 128)
                deliver(b, 1, low(key_sum[at, :]))
                deliver(b, 2, low(value_sum[at, :]))

    def vec_copies():
        copies = []
        for k in range(1, 8):
            copies.append(
                remote_copy(
                    vec_send.at[peer(k)],
                    vec_in.at[seq],
                    vec_sem.at[0, k - 1],
                    vec_sem.at[1, k - 1],
                    (dp, peer(k)),
                )
            )
        return copies

    def vec_dp_copies():
        where = vec_dp.at[dp]
        return [
            remote_copy(where, where, vec_sem.at[0, 6 + k], vec_sem.at[1, 6 + k], dp_peer(k))
            for k in (1, 2, 3)
        ]

    def send_vectors():
        lane = lax.broadcasted_iota(jnp.int32, (1, 128), 1)
        mine = jnp.zeros((1, 128), jnp.float32)
        for head in range(2):
            value = jnp.sum(jnp.sum(slope_sum[head], axis=0, keepdims=True), axis=-1, keepdims=True)
            mine = mine + jnp.where(lane == seq * 2 + head, value, 0.0)
        for s in range(8):
            vec_send[s] = small[:, s * 128 : s * 128 + 128]
            vec_send[s, 43:44, :] = mine
        vec_in[seq] = vec_send[seq]
        begin(vec_copies())

    def sum_vectors():
        finish(vec_copies())
        value = vec_in[0]
        for i in range(1, 8):
            value = value + vec_in[i]
        vec_dp[dp] = value
        begin(vec_dp_copies())

    def finish_vectors():
        finish(vec_dp_copies())
        vec_out[...] = (vec_dp[0] + vec_dp[1]) + (vec_dp[2] + vec_dp[3])

    def stage(first, second):
        left[...] = first
        right[...] = second

    def step_work(step, _):
        sum_step(step)

        def at(first, count=1):
            return pl.when((step >= first) & (step < first + count))

        @at(0)
        def _():
            load(0, REAR_DOWN).start()
            load(1, REAR_DOWN + 1).start()
            prepare()
            result[...] = low(norm_rows(after_rear[...], vector(5), vector(11)))
            grad[...] = norm_back(after_rear[...], 5, f32(cotangent[...]))
            branch[...] = low(0.5 * grad[...])
            for j in range(4):
                down_back(j, REAR_DOWN)
                load(j % 2, REAR_DOWN + 2 + j if j < 2 else REAR_UP + j - 2).start()

        @at(1)
        def _():
            for b in range(4):
                up_back(b, REAR_UP)
                if b < 2:
                    load(b, REAR_UP + 2 + b).start()
            load(0, POINT_OUT).start()
            grad[...] += norm_back(after_conv[...], 4, total[...])
            conv_branch[...] = low(grad[...])

        @at(2)
        def _():
            act_grad = nt(conv_branch[...], weight(0, POINT_OUT))
            act_grad = silu_slope(norm_rows(mixed[...], vector(3), vector(9)), act_grad)
            value = low(norm_back(mixed[...], 3, act_grad))
            mixed_w[:, HALO : HALO + frame_count] = value.reshape(rows, frame_count, width)

            @pl.when(seq > 0)
            def _():
                halo_copy(0).start()

            @pl.when(seq < 7)
            def _():
                halo_copy(1).start()

            load(0, POINT_IN).start()
            load(1, POINT_IN + 1).start()

        @at(3)
        def _():
            @pl.when(seq > 0)
            def _():
                halo_copy(0).wait_send()
                halo_copy(1).wait_recv()

            @pl.when(seq < 7)
            def _():
                halo_copy(1).wait_send()
                halo_copy(0).wait_recv()

            mixed_f[...] = f32(mixed_w[...])
            convolve_back(0)

        @at(4)
        def _():
            convolve_back(1)

        @at(5)
        def _():
            gate = logistic(f32(conv_pre[1]))
            gate_grads[0] = low(total[...] * gate)
            gate_grads[1] = low(total[...] * f32(conv_pre[0]) * gate * (1.0 - gate))
            norm_grad = nt(gate_grads[0], weight(0, POINT_IN))
            load(0, ATTEND_OUT).start()
            norm_grad = norm_grad + nt(gate_grads[1], weight(1, POINT_IN + 1))
            grad[...] += norm_back(after_attend[...], 2, norm_grad)
            attend_branch[...] = low(grad[...])
            value = low(nt(attend_branch[...], weight(0, ATTEND_OUT)))
            for s in range(8):
                g_out[s] = value[:, s * 128 : s * 128 + 128].reshape(rows, frame_count, 128)
            g_in[seq] = g_out[seq]
            for k in range(1, 8):
                ga_copy(k).start()
            load(0, PROJECT).start()
            load(1, PROJECT + 1).start()

        @at(7)
        def _():
            for k in range(1, 8):
                ga_copy(k, True).wait_recv()
                ga_copy(k).wait_send()

        @at(7, 4)
        def _():
            def one(i, _):
                attend_back_step((step - 7) * 2 + i)
                return 0

            lax.fori_loop(0, 2, one, 0)

        @at(12)
        def _():
            for c in range(3):
                for r in range(rows):
                    for k in range(1, 8):
                        pk_copy(peer(k), c, r, True).wait_recv()
                        pk_copy(peer(k), c, r).wait_send()
                for s in range(8):
                    parts[c, :, s * 128 : s * 128 + 128] = p_in[s, c].reshape(
                        rows * frame_count, 128
                    )
            norm_grad = nt(parts[0], weight(0, PROJECT))
            load(0, PROJECT + 2).start()
            norm_grad = norm_grad + nt(parts[1], weight(1, PROJECT + 1))
            load(1, DOWN + 1).start()
            norm_grad = norm_grad + nt(parts[2], weight(0, PROJECT + 2))
            load(0, DOWN).start()
            grad[...] += norm_back(after_front[...], 1, norm_grad)
            branch[...] = low(0.5 * grad[...])

        @at(8)
        def _():
            for copy in keep_copies():
                copy.start()

        @at(13, 2)
        def _():
            @pl.when(step == 13)
            def _():
                for copy in keep_copies():
                    copy.wait()

            for i in range(2):
                j = (step - 13) * 2 + i
                down_back(j, DOWN)
                load(i, lax.rem(DOWN + 2 + j, PROJECT)).start()

        @at(15, 2)
        def _():
            for i in range(2):
                b = (step - 15) * 2 + i
                up_back(b, UP)

                @pl.when(b < 2)
                def _(b=b, i=i):
                    load(i, UP + 2 + b).start()

        @at(17)
        def _():
            frames_grad[...] = low(
                grad[...] + norm_back(f32(frames[...]), 0, total[...])
            )
            send_vectors()

        @at(19)
        def _():
            sum_vectors()

        @at(21)
        def _():
            finish_vectors()

        @at(0, JOB_RU)
        def _():
            stage(hid[step], branch[...])

        @at(JOB_RU, 4)
        def _():
            stage(norm4[...], strided(step - JOB_RU))

        @at(JOB_PO)
        def _():
            stage(act[...], conv_branch[...])

        @at(JOB_PI, 2)
        def _():
            stage(norm2[...], gate_grads[step - JOB_PI])

        @at(JOB_AO)
        def _():
            stage(attended[...], attend_branch[...])

        @at(JOB_P, 3)
        def _():
            stage(norm1[...], parts[step - JOB_P])

        @at(JOB_FD, 4)
        def _():
            stage(hid[step - JOB_FD], branch[...])

        @at(JOB_FU, 4)
        def _():
            stage(norm0[...], strided(step - JOB_FU))

        @at(0, JOBS)
        def _():
            product(step, lax.rem(step, RING))

        return 0

    lax.fori_loop(0, JOBS + OUT_LAG, step_work, 0)
    out_done(JOBS - 2)
    out_done(JOBS - 1)


class Refs:
    pass


def layer(weights, gains, biases, depth, segments, frames, cotangent, slopes):
    bf16, single = jnp.bfloat16, jnp.float32
    tokens, width = frames.shape
    tall = 128 + 2 * HALO
    dma = pltpu.SemaphoreType.DMA
    vmem, hbm = pl.BlockSpec(memory_space=pltpu.VMEM), pl.BlockSpec(memory_space=pltpu.HBM)

    def buf(kind, *sizes):
        return pltpu.VMEM(sizes, kind)

    plain, wide = buf(bf16, tokens, width), buf(single, tokens, width)
    four = buf(bf16, 4, tokens, width)
    quarter = (PIECE, width)
    scratch = dict(
        vec_all=buf(bf16, 8, VECTORS, 128),
        seg_all=buf(jnp.int32, 8, 8, 128),
        norm0=plain,
        norm1=plain,
        norm2=plain,
        norm4=plain,
        attended=plain,
        act=plain,
        pre=four,
        hid=four,
        packed=buf(bf16, 8, 3, 2, 128, 128),
        conv_pre=buf(bf16, 2, tokens, width),
        gated=buf(bf16, 2, tall, width),
        mixed=wide,
        after_front=wide,
        after_attend=wide,
        after_conv=wide,
        after_rear=wide,
        wbuf=buf(bf16, 3, 8, 128, width),
        vectors=buf(single, VECTORS, width),
        pool=buf(bf16, 4 * RING + 8, 128, width),
        pk_out=buf(bf16, 8, 3, 2, 128, 128),
        att_out=buf(bf16, 8, 2, 128, 128),
        att_in=buf(bf16, 8, 2, 128, 128),
        att_keep=buf(single, 2, 1024, 128),
        log_sum=buf(single, 2, 2, 1, 1024),
        logits=buf(single, TILES, TILE, QUERIES),
        scores=buf(bf16, TILES * TILE, QUERIES),
        distances=buf(single, 2 * TILES - 1, TILE, TILE),
        gated_f=buf(single, 2, tall, width),
        seg_plane=buf(single, 2, tall, 128),
        seg_cols=buf(single, 2, 1024, 1),
        seg_rows=buf(single, 8, 1024),
        vec_wide=buf(single, VECTORS, 128),
        vec=buf(bf16, VECTORS, 128),
        seg=buf(jnp.int32, 8, 128),
        small=buf(single, VECTORS, width),
        left=plain,
        right=plain,
        branch=plain,
        conv_branch=plain,
        gate_grads=buf(bf16, 2, tokens, width),
        attend_branch=plain,
        parts=buf(bf16, 3, tokens, width),
        grad=wide,
        total=wide,
        mixed_w=buf(bf16, 2, tall, width),
        mixed_f=buf(single, 2, tall, width),
        g_in=buf(bf16, 8, 2, 128, 128),
        p_in=buf(bf16, 8, 3, 2, 128, 128),
        key_sum=buf(single, 1024, 128),
        value_sum=buf(single, 1024, 128),
        slope_sum=buf(single, 2, 8, QUERIES),
        out_buf=buf(single, 2, 128, width),
        h_buf=buf(bf16, 4, 2, 2, *quarter),
        a_buf=buf(bf16, 2, 2, *quarter),
        b_buf=buf(bf16, 2, 2, *quarter),
        q_buf=buf(bf16, 4, *quarter),
        a_in=buf(bf16, RING, 2, 2, *quarter),
        b_in=buf(bf16, RING, 2, 2, *quarter),
        a2_in=buf(bf16, RING, 2, *quarter),
        b2_in=buf(bf16, RING, 2, *quarter),
        z_in=buf(bf16, RING, 3, *quarter),
        o_buf=buf(bf16, RING, 4, *quarter),
        vec_send=buf(single, 8, VECTORS, 128),
        vec_in=buf(single, 8, VECTORS, 128),
        vec_dp=buf(single, 4, VECTORS, 128),
    )
    forward_sems = [(2, 7, CHUNKS, 3), (4, CHUNKS), (2, 2, 7), (2, 8, 3), (2, 8, 2), (2, 2), (3,), (2,)]
    backward_sems = [(2, 12, RING), (2, 10), (2,), (2,), (2, 8), (2, 8, 3, 2), (2, 2), (2,)]
    count = len(forward_sems)

    def kernel(*refs):
        e = Refs()
        e.sources = refs[:8]
        e.gains, e.biases, e.depth, e.segments, e.frames, e.cotangent, e.slopes = refs[8:15]
        e.result, e.frames_grad, e.vec_out = refs[15:18]
        e.grads = refs[18:26]
        e.full, e.pre_keep, e.hid_keep = refs[26:29]
        for name, ref in zip(scratch, refs[29:]):
            setattr(e, name, ref)
        sems = refs[29 + len(scratch) :]
        e.forward_sems, e.backward_sems = sems[:count], sems[count:]
        for wide_ref in (e.gated, e.mixed_w):
            wide_ref[:, :HALO] = jnp.zeros((2, HALO, width), bf16)
            wide_ref[:, HALO + 128 :] = jnp.zeros((2, HALO, width), bf16)
        forward_part(e)
        backward_part(e)

    shape = jax.ShapeDtypeStruct
    return pl.pallas_call(
        kernel,
        in_specs=[hbm] * 8 + [vmem] * 6 + [pl.BlockSpec(memory_space=pltpu.SMEM)],
        out_specs=[vmem] * 3 + [hbm] * 11,
        out_shape=[
            shape((tokens, width), bf16),
            shape((tokens, width), bf16),
            shape((VECTORS, 128), single),
        ]
        + [shape(weight.shape, single) for weight in weights]
        + [shape((CHUNKS, 8, 128, width), bf16)]
        + [shape((4, tokens, width), bf16)] * 2,
        scratch_shapes=list(scratch.values())
        + [dma(sizes) for sizes in forward_sems + backward_sems]
        + [pltpu.SemaphoreType.REGULAR],
        compiler_params=pltpu.CompilerParams(
            collective_id=0, has_side_effects=True, vmem_limit_bytes=VMEM_LIMIT
        ),
        name="layer",
    )(*weights, gains, biases, depth, segments, frames, cotangent, slopes)


def body_staged(
    frames,
    segments,
    cotangent,
    norm_gains,
    norm_biases,
    front_up,
    front_down,
    attend_in,
    attend_out,
    slopes,
    point_in,
    depthwise,
    point_out,
    rear_up,
    rear_down,
):
    width = frames.shape[2]
    token_count = frames.shape[0] * frames.shape[1]
    taps = depthwise.shape[0]

    weights = (
        front_up,
        front_down,
        attend_in,
        attend_out,
        point_in,
        point_out,
        rear_up,
        rear_down,
    )
    tokens = frames.reshape(token_count, width)
    result, frames_grad, vectors, *grads = layer(
        weights,
        norm_gains,
        norm_biases,
        depthwise,
        segments,
        tokens,
        cotangent.reshape(token_count, width),
        slopes,
    )
    grads = grads[:8]
    return (
        result.reshape(frames.shape),
        frames_grad.reshape(frames.shape),
        vectors[:6],
        vectors[6:12],
        *grads[:4],
        vectors[12 + taps, : slopes.shape[0]],
        grads[4],
        vectors[12 : 12 + taps],
        *grads[5:],
    )


def solution(mesh):
    placed = (
        P("dp", "seq", None),
        P("dp", "seq"),
        P("dp", "seq", None),
        P(None, "seq"),
        P(None, "seq"),
        P("seq", None),
        P("seq", None),
        P("seq", None),
        P("seq", None),
        P(),
        P("seq", None),
        P(None, "seq"),
        P("seq", None),
        P("seq", None),
        P("seq", None),
    )
    sizes = mesh.shape
    staged = sizes["dp"] == 4 and sizes["seq"] == 8
    return jax.shard_map(
        body_staged if staged else body,
        mesh=mesh,
        in_specs=placed,
        out_specs=(
            P("dp", "seq", None),
            P("dp", "seq", None),
            P(None, "seq"),
            P(None, "seq"),
            P("seq", None),
            P("seq", None),
            P("seq", None),
            P("seq", None),
            P(),
            P("seq", None),
            P(None, "seq"),
            P("seq", None),
            P("seq", None),
            P("seq", None),
        ),
        check_vma=False,
    )
```

```python
import jax
import jax.numpy as jnp
from jax import lax
from jax.experimental import pallas as pl
from jax.experimental.pallas import tpu as pltpu
from jax.sharding import PartitionSpec as P


def padded(value, sides, width):
    for axis, dim in sides:
        peers, length = (lax.axis_size(axis), value.shape[dim])
        up = [(i, (i + 1) % peers) for i in range(peers - 1)]
        down = [(j, i) for i, j in up]
        last = lax.slice_in_dim(value, length - width, length, axis=dim)
        leading = lax.slice_in_dim(value, 0, width, axis=dim)
        before = lax.ppermute(last, axis, up)
        after = lax.ppermute(leading, axis, down)
        value = jnp.concatenate([before, value, after], axis=dim)
    return value


def shifted(block, axis, distance):
    devices = range(lax.axis_size(axis))
    route = [((i - distance) % len(devices), i) for i in devices]
    return lax.ppermute(block, axis, route)


def layer_norm(stream, norm_gain, norm_bias):
    average = jnp.mean(stream, axis=-1, keepdims=True)
    centred = stream - average
    spread = jnp.mean(centred * centred, axis=-1, keepdims=True)
    return centred * lax.rsqrt(spread + 1e-05) * norm_gain + norm_bias


def feed_forward(stream, norm_gain, norm_bias, weight_up, weight_down):
    normed, norm_pull = jax.vjp(layer_norm, stream, norm_gain, norm_bias)
    normed_low = normed.astype(jnp.bfloat16)
    inner_act = jnp.dot(normed_low, weight_up, preferred_element_type=jnp.float32)
    hidden, act_pull = jax.vjp(jax.nn.silu, inner_act)
    hidden_low = hidden.astype(jnp.bfloat16)
    branch = jnp.dot(hidden_low, weight_down, preferred_element_type=jnp.float32)
    return (stream + 0.5 * branch, (norm_pull, normed_low, act_pull, hidden_low))


def feed_backward(grad_in, saved_state, weight_up, weight_down):
    norm_pull, normed_low, act_pull, hidden_low = saved_state
    branch_low = (0.5 * grad_in).astype(jnp.bfloat16)
    down_grad = jnp.einsum("tf,td->fd", hidden_low, branch_low, preferred_element_type=jnp.float32)
    hidden_grad = jnp.einsum(
        "td,fd->tf", branch_low, weight_down, preferred_element_type=jnp.float32
    )
    inner_grad = act_pull(hidden_grad)[0].astype(jnp.bfloat16)
    up_grad = jnp.einsum("td,tf->df", normed_low, inner_grad, preferred_element_type=jnp.float32)
    normed_grad = jnp.einsum("tf,df->td", inner_grad, weight_up, preferred_element_type=jnp.float32)
    stream_grad, gain_grad, bias_grad = norm_pull(normed_grad)
    return (grad_in + stream_grad, gain_grad, bias_grad, up_grad, down_grad)


def score_block(query_heads, key_piece, query_start, key_start, query_seg, key_seg, slopes):
    row_count, key_count, feature_count = key_piece.shape
    head_count = query_heads.shape[2]
    head_size = query_heads.shape[3]
    key_heads = key_piece.reshape(row_count, key_count, head_count, head_size)
    raw_score = jnp.einsum(
        "rqhd,rkhd->rqhk", query_heads, key_heads, preferred_element_type=jnp.float32
    ) * head_size ** (-0.5)
    query_place = query_start + jnp.arange(query_heads.shape[1], dtype=jnp.int32)
    key_place = key_start + jnp.arange(key_count, dtype=jnp.int32)
    log_distance = jnp.log1p(jnp.abs(query_place[:, None] - key_place[None, :]).astype(jnp.float32))
    is_live = (query_seg[:, :, None] == key_seg[:, None, :])[:, :, None, :]
    logits = jnp.where(
        is_live, raw_score - slopes[None, None, :, None] * log_distance[None, :, None, :], -1e30
    )
    return (logits, is_live, log_distance, key_heads)


def prob_grads(
    query_heads,
    grad_heads,
    log_sum,
    row_delta,
    query_start,
    query_seg,
    key_piece,
    value_piece,
    key_start,
    key_seg,
    slopes,
):
    logits, is_live, log_distance, key_heads = score_block(
        query_heads, key_piece, query_start, key_start, query_seg, key_seg, slopes
    )
    row_prob = jnp.where(is_live, jnp.exp(logits - log_sum[..., None]), 0.0)
    value_heads = value_piece.reshape(key_heads.shape)
    prob_grad = jnp.einsum(
        "rqhd,rkhd->rqhk", grad_heads, value_heads, preferred_element_type=jnp.float32
    )
    score_grad = row_prob * (prob_grad - row_delta[..., None])
    return (row_prob, score_grad, score_grad.astype(jnp.bfloat16), log_distance, key_heads)


def body(
    frames,
    segments,
    cotangent,
    norm_gains,
    norm_biases,
    front_up,
    front_down,
    attend_in,
    attend_out,
    slopes,
    point_in,
    depthwise,
    point_out,
    rear_up,
    rear_down,
):
    row_count, frame_count, feature_count = frames.shape
    head_count = slopes.shape[0]
    head_size = feature_count // head_count
    token_count = row_count * frame_count
    seq_size = lax.axis_size("seq")
    seq_index = lax.axis_index("seq")
    query_start = seq_index * frame_count
    score_scale = head_size ** (-0.5)
    (
        gains_w,
        biases_w,
        front_up_w,
        front_down_w,
        attend_in_w,
        attend_out_w,
        point_in_w,
        depth_w,
        point_out_w,
        rear_up_w,
        rear_down_w,
    ) = (
        lax.all_gather(norm_gains, "seq", axis=1, tiled=True),
        lax.all_gather(norm_biases, "seq", axis=1, tiled=True),
        lax.all_gather(front_up, "seq", axis=0, tiled=True),
        lax.all_gather(front_down, "seq", axis=0, tiled=True),
        lax.all_gather(attend_in, "seq", axis=0, tiled=True),
        lax.all_gather(attend_out, "seq", axis=0, tiled=True),
        lax.all_gather(point_in, "seq", axis=0, tiled=True),
        lax.all_gather(depthwise, "seq", axis=1, tiled=True),
        lax.all_gather(point_out, "seq", axis=0, tiled=True),
        lax.all_gather(rear_up, "seq", axis=0, tiled=True),
        lax.all_gather(rear_down, "seq", axis=0, tiled=True),
    )
    gains_f = gains_w.astype(jnp.float32)
    biases_f = biases_w.astype(jnp.float32)
    depth_f = depth_w.astype(jnp.float32)
    kernel_len = depth_f.shape[0]
    half_k = kernel_len // 2
    segment_row = lax.all_gather(segments, "seq", axis=1, tiled=True)
    start_stream = frames.astype(jnp.float32).reshape(token_count, feature_count)
    after_front, front_saved = feed_forward(
        start_stream, gains_f[0], biases_f[0], front_up_w, front_down_w
    )
    attend_normed, attend_pull = jax.vjp(layer_norm, after_front, gains_f[1], biases_f[1])
    attend_low = attend_normed.astype(jnp.bfloat16)
    projected = jnp.dot(attend_low, attend_in_w, preferred_element_type=jnp.float32).astype(
        jnp.bfloat16
    )
    query_heads = projected[:, :feature_count].reshape(
        row_count, frame_count, head_count, head_size
    )
    key_low = projected[:, feature_count : 2 * feature_count].reshape(
        row_count, frame_count, feature_count
    )
    value_low = projected[:, 2 * feature_count :].reshape(row_count, frame_count, feature_count)
    stat_shape = (row_count, frame_count, head_count)
    start = jnp.int32(0)
    key_piece = lax.all_gather(key_low, "seq", axis=1, tiled=True)
    value_piece = lax.all_gather(value_low, "seq", axis=1, tiled=True)
    key_seg = segment_row
    row_top = jnp.full(stat_shape, -1e30, jnp.float32)
    logits, is_live, log_distance, key_heads = score_block(
        query_heads, key_piece, query_start, start, segments, key_seg, slopes
    )
    new_top = jnp.maximum(row_top, jnp.max(logits, axis=-1))
    row_exp = jnp.where(is_live, jnp.exp(logits - new_top[..., None]), 0.0)
    value_heads = value_piece.reshape(key_heads.shape)
    accum = jnp.einsum(
        "rqhk,rkhd->rqhd",
        row_exp.astype(jnp.bfloat16),
        value_heads,
        preferred_element_type=jnp.float32,
    )
    row_top, row_total, accum = (new_top, jnp.sum(row_exp, axis=-1), accum)
    attended = accum / row_total[..., None]
    log_sum = row_top + jnp.log(row_total)
    attended_low = attended.reshape(token_count, feature_count).astype(jnp.bfloat16)
    after_attend = after_front + jnp.dot(
        attended_low, attend_out_w, preferred_element_type=jnp.float32
    )
    conv_normed, conv_pull = jax.vjp(layer_norm, after_attend, gains_f[2], biases_f[2])
    conv_low = conv_normed.astype(jnp.bfloat16)
    conv_pre = jnp.dot(conv_low, point_in_w, preferred_element_type=jnp.float32)

    def gate_unit(inner_act):
        return inner_act[:, :feature_count] * jax.nn.sigmoid(inner_act[:, feature_count:])

    gated, gate_pull = jax.vjp(gate_unit, conv_pre)
    gated_low = gated.astype(jnp.bfloat16).reshape(row_count, frame_count, feature_count)
    gated_wide = padded(gated_low, (("seq", 1),), half_k).astype(jnp.float32)
    padded_seg = jnp.pad(segment_row, ((0, 0), (half_k, half_k)), constant_values=-1)
    seg_window = lax.dynamic_slice_in_dim(padded_seg, query_start, frame_count + 2 * half_k, 1)
    same_list = [
        (seg_window[:, offset : offset + frame_count] == segments)[..., None]
        for offset in range(kernel_len)
    ]
    mixed_conv = jnp.zeros((row_count, frame_count, feature_count), jnp.float32)
    for offset in range(kernel_len):
        mixed_conv = mixed_conv + jnp.where(
            same_list[offset], depth_f[offset] * gated_wide[:, offset : offset + frame_count], 0.0
        )

    def norm_silu(stream, norm_gain, norm_bias):
        return jax.nn.silu(layer_norm(stream, norm_gain, norm_bias))

    activated, activated_pull = jax.vjp(
        norm_silu, mixed_conv.reshape(token_count, feature_count), gains_f[3], biases_f[3]
    )
    activated_low = activated.astype(jnp.bfloat16)
    after_conv = after_attend + jnp.dot(
        activated_low, point_out_w, preferred_element_type=jnp.float32
    )
    after_rear, rear_saved = feed_forward(
        after_conv, gains_f[4], biases_f[4], rear_up_w, rear_down_w
    )
    final_out, final_pull = jax.vjp(layer_norm, after_rear, gains_f[5], biases_f[5])
    result = final_out.astype(jnp.bfloat16).reshape(row_count, frame_count, feature_count)
    grad_rear, gain_five, bias_five = final_pull(
        cotangent.astype(jnp.float32).reshape(token_count, feature_count)
    )
    grad_conv, gain_four, bias_four, rear_up_grad, rear_down_grad = feed_backward(
        grad_rear, rear_saved, rear_up_w, rear_down_w
    )
    conv_branch = grad_conv.astype(jnp.bfloat16)
    point_out_grad = jnp.einsum(
        "td,te->de", activated_low, conv_branch, preferred_element_type=jnp.float32
    )
    activated_grad = jnp.einsum(
        "te,de->td", conv_branch, point_out_w, preferred_element_type=jnp.float32
    )
    mixed_grad, gain_three, bias_three = activated_pull(activated_grad)
    mixed_low = mixed_grad.astype(jnp.bfloat16).reshape(row_count, frame_count, feature_count)
    grad_wide = padded(mixed_low, (("seq", 1),), half_k).astype(jnp.float32)
    mixed_back = mixed_low.astype(jnp.float32)
    depth_rows = [
        jnp.sum(
            jnp.where(
                same_list[offset], mixed_back * gated_wide[:, offset : offset + frame_count], 0.0
            ),
            axis=(0, 1),
        )
        for offset in range(kernel_len)
    ]
    depthwise_grad = jnp.stack(depth_rows)
    gated_grad = jnp.zeros((row_count, frame_count, feature_count), jnp.float32)
    for offset in range(kernel_len):
        mirror = 2 * half_k - offset
        gated_grad = gated_grad + jnp.where(
            same_list[mirror], depth_f[offset] * grad_wide[:, mirror : mirror + frame_count], 0.0
        )
    pre_grad = gate_pull(gated_grad.reshape(token_count, feature_count))[0].astype(jnp.bfloat16)
    point_in_grad = jnp.einsum("td,tc->dc", conv_low, pre_grad, preferred_element_type=jnp.float32)
    conv_normed_grad = jnp.einsum(
        "tc,dc->td", pre_grad, point_in_w, preferred_element_type=jnp.float32
    )
    conv_stream_grad, gain_two, bias_two = conv_pull(conv_normed_grad)
    grad_attend = grad_conv + conv_stream_grad
    attend_branch = grad_attend.astype(jnp.bfloat16)
    attend_out_grad = jnp.einsum(
        "td,te->de", attended_low, attend_branch, preferred_element_type=jnp.float32
    )
    attended_grad = jnp.einsum(
        "te,de->td", attend_branch, attend_out_w, preferred_element_type=jnp.float32
    )
    grad_heads = attended_grad.astype(jnp.bfloat16).reshape(
        row_count, frame_count, head_count, head_size
    )
    row_delta = jnp.sum(grad_heads.astype(jnp.float32) * attended, axis=-1)

    def query_terms(state, key_piece, value_piece, start, key_seg):
        query_grad, slope_grad = state
        row_prob, score_grad, score_low, log_distance, key_heads = prob_grads(
            query_heads,
            grad_heads,
            log_sum,
            row_delta,
            query_start,
            segments,
            key_piece,
            value_piece,
            start,
            key_seg,
            slopes,
        )
        query_grad = (
            query_grad
            + jnp.einsum(
                "rqhk,rkhd->rqhd", score_low, key_heads, preferred_element_type=jnp.float32
            )
            * score_scale
        )
        slope_grad = slope_grad - jnp.einsum("rqhk,qk->h", score_grad, log_distance)
        return (query_grad, slope_grad, row_prob, score_low)

    query_zero = jnp.zeros((row_count, frame_count, head_count, head_size), jnp.float32)
    slope_zero = jnp.zeros((head_count,), jnp.float32)
    local_zero = jnp.zeros((row_count, frame_count, feature_count), jnp.float32)

    def accumulate(step, query_grad, slope_grad, pair_kv, pair_acc):
        owner = (seq_index + step) % seq_size
        start = owner * frame_count
        key_seg = lax.dynamic_slice_in_dim(segment_row, start, frame_count, 1)
        grad_q = query_grad
        grad_s = slope_grad
        key_acc = pair_acc[0]
        value_acc = pair_acc[1]
        grad_q, grad_s, row_prob, score_low = query_terms(
            (grad_q, grad_s), pair_kv[0], pair_kv[1], start, key_seg
        )
        key_acc = key_acc + (
            jnp.einsum(
                "rqhk,rqhd->rkhd", score_low, query_heads, preferred_element_type=jnp.float32
            )
            * score_scale
        ).reshape(row_count, frame_count, feature_count)
        value_acc = value_acc + jnp.einsum(
            "rqhk,rqhd->rkhd",
            row_prob.astype(jnp.bfloat16),
            grad_heads,
            preferred_element_type=jnp.float32,
        ).reshape(row_count, frame_count, feature_count)
        query_grad, slope_grad, key_acc, value_acc = (grad_q, grad_s, key_acc, value_acc)
        pair_acc = shifted(jnp.stack([key_acc, value_acc]).astype(jnp.bfloat16), "seq", -1).astype(
            jnp.float32
        )
        return (query_grad, slope_grad, pair_acc)

    def cycle_step(step, carry):
        query_grad, slope_grad, pair_kv, pair_acc = carry
        next_kv = shifted(pair_kv, "seq", -1)
        query_grad, slope_grad, pair_acc = accumulate(
            step, query_grad, slope_grad, pair_kv, pair_acc
        )
        return (query_grad, slope_grad, next_kv, pair_acc)

    pair_start = jnp.stack([key_low, value_low])
    acc_start = jnp.stack([local_zero, local_zero])
    query_grad, slope_grad, pair_kv, pair_acc = lax.fori_loop(
        0, seq_size - 1, cycle_step, (query_zero, slope_zero, pair_start, acc_start)
    )
    query_grad, slope_grad, pair_acc = accumulate(
        seq_size - 1, query_grad, slope_grad, pair_kv, pair_acc
    )
    key_grad = pair_acc[0]
    value_grad = pair_acc[1]
    projected_grad = jnp.concatenate(
        [
            query_grad.reshape(token_count, feature_count),
            key_grad.reshape(token_count, feature_count),
            value_grad.reshape(token_count, feature_count),
        ],
        axis=1,
    ).astype(jnp.bfloat16)
    attend_in_grad = jnp.einsum(
        "td,tc->dc", attend_low, projected_grad, preferred_element_type=jnp.float32
    )
    attend_normed_grad = jnp.einsum(
        "tc,dc->td", projected_grad, attend_in_w, preferred_element_type=jnp.float32
    )
    attend_stream_grad, gain_one, bias_one = attend_pull(attend_normed_grad)
    grad_front = grad_attend + attend_stream_grad
    start_grad, gain_zero, bias_zero, front_up_grad, front_down_grad = feed_backward(
        grad_front, front_saved, front_up_w, front_down_w
    )
    frames_grad = start_grad.astype(jnp.bfloat16).reshape(row_count, frame_count, feature_count)
    gains_local = jnp.stack([gain_zero, gain_one, gain_two, gain_three, gain_four, gain_five])
    biases_local = jnp.stack([bias_zero, bias_one, bias_two, bias_three, bias_four, bias_five])
    slope_rows = jnp.broadcast_to(slope_grad[None, :], (seq_size, head_count))
    shares = (
        lax.psum_scatter(
            gains_local.astype(jnp.bfloat16), "seq", scatter_dimension=1, tiled=True
        ).astype(jnp.float32),
        lax.psum_scatter(
            biases_local.astype(jnp.bfloat16), "seq", scatter_dimension=1, tiled=True
        ).astype(jnp.float32),
        lax.psum_scatter(
            front_up_grad.astype(jnp.bfloat16), "seq", scatter_dimension=0, tiled=True
        ).astype(jnp.float32),
        lax.psum_scatter(
            front_down_grad.astype(jnp.bfloat16), "seq", scatter_dimension=0, tiled=True
        ).astype(jnp.float32),
        lax.psum_scatter(
            attend_in_grad.astype(jnp.bfloat16), "seq", scatter_dimension=0, tiled=True
        ).astype(jnp.float32),
        lax.psum_scatter(
            attend_out_grad.astype(jnp.bfloat16), "seq", scatter_dimension=0, tiled=True
        ).astype(jnp.float32),
        lax.psum_scatter(
            slope_rows.astype(jnp.bfloat16), "seq", scatter_dimension=0, tiled=True
        ).astype(jnp.float32),
        lax.psum_scatter(
            point_in_grad.astype(jnp.bfloat16), "seq", scatter_dimension=0, tiled=True
        ).astype(jnp.float32),
        lax.psum_scatter(
            depthwise_grad.astype(jnp.bfloat16), "seq", scatter_dimension=1, tiled=True
        ).astype(jnp.float32),
        lax.psum_scatter(
            point_out_grad.astype(jnp.bfloat16), "seq", scatter_dimension=0, tiled=True
        ).astype(jnp.float32),
        lax.psum_scatter(
            rear_up_grad.astype(jnp.bfloat16), "seq", scatter_dimension=0, tiled=True
        ).astype(jnp.float32),
        lax.psum_scatter(
            rear_down_grad.astype(jnp.bfloat16), "seq", scatter_dimension=0, tiled=True
        ).astype(jnp.float32),
    )
    totals = (
        lax.psum(shares[0].astype(jnp.bfloat16), "dp").astype(jnp.float32),
        lax.psum(shares[1].astype(jnp.bfloat16), "dp").astype(jnp.float32),
        lax.psum(shares[2].astype(jnp.bfloat16), "dp").astype(jnp.float32),
        lax.psum(shares[3].astype(jnp.bfloat16), "dp").astype(jnp.float32),
        lax.psum(shares[4].astype(jnp.bfloat16), "dp").astype(jnp.float32),
        lax.psum(shares[5].astype(jnp.bfloat16), "dp").astype(jnp.float32),
        lax.psum(shares[6].astype(jnp.bfloat16), "dp").astype(jnp.float32),
        lax.psum(shares[7].astype(jnp.bfloat16), "dp").astype(jnp.float32),
        lax.psum(shares[8].astype(jnp.bfloat16), "dp").astype(jnp.float32),
        lax.psum(shares[9].astype(jnp.bfloat16), "dp").astype(jnp.float32),
        lax.psum(shares[10].astype(jnp.bfloat16), "dp").astype(jnp.float32),
        lax.psum(shares[11].astype(jnp.bfloat16), "dp").astype(jnp.float32),
    )
    return (
        result,
        frames_grad,
        totals[0],
        totals[1],
        totals[2],
        totals[3],
        totals[4],
        totals[5],
        totals[6].reshape(head_count),
        totals[7],
        totals[8],
        totals[9],
        totals[10],
        totals[11],
    )


def place():
    dp, seq = lax.axis_index("dp"), lax.axis_index("seq")
    return dp // 2, dp % 2, seq // 2, seq % 2


QUERIES = 256


def head_lanes(value, head, scale=1.0):
    lane = lax.broadcasted_iota(jnp.int32, value.shape, 1)
    mine = (lane >= 64 * head) & (lane < 64 * head + 64)
    return jnp.where(mine, value * jnp.asarray(scale, value.dtype), jnp.zeros_like(value))


def nt(a, b):
    return lax.dot_general(a, b, (((1,), (1,)), ((), ())), preferred_element_type=jnp.float32)


MESH_ID = pl.DeviceIdType.MESH
PIECE = 32
HALO = 16
TILE, TILES = 128, 8
UP, DOWN, PROJECT, ATTEND_OUT, POINT_IN, POINT_OUT, REAR_UP, REAR_DOWN = 0, 4, 8, 11, 12, 14, 15, 19
CHUNKS = 23
TALL = (False, True, False, False, False, False, False, True)
LEAD = 3
VMEM_LIMIT = 63 * 2**20
STAGE = 1
STEP = 4 * STAGE
VECTORS = 48


def low(value):
    return value.astype(jnp.bfloat16)


def f32(value):
    return value.astype(jnp.float32)


def dot(a, b):
    return jnp.dot(a, b, preferred_element_type=jnp.float32)


def norm_rows(v, gain, bias):
    centred = v - jnp.mean(v, axis=-1, keepdims=True)
    spread = jnp.mean(centred * centred, axis=-1, keepdims=True)
    return centred * lax.rsqrt(spread + 1e-05) * gain + bias


def logistic(v):
    return 1.0 / (1.0 + jnp.exp(-v))


def remote_copy(src, dst, send_sem, recv_sem, there):
    return pltpu.make_async_remote_copy(
        src_ref=src,
        dst_ref=dst,
        send_sem=send_sem,
        recv_sem=recv_sem,
        device_id=there,
        device_id_type=MESH_ID,
    )


def attend_block(e, first_head, row, block):
    q = e.packed[pl.ds(block * 2, 2), 0, row].reshape(QUERIES, 128)
    value_t = e.packed[:, 2, row].reshape(TILES * TILE, 128).T
    first = pl.multiple_of(block * QUERIES, QUERIES)
    query_seg = e.seg_rows[pl.ds(row, 1), pl.ds(first, QUERIES)]
    outs = []
    for head in range(2):
        q_head = head_lanes(q, head, 0.125)
        slope = e.slopes[first_head + head]
        top = jnp.full((1, QUERIES), -1e30, jnp.float32)
        for kb in range(TILES):
            logit = logit_tile(e, q_head, slope, query_seg, row, block, kb)[0]
            e.logits[kb] = logit
            top = jnp.maximum(top, jnp.max(logit, axis=0, keepdims=True))
        total = jnp.zeros((1, QUERIES), jnp.float32)
        for kb in range(TILES):
            power = jnp.exp(e.logits[kb] - top)
            total = total + jnp.sum(power, axis=0, keepdims=True)
            e.scores[kb * TILE : kb * TILE + TILE, :] = low(power)
        e.log_sum[row, head, :, pl.ds(first, QUERIES)] = top + jnp.log(total)
        out = dot(value_t, e.scores[...])
        outs.append(out[64 * head : 64 * head + 64] / total)
    return jnp.concatenate(outs, axis=0).T


def logit_tile(e, q_head, slope, query_seg, row, block, kb):
    logit = nt(e.packed[kb, 1, row], q_head)
    distance = jnp.concatenate(
        [e.distances[kb - 2 * block + TILES - 1], e.distances[kb - 2 * block + TILES - 2]], axis=1
    )
    same = e.seg_cols[row, kb * TILE : kb * TILE + TILE, :] == query_seg
    return jnp.where(same, logit - slope * distance, -1e30), distance


def forward_part(e):
    sources, gains, biases, depth, segments, frames = (
        e.sources,
        e.gains,
        e.biases,
        e.depth,
        e.segments,
        e.frames,
    )
    full, vec_all, seg_all, packed, gated, mixed, act = (
        e.full,
        e.vec_all,
        e.seg_all,
        e.packed,
        e.gated,
        e.mixed,
        e.act,
    )
    norm0, norm1, norm2, norm4, attended, conv_pre = (
        e.norm0,
        e.norm1,
        e.norm2,
        e.norm4,
        e.attended,
        e.conv_pre,
    )
    after_front, after_attend, after_conv, after_rear = (
        e.after_front,
        e.after_attend,
        e.after_conv,
        e.after_rear,
    )
    pre, hid, wbuf, vectors, shards, acc = e.pre, e.hid, e.wbuf, e.vectors, e.pool, e.total
    pk_out, att_out, att_in, gated_f = e.pk_out, e.att_out, e.att_in, e.gated_f
    seg_plane, seg_cols, seg_rows = e.seg_plane, e.seg_cols, e.seg_rows
    vec_wide, vec, seg = e.vec_wide, e.vec, e.seg
    gather_sem, own_sem, small_sem, pk_sem, att_sem, halo_sem, load_sem, keep_sem = e.forward_sems
    y, x, z, core = place()
    dp, seq = y * 2 + x, z * 2 + core
    rows, width = 2, 1024
    frame_count = 128
    length = 8 * frame_count
    over_x = (y * 2 + 1 - x, seq)
    over_y = ((1 - y) * 2 + x, seq)
    over_core = (dp, z * 2 + 1 - core)

    def peer(k):
        return lax.rem(seq + k, 8)

    def read(t):
        first = 0
        for source, tall in zip(sources, TALL):
            count = source.shape[0] // 128 if tall else source.shape[1] // width
            if t < first + count:
                at = pl.ds((t - first) * (128 if tall else width), 128 if tall else width)
                where = source.at[at, :] if tall else source.at[:, at]
                return pltpu.make_async_copy(where, shards.at[t], own_sem.at[3, t])
            first += count

    def read_done(t):
        pltpu.make_async_copy(shards.at[t], shards.at[t], own_sem.at[3, t]).wait()

    barrier = pltpu.get_barrier_semaphore()
    for there in [(dp, peer(k)) for k in range(1, 8)] + [(lax.rem(dp + k, 4), seq) for k in (1, 2, 3)]:
        pl.semaphore_signal(barrier, inc=1, device_id=there, device_id_type=MESH_ID)
    for t in range(CHUNKS):
        read(t).start()
    vec_wide[...] = jnp.zeros_like(vec_wide)
    vec_wide[0:6, :] = f32(gains[...])
    vec_wide[6:12, :] = f32(biases[...])
    vec_wide[12:43, :] = f32(depth[...])
    vec[...] = low(vec_wide[...])
    seg[...] = jnp.zeros_like(seg)
    seg[0:rows, :] = segments[...]

    pl.semaphore_wait(barrier, 10)

    q_own, q_x, q_y = PIECE * dp, PIECE * (y * 2 + 1 - x), PIECE * ((1 - y) * 2 + x)

    def travel(kind, t, k, first, rows_, there, src=None):
        source = seq if src is not None else lax.rem(z - k + 4, 4) * 2 + core
        where = full.at[t, source, pl.ds(pl.multiple_of(first, 16), rows_)]
        return remote_copy(
            where if src is None else src,
            where,
            gather_sem.at[0, kind, t, k - 1],
            gather_sem.at[1, kind, t, k - 1],
            there,
        )

    def line(t, k):
        src = shards.at[t, pl.ds(pl.multiple_of(q_own, 16), PIECE)]
        return travel(0, t, k, q_own, PIECE, (dp, lax.rem(z + k, 4) * 2 + core), src)

    def to_x(t, k):
        return travel(1, t, k, q_own, PIECE, over_x)

    def to_y(t, k):
        return travel(2, t, k, q_own, PIECE, over_y)

    def on_x(t, k):
        return travel(3, t, k, q_y, PIECE // 2, over_x)

    def on_y(t, k):
        return travel(4, t, k, q_x + PIECE // 2, PIECE // 2, over_y)

    def to_core(t, k):
        return travel(5, t, k, 0, 4 * PIECE, over_core)

    def own_to_core(t):
        return remote_copy(
            shards.at[t], full.at[t, seq], own_sem.at[0, t], own_sem.at[1, t], over_core
        )

    def own_to_full(t):
        return pltpu.make_async_copy(shards.at[t], full.at[t, seq], own_sem.at[2, t])

    def small_copies():
        copies = []
        for k in range(1, 8):
            for i, (src, dst) in enumerate(((vec, vec_all), (seg, seg_all))):
                copies.append(
                    remote_copy(
                        src,
                        dst.at[seq],
                        small_sem.at[0, i, k - 1],
                        small_sem.at[1, i, k - 1],
                        (dp, peer(k)),
                    )
                )
        return copies

    for copy in small_copies():
        copy.start()
    vec_all[seq] = vec[...]
    seg_all[seq] = seg[...]
    def relay(t):
        where = full.at[t, lax.rem(z + 2, 4) * 2 + core, pl.ds(pl.multiple_of(q_own, 16), PIECE)]
        return remote_copy(
            where,
            where,
            gather_sem.at[0, 6, t, 0],
            gather_sem.at[1, 0, t, 2 * z - 2],
            (dp, 3 * (z - 1) * 2 + core),
        )

    def direct(k):
        return {1: z != 3, 2: z >= 0, 3: z != 0}[k]

    def in_time(k):
        return {1: z != 0, 2: z >= 0, 3: z != 3}[k]

    relays = (z == 1) | (z == 2)

    def start_line(t):
        read_done(t)
        own_to_core(t).start()
        own_to_full(t).start()
        for k in (1, 2, 3):

            @pl.when(direct(k))
            def _():
                line(t, k).start()

    def arrived(t, k):
        line(t, k).wait_recv()
        to_x(t, k).start()
        to_y(t, k).start()

    for t in range(LEAD):
        start_line(t)

    def gather_step(step):
        for i in range(2):
            ahead = LEAD + 2 * step + i

            @pl.when(ahead < CHUNKS)
            def _(ahead=ahead):
                start_line(ahead)

        @pl.when(step < CHUNKS)
        def _():
            for k in (2, 1, 3):

                @pl.when(in_time(k))
                def _():
                    arrived(step, k)

                if k == 2:

                    @pl.when(relays)
                    def _():
                        relay(step).start()

        late = step - STAGE

        @pl.when((late >= 0) & (late < CHUNKS))
        def _():
            for k in (1, 3):

                @pl.when(jnp.logical_not(in_time(k)))
                def _():
                    arrived(late, k)

        second, third, last = step - 2 * STAGE, step - 3 * STAGE, step - 4 * STAGE

        @pl.when((second >= 0) & (second < CHUNKS))
        def _():
            for k in (1, 2, 3):
                to_y(second, k).wait_recv()
                on_x(second, k).start()
                to_x(second, k).wait_recv()
                on_y(second, k).start()

        @pl.when((third >= 0) & (third < CHUNKS))
        def _():
            for k in (1, 2, 3):
                on_x(third, k).wait_recv()
                on_y(third, k).wait_recv()
                to_core(third, k).start()

        @pl.when((last >= 0) & (last < CHUNKS))
        def _():
            for k in (1, 2, 3):
                to_core(last, k).wait_recv()
            own_to_core(last).wait_recv()
            own_to_full(last).wait()

    def load(u):
        return pltpu.make_async_copy(full.at[u], wbuf.at[lax.rem(u, 3)], load_sem.at[lax.rem(u, 3)])

    def weight(u):
        load(u).wait()
        return wbuf[lax.rem(u, 3)].reshape(width, width)

    def vector(i):
        return vectors[i : i + 1, :]

    def norm(v, i):
        return low(norm_rows(v, vector(i), vector(6 + i)))

    def prepare():
        for copy in small_copies():
            copy.wait()
        for s in range(8):
            vectors[:, s * 128 : s * 128 + 128] = f32(vec_all[s])
            columns = f32(seg_all[s]).T
            for r in range(rows):
                seg_cols[r, s * 128 : s * 128 + 128, :] = columns[:, r : r + 1]
                seg_rows[r : r + 1, s * 128 : s * 128 + 128] = f32(seg_all[s, r : r + 1, :])
        before = jnp.where(seq > 0, f32(seg_all[lax.max(seq - 1, 0)]), -1.0).T
        middle = f32(seg_all[seq]).T
        after = jnp.where(seq < 7, f32(seg_all[lax.min(seq + 1, 7)]), -1.0).T
        for r in range(rows):
            for first, col in (
                (0, before[frame_count - HALO :, r : r + 1]),
                (HALO, middle[:, r : r + 1]),
                (HALO + frame_count, after[:HALO, r : r + 1]),
            ):
                seg_plane[r, first : first + col.shape[0], :] = jnp.broadcast_to(col, (col.shape[0], 128))
        keys = lax.broadcasted_iota(jnp.int32, (TILE, TILE), 0)
        queries = lax.broadcasted_iota(jnp.int32, (TILE, TILE), 1)
        for i in range(2 * TILES - 1):
            apart = jnp.abs(keys - queries + TILE * (i - TILES + 1))
            e.distances[i] = jnp.log(1.0 + apart.astype(jnp.float32))
        norm0[...] = norm(f32(frames[...]), 0)

    def up(u, j, source):
        value = dot(source[...], weight(u))
        active = low(value * logistic(value))
        value = low(value)
        for half in range(2):
            to = pl.ds(pl.multiple_of((j * 2 + half) * 128, 128), 128)
            for i in range(4):
                first = half * 512 + i * 128
                pre[i, :, to] = value[:, first : first + 128]
                hid[i, :, to] = active[:, first : first + 128]

    def down(u, j, stream, target):
        value = dot(hid[j], weight(u))

        @pl.when(j == 0)
        def _():
            acc[...] = value

        @pl.when(j > 0)
        def _():
            acc[...] += value

        @pl.when(j == 3)
        def _():
            target[...] = f32(stream[...]) + 0.5 * acc[...]

    def keep_copies():
        return [
            pltpu.make_async_copy(pre, e.pre_keep, keep_sem.at[0]),
            pltpu.make_async_copy(hid, e.hid_keep, keep_sem.at[1]),
        ]

    def pk_copy(c, k, recv=False):
        there = peer(k)
        return remote_copy(
            pk_out.at[there, c],
            packed.at[there if recv else seq, c],
            pk_sem.at[0, there, c],
            pk_sem.at[1, there if recv else seq, c],
            (dp, there),
        )

    def project(u, c):
        value = low(dot(norm1[...], weight(u)))
        for s in range(8):
            pk_out[s, c] = value[:, s * 128 : s * 128 + 128].reshape(rows, frame_count, 128)
        packed[seq, c] = pk_out[seq, c]
        for k in range(1, 8):
            pk_copy(c, k).start()

    def att_copy(b, r, recv=False):
        return remote_copy(
            att_out.at[b, r],
            att_in.at[b if recv else seq, r],
            att_sem.at[0, b, r],
            att_sem.at[1, b if recv else seq, r],
            (dp, b),
        )

    def attend_step(i):
        row, block = i // 4, lax.rem(i, 4)
        out = attend_block(e, seq * 2, row, block)
        e.att_keep[row, pl.ds(pl.multiple_of(block * QUERIES, QUERIES), QUERIES), :] = out
        out = low(out)
        for half in range(2):
            b = block * 2 + half
            att_out[b, row] = out[half * 128 : half * 128 + 128]

            @pl.when(b != seq)
            def _():
                att_copy(b, row).start()

            @pl.when(b == seq)
            def _():
                att_in[b, row] = out[half * 128 : half * 128 + 128]

    def halo_copy(side):
        if side == 0:
            src, dst, there = gated.at[:, pl.ds(HALO, HALO)], gated.at[:, pl.ds(HALO + frame_count, HALO)], lax.rem(seq + 7, 8)
        else:
            src, dst, there = gated.at[:, pl.ds(frame_count, HALO)], gated.at[:, pl.ds(0, HALO)], lax.rem(seq + 1, 8)
        return remote_copy(src, dst, halo_sem.at[0, side], halo_sem.at[1, side], (dp, there))

    def convolve():
        @pl.when(seq > 0)
        def _():
            halo_copy(0).wait_send()
            halo_copy(1).wait_recv()

        @pl.when(seq < 7)
        def _():
            halo_copy(1).wait_send()
            halo_copy(0).wait_recv()

        gated_f[...] = f32(gated[...])

        def lanes(i, _):
            at = pl.ds(pl.multiple_of(i * 128, 128), 128)
            for r in range(rows):
                own = seg_plane[r, HALO : HALO + frame_count, :]
                total = jnp.zeros((frame_count, 128), jnp.float32)
                for shift in range(8):
                    near = gated_f[r, shift : shift + frame_count + 24, at]
                    seg_near = seg_plane[r, shift : shift + frame_count + 24, :]
                    for first in range(0, 32, 8):
                        tap = shift + first - 1
                        if 0 <= tap < 31:
                            same = seg_near[first : first + frame_count] == own
                            term = near[first : first + frame_count] * vectors[12 + tap : 13 + tap, at]
                            total = total + jnp.where(same, term, 0.0)
                mixed[r * frame_count : (r + 1) * frame_count, at] = total
            return 0

        lax.fori_loop(0, width // 128, lanes, 0)

    def step_work(step, _):
        gather_step(step)

        now = step - STEP

        def at(first, count=1):
            return pl.when((now >= first) & (now < first + count))

        @at(0)
        def _():
            prepare()

        @at(1, 4)
        def _():
            up(now - 1, now - 1, norm0)

        @at(5, 4)
        def _():
            down(now - 1, now - 5, frames, after_front)

        @at(9, 3)
        def _():
            @pl.when(now == 9)
            def _():
                norm1[...] = norm(after_front[...], 1)
                for copy in keep_copies():
                    copy.start()

            project(now - 1, now - 9)

        @at(14)
        def _():
            for c in range(3):
                for k in range(1, 8):
                    pk_copy(c, k, True).wait_recv()

        @at(14, 3)
        def _():
            def one(i, _):
                attend_step(i)
                return 0

            first = (now - 14) * 3
            lax.fori_loop(first, lax.min(first + 3, 8), one, 0)

        @at(18)
        def _():
            for r in range(rows):
                for k in range(1, 8):
                    att_copy(peer(k), r, True).wait_recv()
            for s in range(8):
                attended[:, s * 128 : s * 128 + 128] = att_in[s].reshape(rows * frame_count, 128)
            after_attend[...] = after_front[...] + dot(attended[...], weight(ATTEND_OUT))
            load(14).start()
            norm2[...] = norm(after_attend[...], 2)

        @at(18)
        def _():
            acc[...] = dot(norm2[...], weight(POINT_IN))
            conv_pre[0] = low(acc[...])
            gate = dot(norm2[...], weight(POINT_IN + 1))
            conv_pre[1] = low(gate)
            value = low(acc[...] * logistic(gate))
            gated[:, HALO : HALO + frame_count] = value.reshape(rows, frame_count, width)

            @pl.when(seq > 0)
            def _():
                halo_copy(0).start()

            @pl.when(seq < 7)
            def _():
                halo_copy(1).start()

        @at(19)
        def _():
            convolve()
            value = norm_rows(mixed[...], vector(3), vector(9))
            act[...] = low(value * logistic(value))
            after_conv[...] = after_attend[...] + dot(act[...], weight(POINT_OUT))
            norm4[...] = norm(after_conv[...], 4)

        @at(20, 2)
        def _():
            @pl.when(now == 20)
            def _():
                for copy in keep_copies():
                    copy.wait()

            for i in range(2):
                j = (now - 20) * 2 + i
                up(j + REAR_UP, j, norm4)

        @at(22, 2)
        def _():
            for i in range(2):
                j = (now - 22) * 2 + i
                down(j + REAR_DOWN, j, after_conv, after_rear)

        @at(0, 14)
        def _():
            load(now).start()

        for when, chunks in ((18, (15, 16)), (19, (17,)), (20, (18, 19)), (21, (20, 21)), (22, (22,))):

            @at(when)
            def _(chunks=chunks):
                for u in chunks:
                    load(u).start()

        return 0

    lax.fori_loop(0, STEP + 24, step_work, 0)

    def drain(t, _):
        for kind in (to_x, to_y, on_x, on_y, to_core):
            for k in (1, 2, 3):
                kind(t, k).wait_send()
        for k in (1, 2, 3):

            @pl.when(direct(k))
            def _():
                line(t, k).wait_send()

        @pl.when(relays)
        def _():
            relay(t).wait_send()

        own_to_core(t).wait_send()
        return 0

    lax.fori_loop(0, CHUNKS, drain, 0)
    for c in range(3):
        for k in range(1, 8):
            pk_copy(c, k).wait_send()
    for r in range(rows):
        for k in range(1, 8):
            att_copy(peer(k), r).wait_send()


JOB_RU, JOB_PO, JOB_PI, JOB_AO, JOB_P, JOB_FD, JOB_FU, JOBS = 4, 8, 9, 11, 12, 15, 19, 23
RING, SHARES = 4, 5
GRADS = ((7, True), (6, False), (5, False), (4, False), (3, False), (2, False), (1, True), (0, False))
OUT_LAG = 6


def silu_slope(pre, grad):
    gate = logistic(pre)
    return grad * gate * (1.0 + pre * (1.0 - gate))


def tn(a, b):
    return lax.dot_general(a, b, (((0,), (0,)), ((), ())), preferred_element_type=jnp.float32)


def backward_part(e):
    full, gated, mixed, act, packed = e.full, e.gated, e.mixed, e.act, e.packed
    norm0, norm1, norm2, norm4, attended, conv_pre = (
        e.norm0,
        e.norm1,
        e.norm2,
        e.norm4,
        e.attended,
        e.conv_pre,
    )
    after_front, after_attend, after_conv, after_rear = (
        e.after_front,
        e.after_attend,
        e.after_conv,
        e.after_rear,
    )
    frames, cotangent, slopes = e.frames, e.cotangent, e.slopes
    result, frames_grad, vec_out, grads = e.result, e.frames_grad, e.vec_out, e.grads
    pre_grads, hid, wbuf, vectors, pool = e.pre, e.hid, e.wbuf, e.vectors, e.pool
    small, right, branch, conv_branch = e.small, e.right, e.branch, e.conv_branch
    gate_grads, attend_branch, parts = e.gate_grads, e.attend_branch, e.parts
    grad, total, gated_f, mixed_w, mixed_f = e.grad, e.total, e.gated_f, e.mixed_w, e.mixed_f
    seg_plane, seg_rows = e.seg_plane, e.seg_rows
    g_out, g_in, p_out, p_in = e.att_out, e.g_in, e.pk_out, e.p_in
    key_sum, value_sum, slope_sum, out_buf = e.key_sum, e.value_sum, e.slope_sum, e.out_buf
    h_buf, a_buf, b_buf, q_buf = e.h_buf, e.a_buf, e.b_buf, e.q_buf
    a_in, b_in, a2_in, b2_in, z_in, o_buf = e.a_in, e.b_in, e.a2_in, e.b2_in, e.z_in, e.o_buf
    vec_send, vec_in, vec_dp = e.vec_send, e.vec_in, e.vec_dp
    sem, vec_sem, load_sem, keep_sem, ga_sem, pk_sem, halo_sem, out_sem, sync = e.backward_sems
    y, x, z, core = place()
    dp, seq = y * 2 + x, z * 2 + core
    rows, width, frame_count = 2, 1024, 128
    length = 8 * frame_count
    over_x = (y * 2 + 1 - x, seq)
    over_y = ((1 - y) * 2 + x, seq)
    over_core = (dp, z * 2 + 1 - core)

    def peer(k):
        return lax.rem(seq + k, 8)

    def dp_peer(k):
        return (lax.rem(dp + k, 4), seq)

    pl.semaphore_signal(sync, inc=1, device_id=over_core, device_id_type=MESH_ID)
    pl.semaphore_wait(sync, 1)
    mine = 4 * RING

    def remote(src, dst, t, slot, there):
        return remote_copy(
            src, dst, sem.at[0, slot, lax.rem(t, RING)], sem.at[1, slot, lax.rem(t, RING)], there
        )

    def turn(t):
        return lax.rem(t, 2)

    def core_copies(t, r):
        return [
            remote(pool.at[pl.ds(mine + 4, 4)], pool.at[pl.ds(4 * r, 4)], t, 0, over_core)
        ]

    def first_copies(t, r):
        return [
            remote(h_buf.at[turn(t), pl.ds(0, 2), :, 1 - x], a_in.at[r], t, 1, over_x),
            remote(h_buf.at[turn(t), pl.ds(2, 2), 1 - y], b_in.at[r], t, 2, over_y),
        ]

    def second_copies(t, r):
        return [
            remote(a_buf.at[turn(t), :, 1 - y], a2_in.at[r], t, 3, over_y),
            remote(b_buf.at[turn(t), :, 1 - x], b2_in.at[r], t, 4, over_x),
        ]

    def line_copies(t, r):
        copies = []
        for k in (1, 2, 3):
            to = lax.rem(z + k, 4)
            copies.append(remote(q_buf.at[turn(t), to], z_in.at[r, k - 1], t, 4 + k, (dp, to * 2 + core)))
        return copies

    def share_copies(t, r):
        where = o_buf.at[lax.rem(t, SHARES), dp]
        return [remote(where, where, t, 8, over_x), remote(where, where, t, 9, over_y)]

    def across_copies(t, r):
        one = o_buf.at[lax.rem(t, SHARES), (1 - y) * 2 + x, pl.ds(0, PIECE // 2)]
        two = o_buf.at[lax.rem(t, SHARES), y * 2 + 1 - x, pl.ds(PIECE // 2, PIECE // 2)]
        return [remote(one, one, t, 10, over_x), remote(two, two, t, 11, over_y)]

    def out_start(t):
        slot = lax.rem(t, 2)
        first = 0
        for out, tall in GRADS:
            ref = grads[out]
            size = 128 if tall else width
            count = ref.shape[0] // size if tall else ref.shape[1] // size

            @pl.when((t >= first) & (t < first + count))
            def _(ref=ref, tall=tall, size=size, first=first):
                at = pl.ds(pl.multiple_of((t - first) * size, size), size)
                where = ref.at[at, :] if tall else ref.at[:, at]
                pltpu.make_async_copy(out_buf.at[slot], where, out_sem.at[slot]).start()

            first += count

    def out_done(t):
        slot = lax.rem(t, 2)
        pltpu.make_async_copy(out_buf.at[slot], out_buf.at[slot], out_sem.at[slot]).wait()

    def finish(copies):
        for copy in copies:
            copy.wait()

    def begin(copies):
        for copy in copies:
            copy.start()

    def write_out(t, r):
        finish(across_copies(t, r))

        @pl.when(t >= 2)
        def _():
            out_done(t - 2)

        out_buf[lax.rem(t, 2)] = f32(o_buf[lax.rem(t, SHARES)].reshape(128, width))
        out_start(t)

    def pass_on(t, r):
        finish(share_copies(t, r))
        begin(across_copies(t, r))

    def total_line(t, r):
        finish(line_copies(t, r))
        value = f32(q_buf[turn(t), z]) + f32(z_in[r, 0]) + f32(z_in[r, 1]) + f32(z_in[r, 2])
        o_buf[lax.rem(t, SHARES), dp] = low(value)
        begin(share_copies(t, r))

    def total_second(t, r):
        finish(second_copies(t, r))
        q_buf[turn(t), 0:2] = low(f32(a_buf[turn(t), :, y]) + f32(a2_in[r]))
        q_buf[turn(t), 2:4] = low(f32(b_buf[turn(t), :, x]) + f32(b2_in[r]))
        begin(line_copies(t, r))

    def total_first(t, r):
        finish(first_copies(t, r))
        a_buf[turn(t)] = low(f32(h_buf[turn(t), 0:2, :, x]) + f32(a_in[r]))
        b_buf[turn(t)] = low(f32(h_buf[turn(t), 2:4, y]) + f32(b_in[r]))
        begin(second_copies(t, r))

    def total_core(t, r):
        finish(core_copies(t, r))
        for i in range(4):
            value = low(f32(pool[mine + i]) + f32(pool[4 * r + i]))
            h_buf[turn(t), i] = value.reshape(2, 2, PIECE, width)
        begin(first_copies(t, r))

    def product(t, left, right):
        for i in range(8):
            part = tn(left[:, 128 * i : 128 * i + 128], right[...])
            pool[mine + 4 * lax.rem(core + i, 2) + i // 2] = low(part)
        begin(core_copies(t, lax.rem(t, RING)))

    sums = [total_core, total_first, total_second, total_line, pass_on, write_out]

    def sum_step(step):
        for depth in range(1, 7):
            t = step - depth

            @pl.when((t >= 0) & (t < JOBS))
            def _(t=t, depth=depth):
                sums[depth - 1](t, lax.rem(t, RING))

    def load(i, u):
        return pltpu.make_async_copy(full.at[u], wbuf.at[i], load_sem.at[i])

    def weight(i, u):
        load(i, u).wait()
        return wbuf[i].reshape(width, width)

    def keep_copies():
        return [
            pltpu.make_async_copy(e.pre_keep, pre_grads, keep_sem.at[0]),
            pltpu.make_async_copy(e.hid_keep, hid, keep_sem.at[1]),
        ]

    def vector(i):
        return vectors[i : i + 1, :]

    def norm_back(v, i, dy):
        centred = v - jnp.mean(v, axis=-1, keepdims=True)
        rstd = lax.rsqrt(jnp.mean(centred * centred, axis=-1, keepdims=True) + 1e-05)
        n = centred * rstd
        small[i : i + 1, :] = jnp.sum(dy * n, axis=0, keepdims=True)
        small[6 + i : 7 + i, :] = jnp.sum(dy, axis=0, keepdims=True)
        dn = dy * vector(i)
        first = jnp.mean(dn, axis=-1, keepdims=True)
        second = jnp.mean(dn * n, axis=-1, keepdims=True)
        return rstd * (dn - first - n * second)

    def strided(b):
        blocks = []
        for half in range(2):
            at = pl.ds(pl.multiple_of((b * 2 + half) * 128, 128), 128)
            blocks += [pre_grads[j, :, at] for j in range(4)]
        return jnp.concatenate(blocks, axis=1)

    def down_back(j, down):
        hidden_grad = nt(branch[...], weight(lax.rem(j, 2), down + j))
        pre_grads[j] = low(silu_slope(f32(pre_grads[j]), hidden_grad))

    def up_back(b, up):
        value = nt(strided(b), weight(lax.rem(b, 2), up + b))

        @pl.when(b == 0)
        def _():
            total[...] = value

        @pl.when(b > 0)
        def _():
            total[...] += value

    def prepare():
        small[...] = jnp.zeros_like(small)
        slope_sum[...] = jnp.zeros_like(slope_sum)

    def halo_copy(side):
        if side == 0:
            src, dst = pl.ds(HALO, HALO), pl.ds(HALO + frame_count, HALO)
            there = lax.rem(seq + 7, 8)
        else:
            src, dst = pl.ds(frame_count, HALO), pl.ds(0, HALO)
            there = lax.rem(seq + 1, 8)
        return remote_copy(
            mixed_w.at[:, src],
            mixed_w.at[:, dst],
            halo_sem.at[0, side],
            halo_sem.at[1, side],
            (dp, there),
        )

    def convolve_back(r):
        def lanes(i, _):
            at = pl.ds(pl.multiple_of(i * 128, 128), 128)
            own = seg_plane[r, HALO : HALO + frame_count, :]
            mine = mixed_f[r, HALO : HALO + frame_count, at]
            value = jnp.zeros((frame_count, 128), jnp.float32)
            for shift in range(8):
                window = slice(shift, shift + frame_count + 24)
                seg_near = seg_plane[r, window, :]
                gated_near = gated_f[r, window, at]
                mixed_near = mixed_f[r, window, at]
                for first in range(0, 32, 8):
                    tap = shift + first - 1
                    if 0 <= tap < 31:
                        here = slice(first, first + frame_count)
                        same = seg_near[here] == own
                        near = jnp.where(same, gated_near[here], 0.0)
                        small[12 + tap : 13 + tap, at] += jnp.sum(near * mine, axis=0, keepdims=True)
                        came = jnp.where(same, mixed_near[here], 0.0)
                        value = value + came * vectors[12 + 30 - tap : 13 + 30 - tap, at]
            total[r * frame_count : (r + 1) * frame_count, at] = value
            return 0

        lax.fori_loop(0, width // 128, lanes, 0)

    def ga_copy(k, recv=False):
        there = peer(k)
        return remote_copy(
            g_out.at[there],
            g_in.at[there if recv else seq],
            ga_sem.at[0, there],
            ga_sem.at[1, there if recv else seq],
            (dp, there),
        )

    def pk_copy(there, c, r, recv=False):
        return remote_copy(
            p_out.at[there, c, r],
            p_in.at[there if recv else seq, c, r],
            pk_sem.at[0, there, c, r],
            pk_sem.at[1, there if recv else seq, c, r],
            (dp, there),
        )

    def attend_back_step(i):
        row, block = i // 4, lax.rem(i, 4)
        first = pl.multiple_of(block * QUERIES, QUERIES)
        query_seg = seg_rows[pl.ds(row, 1), pl.ds(first, QUERIES)]
        q = packed[pl.ds(block * 2, 2), 0, row].reshape(QUERIES, 128)
        g = g_in[pl.ds(block * 2, 2), row].reshape(QUERIES, 128)
        key_t = packed[:, 1, row].reshape(length, 128).T
        deltas = (f32(g) * e.att_keep[row, pl.ds(first, QUERIES), :]).T

        @pl.when(block == 0)
        def _():
            key_sum[...] = jnp.zeros_like(key_sum)
            value_sum[...] = jnp.zeros_like(value_sum)

        outs = []
        for head in range(2):
            q_head = head_lanes(q, head, 0.125)
            g_head = head_lanes(g, head)
            slope = slopes[seq * 2 + head]
            log_sum = e.log_sum[row, head, :, pl.ds(first, QUERIES)]
            delta = jnp.sum(deltas[64 * head : 64 * head + 64], axis=0, keepdims=True)
            slope_total = jnp.zeros((8, QUERIES), jnp.float32)
            for kb in range(TILES):
                at = slice(kb * TILE, kb * TILE + TILE)
                logit, distance = logit_tile(e, q_head, slope, query_seg, row, block, kb)
                prob = jnp.exp(logit - log_sum)
                prob_grad = nt(packed[kb, 2, row], g_head)
                value_sum[at, :] += dot(low(prob), g_head)
                logit_grad = prob * (prob_grad - delta)
                slope_total = slope_total + jnp.sum(
                    (logit_grad * distance).reshape(TILE // 8, 8, QUERIES), axis=0
                )
                score = low(logit_grad)
                e.scores[at, :] = score
                key_sum[at, :] += dot(score, q_head)
            slope_sum[head] -= slope_total
            query_t = dot(key_t, e.scores[...])
            outs.append(query_t[64 * head : 64 * head + 64] * 0.125)
        query = low(jnp.concatenate(outs, axis=0).T)

        def deliver(b, c, value):
            p_out[b, c, row] = value

            @pl.when(b != seq)
            def _():
                pk_copy(b, c, row).start()

            @pl.when(b == seq)
            def _():
                p_in[b, c, row] = value

        for half in range(2):
            deliver(block * 2 + half, 0, query[half * 128 : half * 128 + 128])

        @pl.when(block == 3)
        def _():
            for b in range(8):
                at = slice(b * 128, b * 128 + 128)
                deliver(b, 1, low(key_sum[at, :]))
                deliver(b, 2, low(value_sum[at, :]))

    def vec_copies():
        copies = []
        for k in range(1, 8):
            copies.append(
                remote_copy(
                    vec_send.at[peer(k)],
                    vec_in.at[seq],
                    vec_sem.at[0, k - 1],
                    vec_sem.at[1, k - 1],
                    (dp, peer(k)),
                )
            )
        return copies

    def vec_dp_copies():
        where = vec_dp.at[dp]
        return [
            remote_copy(where, where, vec_sem.at[0, 6 + k], vec_sem.at[1, 6 + k], dp_peer(k))
            for k in (1, 2, 3)
        ]

    def send_vectors():
        lane = lax.broadcasted_iota(jnp.int32, (1, 128), 1)
        mine = jnp.zeros((1, 128), jnp.float32)
        for head in range(2):
            value = jnp.sum(jnp.sum(slope_sum[head], axis=0, keepdims=True), axis=-1, keepdims=True)
            mine = mine + jnp.where(lane == seq * 2 + head, value, 0.0)
        for s in range(8):
            vec_send[s] = small[:, s * 128 : s * 128 + 128]
            vec_send[s, 43:44, :] = mine
        vec_in[seq] = vec_send[seq]
        begin(vec_copies())

    def sum_vectors():
        finish(vec_copies())
        value = vec_in[0]
        for i in range(1, 8):
            value = value + vec_in[i]
        vec_dp[dp] = value
        begin(vec_dp_copies())

    def finish_vectors():
        finish(vec_dp_copies())
        vec_out[...] = (vec_dp[0] + vec_dp[1]) + (vec_dp[2] + vec_dp[3])

    def step_work(step, _):
        sum_step(step)

        def at(first, count=1):
            return pl.when((step >= first) & (step < first + count))

        @at(0)
        def _():
            load(0, REAR_DOWN).start()
            load(1, REAR_DOWN + 1).start()
            prepare()
            result[...] = low(norm_rows(after_rear[...], vector(5), vector(11)))
            grad[...] = norm_back(after_rear[...], 5, f32(cotangent[...]))
            branch[...] = low(0.5 * grad[...])

        @at(12, 3)
        def _():
            c = step - 12
            for r in range(rows):
                for k in range(1, 8):
                    pk_copy(peer(k), c, r, True).wait_recv()
                    pk_copy(peer(k), c, r).wait_send()
            for s in range(8):
                parts[c, :, s * 128 : s * 128 + 128] = p_in[s, c].reshape(rows * frame_count, 128)

        @at(0, JOB_RU)
        def _():
            product(step, hid.at[step], branch)

        @at(JOB_RU, 4)
        def _():
            right[...] = strided(step - JOB_RU)
            product(step, norm4, right)

        @at(JOB_PO)
        def _():
            product(step, act, conv_branch)

        @at(JOB_PI, 2)
        def _():
            product(step, norm2, gate_grads.at[step - JOB_PI])

        @at(JOB_AO)
        def _():
            product(step, attended, attend_branch)

        @at(JOB_P, 3)
        def _():
            product(step, norm1, parts.at[step - JOB_P])

        @at(JOB_FD, 4)
        def _():
            product(step, hid.at[step - JOB_FD], branch)

        @at(JOB_FU, 4)
        def _():
            right[...] = strided(step - JOB_FU)
            product(step, norm0, right)

        @at(0)
        def _():
            for j in range(4):
                down_back(j, REAR_DOWN)
                load(j % 2, REAR_DOWN + 2 + j if j < 2 else REAR_UP + j - 2).start()

        @at(1)
        def _():
            for b in range(4):
                up_back(b, REAR_UP)
                if b < 2:
                    load(b, REAR_UP + 2 + b).start()
            load(0, POINT_OUT).start()
            grad[...] += norm_back(after_conv[...], 4, total[...])
            conv_branch[...] = low(grad[...])

        @at(2)
        def _():
            act_grad = nt(conv_branch[...], weight(0, POINT_OUT))
            act_grad = silu_slope(norm_rows(mixed[...], vector(3), vector(9)), act_grad)
            value = low(norm_back(mixed[...], 3, act_grad))
            mixed_w[:, HALO : HALO + frame_count] = value.reshape(rows, frame_count, width)

            @pl.when(seq > 0)
            def _():
                halo_copy(0).start()

            @pl.when(seq < 7)
            def _():
                halo_copy(1).start()

            load(0, POINT_IN).start()
            load(1, POINT_IN + 1).start()

        @at(3)
        def _():
            @pl.when(seq > 0)
            def _():
                halo_copy(0).wait_send()
                halo_copy(1).wait_recv()

            @pl.when(seq < 7)
            def _():
                halo_copy(1).wait_send()
                halo_copy(0).wait_recv()

            mixed_f[...] = f32(mixed_w[...])
            convolve_back(0)

        @at(4)
        def _():
            convolve_back(1)

        @at(5)
        def _():
            gate = logistic(f32(conv_pre[1]))
            gate_grads[0] = low(total[...] * gate)
            gate_grads[1] = low(total[...] * f32(conv_pre[0]) * gate * (1.0 - gate))
            norm_grad = nt(gate_grads[0], weight(0, POINT_IN))
            load(0, ATTEND_OUT).start()
            norm_grad = norm_grad + nt(gate_grads[1], weight(1, POINT_IN + 1))
            grad[...] += norm_back(after_attend[...], 2, norm_grad)
            attend_branch[...] = low(grad[...])
            value = low(nt(attend_branch[...], weight(0, ATTEND_OUT)))
            for s in range(8):
                g_out[s] = value[:, s * 128 : s * 128 + 128].reshape(rows, frame_count, 128)
            g_in[seq] = g_out[seq]
            for k in range(1, 8):
                ga_copy(k).start()
            load(0, PROJECT).start()
            load(1, PROJECT + 1).start()

        @at(7)
        def _():
            for k in range(1, 8):
                ga_copy(k, True).wait_recv()
                ga_copy(k).wait_send()

        @at(7, 4)
        def _():
            def one(i, _):
                attend_back_step((step - 7) * 2 + i)
                return 0

            lax.fori_loop(0, 2, one, 0)

        @at(12)
        def _():
            total[...] = nt(parts[0], weight(0, PROJECT))
            load(0, PROJECT + 2).start()

        @at(13)
        def _():
            total[...] += nt(parts[1], weight(1, PROJECT + 1))
            load(1, DOWN + 1).start()

        @at(14)
        def _():
            for copy in keep_copies():
                copy.wait()
            norm_grad = total[...] + nt(parts[2], weight(0, PROJECT + 2))
            load(0, DOWN).start()
            grad[...] += norm_back(after_front[...], 1, norm_grad)
            branch[...] = low(0.5 * grad[...])

        @at(8)
        def _():
            for copy in keep_copies():
                copy.start()

        @at(15, 2)
        def _():
            for i in range(2):
                j = (step - 15) * 2 + i
                down_back(j, DOWN)
                load(i, lax.rem(DOWN + 2 + j, PROJECT)).start()

        @at(17, 2)
        def _():
            for i in range(2):
                b = (step - 17) * 2 + i
                up_back(b, UP)

                @pl.when(b < 2)
                def _(b=b, i=i):
                    load(i, UP + 2 + b).start()

        @at(19)
        def _():
            frames_grad[...] = low(
                grad[...] + norm_back(f32(frames[...]), 0, total[...])
            )
            send_vectors()

        @at(22)
        def _():
            sum_vectors()

        @at(24)
        def _():
            finish_vectors()

        return 0

    lax.fori_loop(0, JOBS + OUT_LAG, step_work, 0)
    out_done(JOBS - 2)
    out_done(JOBS - 1)


class Refs:
    pass


def layer(weights, gains, biases, depth, segments, frames, cotangent, slopes):
    bf16, single = jnp.bfloat16, jnp.float32
    tokens, width = frames.shape
    tall = 128 + 2 * HALO
    dma = pltpu.SemaphoreType.DMA
    vmem, hbm = pl.BlockSpec(memory_space=pltpu.VMEM), pl.BlockSpec(memory_space=pltpu.HBM)

    def buf(kind, *sizes):
        return pltpu.VMEM(sizes, kind)

    plain, wide = buf(bf16, tokens, width), buf(single, tokens, width)
    four = buf(bf16, 4, tokens, width)
    quarter = (PIECE, width)
    scratch = dict(
        vec_all=buf(bf16, 8, VECTORS, 128),
        seg_all=buf(jnp.int32, 8, 8, 128),
        norm0=plain,
        norm1=plain,
        norm2=plain,
        norm4=plain,
        attended=plain,
        act=plain,
        pre=four,
        hid=four,
        packed=buf(bf16, 8, 3, 2, 128, 128),
        conv_pre=buf(bf16, 2, tokens, width),
        gated=buf(bf16, 2, tall, width),
        mixed=wide,
        after_front=wide,
        after_attend=wide,
        after_conv=wide,
        after_rear=wide,
        wbuf=buf(bf16, 3, 8, 128, width),
        vectors=buf(single, VECTORS, width),
        pool=buf(bf16, 4 * RING + 8, 128, width),
        pk_out=buf(bf16, 8, 3, 2, 128, 128),
        att_out=buf(bf16, 8, 2, 128, 128),
        att_in=buf(bf16, 8, 2, 128, 128),
        att_keep=buf(single, 2, 1024, 128),
        log_sum=buf(single, 2, 2, 1, 1024),
        logits=buf(single, TILES, TILE, QUERIES),
        scores=buf(bf16, TILES * TILE, QUERIES),
        distances=buf(single, 2 * TILES - 1, TILE, TILE),
        gated_f=buf(single, 2, tall, width),
        seg_plane=buf(single, 2, tall, 128),
        seg_cols=buf(single, 2, 1024, 1),
        seg_rows=buf(single, 8, 1024),
        vec_wide=buf(single, VECTORS, 128),
        vec=buf(bf16, VECTORS, 128),
        seg=buf(jnp.int32, 8, 128),
        small=buf(single, VECTORS, width),
        right=plain,
        branch=plain,
        conv_branch=plain,
        gate_grads=buf(bf16, 2, tokens, width),
        attend_branch=plain,
        parts=buf(bf16, 3, tokens, width),
        grad=wide,
        total=wide,
        mixed_w=buf(bf16, 2, tall, width),
        mixed_f=buf(single, 2, tall, width),
        g_in=buf(bf16, 8, 2, 128, 128),
        p_in=buf(bf16, 8, 3, 2, 128, 128),
        key_sum=buf(single, 1024, 128),
        value_sum=buf(single, 1024, 128),
        slope_sum=buf(single, 2, 8, QUERIES),
        out_buf=buf(single, 2, 128, width),
        h_buf=buf(bf16, 2, 4, 2, 2, *quarter),
        a_buf=buf(bf16, 2, 2, 2, *quarter),
        b_buf=buf(bf16, 2, 2, 2, *quarter),
        q_buf=buf(bf16, 2, 4, *quarter),
        a_in=buf(bf16, RING, 2, 2, *quarter),
        b_in=buf(bf16, RING, 2, 2, *quarter),
        a2_in=buf(bf16, RING, 2, *quarter),
        b2_in=buf(bf16, RING, 2, *quarter),
        z_in=buf(bf16, RING, 3, *quarter),
        o_buf=buf(bf16, SHARES, 4, *quarter),
        vec_send=buf(single, 8, VECTORS, 128),
        vec_in=buf(single, 8, VECTORS, 128),
        vec_dp=buf(single, 4, VECTORS, 128),
    )
    forward_sems = [(2, 7, CHUNKS, 3), (4, CHUNKS), (2, 2, 7), (2, 8, 3), (2, 8, 2), (2, 2), (3,), (2,)]
    backward_sems = [(2, 12, RING), (2, 10), (2,), (2,), (2, 8), (2, 8, 3, 2), (2, 2), (2,)]
    count = len(forward_sems)

    def kernel(*refs):
        e = Refs()
        e.sources = refs[:8]
        e.gains, e.biases, e.depth, e.segments, e.frames, e.cotangent, e.slopes = refs[8:15]
        e.result, e.frames_grad, e.vec_out = refs[15:18]
        e.grads = refs[18:26]
        e.full, e.pre_keep, e.hid_keep = refs[26:29]
        for name, ref in zip(scratch, refs[29:]):
            setattr(e, name, ref)
        sems = refs[29 + len(scratch) :]
        e.forward_sems, e.backward_sems = sems[:count], sems[count:]
        for wide_ref in (e.gated, e.mixed_w):
            wide_ref[:, :HALO] = jnp.zeros((2, HALO, width), bf16)
            wide_ref[:, HALO + 128 :] = jnp.zeros((2, HALO, width), bf16)
        forward_part(e)
        backward_part(e)

    shape = jax.ShapeDtypeStruct
    return pl.pallas_call(
        kernel,
        in_specs=[hbm] * 8 + [vmem] * 6 + [pl.BlockSpec(memory_space=pltpu.SMEM)],
        out_specs=[vmem] * 3 + [hbm] * 11,
        out_shape=[
            shape((tokens, width), bf16),
            shape((tokens, width), bf16),
            shape((VECTORS, 128), single),
        ]
        + [shape(weight.shape, single) for weight in weights]
        + [shape((CHUNKS, 8, 128, width), bf16)]
        + [shape((4, tokens, width), bf16)] * 2,
        scratch_shapes=list(scratch.values())
        + [dma(sizes) for sizes in forward_sems + backward_sems]
        + [pltpu.SemaphoreType.REGULAR],
        compiler_params=pltpu.CompilerParams(
            collective_id=0, has_side_effects=True, vmem_limit_bytes=VMEM_LIMIT
        ),
        name="layer",
    )(*weights, gains, biases, depth, segments, frames, cotangent, slopes)


def copy_kernel(*refs):
    count = 10
    sources, vec, targets = refs[:count], refs[count], refs[count + 1 : 2 * count + 1]
    gains, biases, depth, slopes = refs[2 * count + 1 : 2 * count + 5]
    buffers = refs[2 * count + 5 : 3 * count + 5]
    read_sem, write_sem = refs[3 * count + 5 :]
    jobs = []
    for i in range(count):
        rows = sources[i].shape[0]
        height = rows // 4
        for part in range(4):
            at = pl.ds(part * height, height)
            jobs.append((i, at, 4 * i + part))

    def read(job):
        i, at, n = job
        return pltpu.make_async_copy(sources[i].at[at], buffers[i].at[at], read_sem.at[n])

    def write(job):
        i, at, n = job
        return pltpu.make_async_copy(buffers[i].at[at], targets[i].at[at], write_sem.at[n])

    for job in jobs:
        read(job).start()
    gains[...] = vec[0:6, :]
    biases[...] = vec[6:12, :]
    depth[...] = vec[12:43, :]
    slopes[...] = vec[43:44, :]
    for job in jobs:
        read(job).wait()
        write(job).start()
    for job in jobs:
        write(job).wait()


def copy_out(arrays, vec):
    shape = jax.ShapeDtypeStruct
    vmem, hbm = pl.BlockSpec(memory_space=pltpu.VMEM), pl.BlockSpec(memory_space=pltpu.HBM)
    size = sum(array.size * array.dtype.itemsize for array in arrays)
    return pl.pallas_call(
        copy_kernel,
        in_specs=[hbm] * len(arrays) + [vmem],
        out_specs=[hbm] * len(arrays) + [vmem] * 4,
        out_shape=[shape(array.shape, array.dtype) for array in arrays]
        + [shape((height, 128), jnp.float32) for height in (6, 6, 31, 1)],
        scratch_shapes=[pltpu.VMEM(array.shape, array.dtype) for array in arrays]
        + [pltpu.SemaphoreType.DMA((4 * len(arrays),))] * 2,
        compiler_params=pltpu.CompilerParams(vmem_limit_bytes=VMEM_LIMIT),
        cost_estimate=pl.CostEstimate(flops=0, bytes_accessed=2 * size, transcendentals=0),
        name="copy_out",
    )(*arrays, vec)


def body_staged(
    frames,
    segments,
    cotangent,
    norm_gains,
    norm_biases,
    front_up,
    front_down,
    attend_in,
    attend_out,
    slopes,
    point_in,
    depthwise,
    point_out,
    rear_up,
    rear_down,
):
    width = frames.shape[2]
    token_count = frames.shape[0] * frames.shape[1]

    weights = (
        front_up,
        front_down,
        attend_in,
        attend_out,
        point_in,
        point_out,
        rear_up,
        rear_down,
    )
    tokens = frames.reshape(token_count, width)
    result, frames_grad, vectors, *grads = layer(
        weights,
        norm_gains,
        norm_biases,
        depthwise,
        segments,
        tokens,
        cotangent.reshape(token_count, width),
        slopes,
    )
    *arrays, gains_grad, biases_grad, depth_grad, slopes_grad = copy_out(
        [result, frames_grad, *grads[:8]], vectors
    )
    result, frames_grad, *grads = arrays
    return (
        result.reshape(frames.shape),
        frames_grad.reshape(frames.shape),
        gains_grad,
        biases_grad,
        *grads[:4],
        slopes_grad[0, : slopes.shape[0]],
        grads[4],
        depth_grad,
        *grads[5:],
    )


def solution(mesh):
    placed = (
        P("dp", "seq", None),
        P("dp", "seq"),
        P("dp", "seq", None),
        P(None, "seq"),
        P(None, "seq"),
        P("seq", None),
        P("seq", None),
        P("seq", None),
        P("seq", None),
        P(),
        P("seq", None),
        P(None, "seq"),
        P("seq", None),
        P("seq", None),
        P("seq", None),
    )
    sizes = mesh.shape
    staged = sizes["dp"] == 4 and sizes["seq"] == 8
    return jax.shard_map(
        body_staged if staged else body,
        mesh=mesh,
        in_specs=placed,
        out_specs=(
            P("dp", "seq", None),
            P("dp", "seq", None),
            P(None, "seq"),
            P(None, "seq"),
            P("seq", None),
            P("seq", None),
            P("seq", None),
            P("seq", None),
            P(),
            P("seq", None),
            P(None, "seq"),
            P("seq", None),
            P("seq", None),
            P("seq", None),
        ),
        check_vma=False,
    )
```

```python
import jax
import jax.numpy as jnp
from jax import lax
from jax.experimental import pallas as pl
from jax.experimental.pallas import tpu as pltpu
from jax.sharding import PartitionSpec as P


def padded(value, sides, width):
    for axis, dim in sides:
        peers, length = (lax.axis_size(axis), value.shape[dim])
        up = [(i, (i + 1) % peers) for i in range(peers - 1)]
        down = [(j, i) for i, j in up]
        last = lax.slice_in_dim(value, length - width, length, axis=dim)
        leading = lax.slice_in_dim(value, 0, width, axis=dim)
        before = lax.ppermute(last, axis, up)
        after = lax.ppermute(leading, axis, down)
        value = jnp.concatenate([before, value, after], axis=dim)
    return value


def shifted(block, axis, distance):
    devices = range(lax.axis_size(axis))
    route = [((i - distance) % len(devices), i) for i in devices]
    return lax.ppermute(block, axis, route)


def layer_norm(stream, norm_gain, norm_bias):
    average = jnp.mean(stream, axis=-1, keepdims=True)
    centred = stream - average
    spread = jnp.mean(centred * centred, axis=-1, keepdims=True)
    return centred * lax.rsqrt(spread + 1e-05) * norm_gain + norm_bias


def feed_forward(stream, norm_gain, norm_bias, weight_up, weight_down):
    normed, norm_pull = jax.vjp(layer_norm, stream, norm_gain, norm_bias)
    normed_low = normed.astype(jnp.bfloat16)
    inner_act = jnp.dot(normed_low, weight_up, preferred_element_type=jnp.float32)
    hidden, act_pull = jax.vjp(jax.nn.silu, inner_act)
    hidden_low = hidden.astype(jnp.bfloat16)
    branch = jnp.dot(hidden_low, weight_down, preferred_element_type=jnp.float32)
    return (stream + 0.5 * branch, (norm_pull, normed_low, act_pull, hidden_low))


def feed_backward(grad_in, saved_state, weight_up, weight_down):
    norm_pull, normed_low, act_pull, hidden_low = saved_state
    branch_low = (0.5 * grad_in).astype(jnp.bfloat16)
    down_grad = jnp.einsum("tf,td->fd", hidden_low, branch_low, preferred_element_type=jnp.float32)
    hidden_grad = jnp.einsum(
        "td,fd->tf", branch_low, weight_down, preferred_element_type=jnp.float32
    )
    inner_grad = act_pull(hidden_grad)[0].astype(jnp.bfloat16)
    up_grad = jnp.einsum("td,tf->df", normed_low, inner_grad, preferred_element_type=jnp.float32)
    normed_grad = jnp.einsum("tf,df->td", inner_grad, weight_up, preferred_element_type=jnp.float32)
    stream_grad, gain_grad, bias_grad = norm_pull(normed_grad)
    return (grad_in + stream_grad, gain_grad, bias_grad, up_grad, down_grad)


def score_block(query_heads, key_piece, query_start, key_start, query_seg, key_seg, slopes):
    row_count, key_count, feature_count = key_piece.shape
    head_count = query_heads.shape[2]
    head_size = query_heads.shape[3]
    key_heads = key_piece.reshape(row_count, key_count, head_count, head_size)
    raw_score = jnp.einsum(
        "rqhd,rkhd->rqhk", query_heads, key_heads, preferred_element_type=jnp.float32
    ) * head_size ** (-0.5)
    query_place = query_start + jnp.arange(query_heads.shape[1], dtype=jnp.int32)
    key_place = key_start + jnp.arange(key_count, dtype=jnp.int32)
    log_distance = jnp.log1p(jnp.abs(query_place[:, None] - key_place[None, :]).astype(jnp.float32))
    is_live = (query_seg[:, :, None] == key_seg[:, None, :])[:, :, None, :]
    logits = jnp.where(
        is_live, raw_score - slopes[None, None, :, None] * log_distance[None, :, None, :], -1e30
    )
    return (logits, is_live, log_distance, key_heads)


def prob_grads(
    query_heads,
    grad_heads,
    log_sum,
    row_delta,
    query_start,
    query_seg,
    key_piece,
    value_piece,
    key_start,
    key_seg,
    slopes,
):
    logits, is_live, log_distance, key_heads = score_block(
        query_heads, key_piece, query_start, key_start, query_seg, key_seg, slopes
    )
    row_prob = jnp.where(is_live, jnp.exp(logits - log_sum[..., None]), 0.0)
    value_heads = value_piece.reshape(key_heads.shape)
    prob_grad = jnp.einsum(
        "rqhd,rkhd->rqhk", grad_heads, value_heads, preferred_element_type=jnp.float32
    )
    score_grad = row_prob * (prob_grad - row_delta[..., None])
    return (row_prob, score_grad, score_grad.astype(jnp.bfloat16), log_distance, key_heads)


def body(
    frames,
    segments,
    cotangent,
    norm_gains,
    norm_biases,
    front_up,
    front_down,
    attend_in,
    attend_out,
    slopes,
    point_in,
    depthwise,
    point_out,
    rear_up,
    rear_down,
):
    row_count, frame_count, feature_count = frames.shape
    head_count = slopes.shape[0]
    head_size = feature_count // head_count
    token_count = row_count * frame_count
    seq_size = lax.axis_size("seq")
    seq_index = lax.axis_index("seq")
    query_start = seq_index * frame_count
    score_scale = head_size ** (-0.5)
    (
        gains_w,
        biases_w,
        front_up_w,
        front_down_w,
        attend_in_w,
        attend_out_w,
        point_in_w,
        depth_w,
        point_out_w,
        rear_up_w,
        rear_down_w,
    ) = (
        lax.all_gather(norm_gains, "seq", axis=1, tiled=True),
        lax.all_gather(norm_biases, "seq", axis=1, tiled=True),
        lax.all_gather(front_up, "seq", axis=0, tiled=True),
        lax.all_gather(front_down, "seq", axis=0, tiled=True),
        lax.all_gather(attend_in, "seq", axis=0, tiled=True),
        lax.all_gather(attend_out, "seq", axis=0, tiled=True),
        lax.all_gather(point_in, "seq", axis=0, tiled=True),
        lax.all_gather(depthwise, "seq", axis=1, tiled=True),
        lax.all_gather(point_out, "seq", axis=0, tiled=True),
        lax.all_gather(rear_up, "seq", axis=0, tiled=True),
        lax.all_gather(rear_down, "seq", axis=0, tiled=True),
    )
    gains_f = gains_w.astype(jnp.float32)
    biases_f = biases_w.astype(jnp.float32)
    depth_f = depth_w.astype(jnp.float32)
    kernel_len = depth_f.shape[0]
    half_k = kernel_len // 2
    segment_row = lax.all_gather(segments, "seq", axis=1, tiled=True)
    start_stream = frames.astype(jnp.float32).reshape(token_count, feature_count)
    after_front, front_saved = feed_forward(
        start_stream, gains_f[0], biases_f[0], front_up_w, front_down_w
    )
    attend_normed, attend_pull = jax.vjp(layer_norm, after_front, gains_f[1], biases_f[1])
    attend_low = attend_normed.astype(jnp.bfloat16)
    projected = jnp.dot(attend_low, attend_in_w, preferred_element_type=jnp.float32).astype(
        jnp.bfloat16
    )
    query_heads = projected[:, :feature_count].reshape(
        row_count, frame_count, head_count, head_size
    )
    key_low = projected[:, feature_count : 2 * feature_count].reshape(
        row_count, frame_count, feature_count
    )
    value_low = projected[:, 2 * feature_count :].reshape(row_count, frame_count, feature_count)
    stat_shape = (row_count, frame_count, head_count)
    start = jnp.int32(0)
    key_piece = lax.all_gather(key_low, "seq", axis=1, tiled=True)
    value_piece = lax.all_gather(value_low, "seq", axis=1, tiled=True)
    key_seg = segment_row
    row_top = jnp.full(stat_shape, -1e30, jnp.float32)
    logits, is_live, log_distance, key_heads = score_block(
        query_heads, key_piece, query_start, start, segments, key_seg, slopes
    )
    new_top = jnp.maximum(row_top, jnp.max(logits, axis=-1))
    row_exp = jnp.where(is_live, jnp.exp(logits - new_top[..., None]), 0.0)
    value_heads = value_piece.reshape(key_heads.shape)
    accum = jnp.einsum(
        "rqhk,rkhd->rqhd",
        row_exp.astype(jnp.bfloat16),
        value_heads,
        preferred_element_type=jnp.float32,
    )
    row_top, row_total, accum = (new_top, jnp.sum(row_exp, axis=-1), accum)
    attended = accum / row_total[..., None]
    log_sum = row_top + jnp.log(row_total)
    attended_low = attended.reshape(token_count, feature_count).astype(jnp.bfloat16)
    after_attend = after_front + jnp.dot(
        attended_low, attend_out_w, preferred_element_type=jnp.float32
    )
    conv_normed, conv_pull = jax.vjp(layer_norm, after_attend, gains_f[2], biases_f[2])
    conv_low = conv_normed.astype(jnp.bfloat16)
    conv_pre = jnp.dot(conv_low, point_in_w, preferred_element_type=jnp.float32)

    def gate_unit(inner_act):
        return inner_act[:, :feature_count] * jax.nn.sigmoid(inner_act[:, feature_count:])

    gated, gate_pull = jax.vjp(gate_unit, conv_pre)
    gated_low = gated.astype(jnp.bfloat16).reshape(row_count, frame_count, feature_count)
    gated_wide = padded(gated_low, (("seq", 1),), half_k).astype(jnp.float32)
    padded_seg = jnp.pad(segment_row, ((0, 0), (half_k, half_k)), constant_values=-1)
    seg_window = lax.dynamic_slice_in_dim(padded_seg, query_start, frame_count + 2 * half_k, 1)
    same_list = [
        (seg_window[:, offset : offset + frame_count] == segments)[..., None]
        for offset in range(kernel_len)
    ]
    mixed_conv = jnp.zeros((row_count, frame_count, feature_count), jnp.float32)
    for offset in range(kernel_len):
        mixed_conv = mixed_conv + jnp.where(
            same_list[offset], depth_f[offset] * gated_wide[:, offset : offset + frame_count], 0.0
        )

    def norm_silu(stream, norm_gain, norm_bias):
        return jax.nn.silu(layer_norm(stream, norm_gain, norm_bias))

    activated, activated_pull = jax.vjp(
        norm_silu, mixed_conv.reshape(token_count, feature_count), gains_f[3], biases_f[3]
    )
    activated_low = activated.astype(jnp.bfloat16)
    after_conv = after_attend + jnp.dot(
        activated_low, point_out_w, preferred_element_type=jnp.float32
    )
    after_rear, rear_saved = feed_forward(
        after_conv, gains_f[4], biases_f[4], rear_up_w, rear_down_w
    )
    final_out, final_pull = jax.vjp(layer_norm, after_rear, gains_f[5], biases_f[5])
    result = final_out.astype(jnp.bfloat16).reshape(row_count, frame_count, feature_count)
    grad_rear, gain_five, bias_five = final_pull(
        cotangent.astype(jnp.float32).reshape(token_count, feature_count)
    )
    grad_conv, gain_four, bias_four, rear_up_grad, rear_down_grad = feed_backward(
        grad_rear, rear_saved, rear_up_w, rear_down_w
    )
    conv_branch = grad_conv.astype(jnp.bfloat16)
    point_out_grad = jnp.einsum(
        "td,te->de", activated_low, conv_branch, preferred_element_type=jnp.float32
    )
    activated_grad = jnp.einsum(
        "te,de->td", conv_branch, point_out_w, preferred_element_type=jnp.float32
    )
    mixed_grad, gain_three, bias_three = activated_pull(activated_grad)
    mixed_low = mixed_grad.astype(jnp.bfloat16).reshape(row_count, frame_count, feature_count)
    grad_wide = padded(mixed_low, (("seq", 1),), half_k).astype(jnp.float32)
    mixed_back = mixed_low.astype(jnp.float32)
    depth_rows = [
        jnp.sum(
            jnp.where(
                same_list[offset], mixed_back * gated_wide[:, offset : offset + frame_count], 0.0
            ),
            axis=(0, 1),
        )
        for offset in range(kernel_len)
    ]
    depthwise_grad = jnp.stack(depth_rows)
    gated_grad = jnp.zeros((row_count, frame_count, feature_count), jnp.float32)
    for offset in range(kernel_len):
        mirror = 2 * half_k - offset
        gated_grad = gated_grad + jnp.where(
            same_list[mirror], depth_f[offset] * grad_wide[:, mirror : mirror + frame_count], 0.0
        )
    pre_grad = gate_pull(gated_grad.reshape(token_count, feature_count))[0].astype(jnp.bfloat16)
    point_in_grad = jnp.einsum("td,tc->dc", conv_low, pre_grad, preferred_element_type=jnp.float32)
    conv_normed_grad = jnp.einsum(
        "tc,dc->td", pre_grad, point_in_w, preferred_element_type=jnp.float32
    )
    conv_stream_grad, gain_two, bias_two = conv_pull(conv_normed_grad)
    grad_attend = grad_conv + conv_stream_grad
    attend_branch = grad_attend.astype(jnp.bfloat16)
    attend_out_grad = jnp.einsum(
        "td,te->de", attended_low, attend_branch, preferred_element_type=jnp.float32
    )
    attended_grad = jnp.einsum(
        "te,de->td", attend_branch, attend_out_w, preferred_element_type=jnp.float32
    )
    grad_heads = attended_grad.astype(jnp.bfloat16).reshape(
        row_count, frame_count, head_count, head_size
    )
    row_delta = jnp.sum(grad_heads.astype(jnp.float32) * attended, axis=-1)

    def query_terms(state, key_piece, value_piece, start, key_seg):
        query_grad, slope_grad = state
        row_prob, score_grad, score_low, log_distance, key_heads = prob_grads(
            query_heads,
            grad_heads,
            log_sum,
            row_delta,
            query_start,
            segments,
            key_piece,
            value_piece,
            start,
            key_seg,
            slopes,
        )
        query_grad = (
            query_grad
            + jnp.einsum(
                "rqhk,rkhd->rqhd", score_low, key_heads, preferred_element_type=jnp.float32
            )
            * score_scale
        )
        slope_grad = slope_grad - jnp.einsum("rqhk,qk->h", score_grad, log_distance)
        return (query_grad, slope_grad, row_prob, score_low)

    query_zero = jnp.zeros((row_count, frame_count, head_count, head_size), jnp.float32)
    slope_zero = jnp.zeros((head_count,), jnp.float32)
    local_zero = jnp.zeros((row_count, frame_count, feature_count), jnp.float32)

    def accumulate(step, query_grad, slope_grad, pair_kv, pair_acc):
        owner = (seq_index + step) % seq_size
        start = owner * frame_count
        key_seg = lax.dynamic_slice_in_dim(segment_row, start, frame_count, 1)
        grad_q = query_grad
        grad_s = slope_grad
        key_acc = pair_acc[0]
        value_acc = pair_acc[1]
        grad_q, grad_s, row_prob, score_low = query_terms(
            (grad_q, grad_s), pair_kv[0], pair_kv[1], start, key_seg
        )
        key_acc = key_acc + (
            jnp.einsum(
                "rqhk,rqhd->rkhd", score_low, query_heads, preferred_element_type=jnp.float32
            )
            * score_scale
        ).reshape(row_count, frame_count, feature_count)
        value_acc = value_acc + jnp.einsum(
            "rqhk,rqhd->rkhd",
            row_prob.astype(jnp.bfloat16),
            grad_heads,
            preferred_element_type=jnp.float32,
        ).reshape(row_count, frame_count, feature_count)
        query_grad, slope_grad, key_acc, value_acc = (grad_q, grad_s, key_acc, value_acc)
        pair_acc = shifted(jnp.stack([key_acc, value_acc]).astype(jnp.bfloat16), "seq", -1).astype(
            jnp.float32
        )
        return (query_grad, slope_grad, pair_acc)

    def cycle_step(step, carry):
        query_grad, slope_grad, pair_kv, pair_acc = carry
        next_kv = shifted(pair_kv, "seq", -1)
        query_grad, slope_grad, pair_acc = accumulate(
            step, query_grad, slope_grad, pair_kv, pair_acc
        )
        return (query_grad, slope_grad, next_kv, pair_acc)

    pair_start = jnp.stack([key_low, value_low])
    acc_start = jnp.stack([local_zero, local_zero])
    query_grad, slope_grad, pair_kv, pair_acc = lax.fori_loop(
        0, seq_size - 1, cycle_step, (query_zero, slope_zero, pair_start, acc_start)
    )
    query_grad, slope_grad, pair_acc = accumulate(
        seq_size - 1, query_grad, slope_grad, pair_kv, pair_acc
    )
    key_grad = pair_acc[0]
    value_grad = pair_acc[1]
    projected_grad = jnp.concatenate(
        [
            query_grad.reshape(token_count, feature_count),
            key_grad.reshape(token_count, feature_count),
            value_grad.reshape(token_count, feature_count),
        ],
        axis=1,
    ).astype(jnp.bfloat16)
    attend_in_grad = jnp.einsum(
        "td,tc->dc", attend_low, projected_grad, preferred_element_type=jnp.float32
    )
    attend_normed_grad = jnp.einsum(
        "tc,dc->td", projected_grad, attend_in_w, preferred_element_type=jnp.float32
    )
    attend_stream_grad, gain_one, bias_one = attend_pull(attend_normed_grad)
    grad_front = grad_attend + attend_stream_grad
    start_grad, gain_zero, bias_zero, front_up_grad, front_down_grad = feed_backward(
        grad_front, front_saved, front_up_w, front_down_w
    )
    frames_grad = start_grad.astype(jnp.bfloat16).reshape(row_count, frame_count, feature_count)
    gains_local = jnp.stack([gain_zero, gain_one, gain_two, gain_three, gain_four, gain_five])
    biases_local = jnp.stack([bias_zero, bias_one, bias_two, bias_three, bias_four, bias_five])
    slope_rows = jnp.broadcast_to(slope_grad[None, :], (seq_size, head_count))
    shares = (
        lax.psum_scatter(
            gains_local.astype(jnp.bfloat16), "seq", scatter_dimension=1, tiled=True
        ).astype(jnp.float32),
        lax.psum_scatter(
            biases_local.astype(jnp.bfloat16), "seq", scatter_dimension=1, tiled=True
        ).astype(jnp.float32),
        lax.psum_scatter(
            front_up_grad.astype(jnp.bfloat16), "seq", scatter_dimension=0, tiled=True
        ).astype(jnp.float32),
        lax.psum_scatter(
            front_down_grad.astype(jnp.bfloat16), "seq", scatter_dimension=0, tiled=True
        ).astype(jnp.float32),
        lax.psum_scatter(
            attend_in_grad.astype(jnp.bfloat16), "seq", scatter_dimension=0, tiled=True
        ).astype(jnp.float32),
        lax.psum_scatter(
            attend_out_grad.astype(jnp.bfloat16), "seq", scatter_dimension=0, tiled=True
        ).astype(jnp.float32),
        lax.psum_scatter(
            slope_rows.astype(jnp.bfloat16), "seq", scatter_dimension=0, tiled=True
        ).astype(jnp.float32),
        lax.psum_scatter(
            point_in_grad.astype(jnp.bfloat16), "seq", scatter_dimension=0, tiled=True
        ).astype(jnp.float32),
        lax.psum_scatter(
            depthwise_grad.astype(jnp.bfloat16), "seq", scatter_dimension=1, tiled=True
        ).astype(jnp.float32),
        lax.psum_scatter(
            point_out_grad.astype(jnp.bfloat16), "seq", scatter_dimension=0, tiled=True
        ).astype(jnp.float32),
        lax.psum_scatter(
            rear_up_grad.astype(jnp.bfloat16), "seq", scatter_dimension=0, tiled=True
        ).astype(jnp.float32),
        lax.psum_scatter(
            rear_down_grad.astype(jnp.bfloat16), "seq", scatter_dimension=0, tiled=True
        ).astype(jnp.float32),
    )
    totals = (
        lax.psum(shares[0].astype(jnp.bfloat16), "dp").astype(jnp.float32),
        lax.psum(shares[1].astype(jnp.bfloat16), "dp").astype(jnp.float32),
        lax.psum(shares[2].astype(jnp.bfloat16), "dp").astype(jnp.float32),
        lax.psum(shares[3].astype(jnp.bfloat16), "dp").astype(jnp.float32),
        lax.psum(shares[4].astype(jnp.bfloat16), "dp").astype(jnp.float32),
        lax.psum(shares[5].astype(jnp.bfloat16), "dp").astype(jnp.float32),
        lax.psum(shares[6].astype(jnp.bfloat16), "dp").astype(jnp.float32),
        lax.psum(shares[7].astype(jnp.bfloat16), "dp").astype(jnp.float32),
        lax.psum(shares[8].astype(jnp.bfloat16), "dp").astype(jnp.float32),
        lax.psum(shares[9].astype(jnp.bfloat16), "dp").astype(jnp.float32),
        lax.psum(shares[10].astype(jnp.bfloat16), "dp").astype(jnp.float32),
        lax.psum(shares[11].astype(jnp.bfloat16), "dp").astype(jnp.float32),
    )
    return (
        result,
        frames_grad,
        totals[0],
        totals[1],
        totals[2],
        totals[3],
        totals[4],
        totals[5],
        totals[6].reshape(head_count),
        totals[7],
        totals[8],
        totals[9],
        totals[10],
        totals[11],
    )


def place():
    dp, seq = lax.axis_index("dp"), lax.axis_index("seq")
    return dp // 2, dp % 2, seq // 2, seq % 2


QUERIES = 256


def head_lanes(value, head, scale=1.0):
    lane = lax.broadcasted_iota(jnp.int32, value.shape, 1)
    mine = (lane >= 64 * head) & (lane < 64 * head + 64)
    return jnp.where(mine, value * jnp.asarray(scale, value.dtype), jnp.zeros_like(value))


def nt(a, b):
    return lax.dot_general(a, b, (((1,), (1,)), ((), ())), preferred_element_type=jnp.float32)


MESH_ID = pl.DeviceIdType.MESH
PIECE = 32
HALO = 16
TILE, TILES = 128, 8
UP, DOWN, PROJECT, ATTEND_OUT, POINT_IN, POINT_OUT, REAR_UP, REAR_DOWN = 0, 4, 8, 11, 12, 14, 15, 19
CHUNKS = 23
TALL = (False, True, False, False, False, False, False, True)
LEAD = 3
VMEM_LIMIT = 63 * 2**20
STAGE = 1
STEP = 4 * STAGE
VECTORS = 48


def low(value):
    return value.astype(jnp.bfloat16)


def f32(value):
    return value.astype(jnp.float32)


def dot(a, b):
    return jnp.dot(a, b, preferred_element_type=jnp.float32)


def norm_rows(v, gain, bias):
    centred = v - jnp.mean(v, axis=-1, keepdims=True)
    spread = jnp.mean(centred * centred, axis=-1, keepdims=True)
    return centred * lax.rsqrt(spread + 1e-05) * gain + bias


def logistic(v):
    return 1.0 / (1.0 + jnp.exp(-v))


def remote_copy(src, dst, send_sem, recv_sem, there):
    return pltpu.make_async_remote_copy(
        src_ref=src,
        dst_ref=dst,
        send_sem=send_sem,
        recv_sem=recv_sem,
        device_id=there,
        device_id_type=MESH_ID,
    )


def attend_block(e, first_head, row, block):
    q = e.packed[pl.ds(block * 2, 2), 0, row].reshape(QUERIES, 128)
    value_t = e.packed[:, 2, row].reshape(TILES * TILE, 128).T
    first = pl.multiple_of(block * QUERIES, QUERIES)
    query_seg = e.seg_rows[pl.ds(row, 1), pl.ds(first, QUERIES)]
    outs = []
    for head in range(2):
        q_head = head_lanes(q, head, 0.125)
        slope = e.slopes[first_head + head]
        top = jnp.full((1, QUERIES), -1e30, jnp.float32)
        for kb in range(TILES):
            logit = logit_tile(e, q_head, slope, query_seg, row, block, kb)[0]
            e.logits[kb] = logit
            top = jnp.maximum(top, jnp.max(logit, axis=0, keepdims=True))
        total = jnp.zeros((1, QUERIES), jnp.float32)
        for kb in range(TILES):
            power = jnp.exp(e.logits[kb] - top)
            total = total + jnp.sum(power, axis=0, keepdims=True)
            e.scores[kb * TILE : kb * TILE + TILE, :] = low(power)
        e.log_sum[row, head, :, pl.ds(first, QUERIES)] = top + jnp.log(total)
        out = dot(value_t, e.scores[...])
        outs.append(out[64 * head : 64 * head + 64] / total)
    return jnp.concatenate(outs, axis=0).T


def logit_tile(e, q_head, slope, query_seg, row, block, kb):
    logit = nt(e.packed[kb, 1, row], q_head)
    distance = jnp.concatenate(
        [e.distances[kb - 2 * block + TILES - 1], e.distances[kb - 2 * block + TILES - 2]], axis=1
    )
    same = e.seg_cols[row, kb * TILE : kb * TILE + TILE, :] == query_seg
    return jnp.where(same, logit - slope * distance, -1e30), distance


def forward_part(e):
    sources, gains, biases, depth, segments, frames = (
        e.sources,
        e.gains,
        e.biases,
        e.depth,
        e.segments,
        e.frames,
    )
    full, vec_all, seg_all, packed, gated, mixed, act = (
        e.full,
        e.vec_all,
        e.seg_all,
        e.packed,
        e.gated,
        e.mixed,
        e.act,
    )
    norm0, norm1, norm2, norm4, attended, conv_pre = (
        e.norm0,
        e.norm1,
        e.norm2,
        e.norm4,
        e.attended,
        e.conv_pre,
    )
    after_front, after_attend, after_conv, after_rear = (
        e.after_front,
        e.after_attend,
        e.after_conv,
        e.after_rear,
    )
    pre, hid, wbuf, vectors, shards, acc = e.pre, e.hid, e.wbuf, e.vectors, e.pool, e.total
    pk_out, att_out, att_in, gated_f = e.pk_out, e.att_out, e.att_in, e.gated_f
    seg_plane, seg_cols, seg_rows = e.seg_plane, e.seg_cols, e.seg_rows
    vec_wide, vec, seg = e.vec_wide, e.vec, e.seg
    gather_sem, own_sem, small_sem, pk_sem, att_sem, halo_sem, load_sem, keep_sem = e.forward_sems
    y, x, z, core = place()
    dp, seq = y * 2 + x, z * 2 + core
    rows, width = 2, 1024
    frame_count = 128
    length = 8 * frame_count
    over_x = (y * 2 + 1 - x, seq)
    over_y = ((1 - y) * 2 + x, seq)
    over_core = (dp, z * 2 + 1 - core)

    def peer(k):
        return lax.rem(seq + k, 8)

    def read(t):
        first = 0
        for source, tall in zip(sources, TALL):
            count = source.shape[0] // 128 if tall else source.shape[1] // width
            if t < first + count:
                at = pl.ds((t - first) * (128 if tall else width), 128 if tall else width)
                where = source.at[at, :] if tall else source.at[:, at]
                return pltpu.make_async_copy(where, shards.at[t], own_sem.at[3, t])
            first += count

    def read_done(t):
        pltpu.make_async_copy(shards.at[t], shards.at[t], own_sem.at[3, t]).wait()

    barrier = pltpu.get_barrier_semaphore()
    for there in [(dp, peer(k)) for k in range(1, 8)] + [(lax.rem(dp + k, 4), seq) for k in (1, 2, 3)]:
        pl.semaphore_signal(barrier, inc=1, device_id=there, device_id_type=MESH_ID)
    for t in range(CHUNKS):
        read(t).start()
    vec_wide[...] = jnp.zeros_like(vec_wide)
    vec_wide[0:6, :] = f32(gains[...])
    vec_wide[6:12, :] = f32(biases[...])
    vec_wide[12:43, :] = f32(depth[...])
    vec[...] = low(vec_wide[...])
    seg[...] = jnp.zeros_like(seg)
    seg[0:rows, :] = segments[...]

    pl.semaphore_wait(barrier, 10)

    q_own, q_x, q_y = PIECE * dp, PIECE * (y * 2 + 1 - x), PIECE * ((1 - y) * 2 + x)

    def travel(kind, t, k, first, rows_, there, src=None):
        source = seq if src is not None else lax.rem(z - k + 4, 4) * 2 + core
        where = full.at[t, source, pl.ds(pl.multiple_of(first, 16), rows_)]
        return remote_copy(
            where if src is None else src,
            where,
            gather_sem.at[0, kind, t, k - 1],
            gather_sem.at[1, kind, t, k - 1],
            there,
        )

    def line(t, k):
        src = shards.at[t, pl.ds(pl.multiple_of(q_own, 16), PIECE)]
        return travel(0, t, k, q_own, PIECE, (dp, lax.rem(z + k, 4) * 2 + core), src)

    def to_x(t, k):
        return travel(1, t, k, q_own, PIECE, over_x)

    def to_y(t, k):
        return travel(2, t, k, q_own, PIECE, over_y)

    def on_x(t, k):
        return travel(3, t, k, q_y, PIECE // 2, over_x)

    def on_y(t, k):
        return travel(4, t, k, q_x + PIECE // 2, PIECE // 2, over_y)

    def to_core(t, k):
        return travel(5, t, k, 0, 4 * PIECE, over_core)

    def own_to_core(t):
        return remote_copy(
            shards.at[t], full.at[t, seq], own_sem.at[0, t], own_sem.at[1, t], over_core
        )

    def own_to_full(t):
        return pltpu.make_async_copy(shards.at[t], full.at[t, seq], own_sem.at[2, t])

    def small_copies():
        copies = []
        for k in range(1, 8):
            for i, (src, dst) in enumerate(((vec, vec_all), (seg, seg_all))):
                copies.append(
                    remote_copy(
                        src,
                        dst.at[seq],
                        small_sem.at[0, i, k - 1],
                        small_sem.at[1, i, k - 1],
                        (dp, peer(k)),
                    )
                )
        return copies

    for copy in small_copies():
        copy.start()
    vec_all[seq] = vec[...]
    seg_all[seq] = seg[...]
    def relay(t):
        where = full.at[t, lax.rem(z + 2, 4) * 2 + core, pl.ds(pl.multiple_of(q_own, 16), PIECE)]
        return remote_copy(
            where,
            where,
            gather_sem.at[0, 6, t, 0],
            gather_sem.at[1, 0, t, 2 * z - 2],
            (dp, 3 * (z - 1) * 2 + core),
        )

    def direct(k):
        return {1: z != 3, 2: z >= 0, 3: z != 0}[k]

    def in_time(k):
        return {1: z != 0, 2: z >= 0, 3: z != 3}[k]

    relays = (z == 1) | (z == 2)

    def start_line(t):
        read_done(t)
        own_to_core(t).start()
        own_to_full(t).start()
        for k in (1, 2, 3):

            @pl.when(direct(k))
            def _():
                line(t, k).start()

    def arrived(t, k):
        line(t, k).wait_recv()
        to_x(t, k).start()
        to_y(t, k).start()

    for t in range(LEAD):
        start_line(t)

    def gather_step(step):
        for i in range(2):
            ahead = LEAD + 2 * step + i

            @pl.when(ahead < CHUNKS)
            def _(ahead=ahead):
                start_line(ahead)

        @pl.when(step < CHUNKS)
        def _():
            for k in (2, 1, 3):

                @pl.when(in_time(k))
                def _():
                    arrived(step, k)

                if k == 2:

                    @pl.when(relays)
                    def _():
                        relay(step).start()

        late = step - STAGE

        @pl.when((late >= 0) & (late < CHUNKS))
        def _():
            for k in (1, 3):

                @pl.when(jnp.logical_not(in_time(k)))
                def _():
                    arrived(late, k)

        second, third, last = step - 2 * STAGE, step - 3 * STAGE, step - 4 * STAGE

        @pl.when((second >= 0) & (second < CHUNKS))
        def _():
            for k in (1, 2, 3):
                to_y(second, k).wait_recv()
                on_x(second, k).start()
                to_x(second, k).wait_recv()
                on_y(second, k).start()

        @pl.when((third >= 0) & (third < CHUNKS))
        def _():
            for k in (1, 2, 3):
                on_x(third, k).wait_recv()
                on_y(third, k).wait_recv()
                to_core(third, k).start()

        @pl.when((last >= 0) & (last < CHUNKS))
        def _():
            for k in (1, 2, 3):
                to_core(last, k).wait_recv()
            own_to_core(last).wait_recv()
            own_to_full(last).wait()

    def load(u):
        return pltpu.make_async_copy(full.at[u], wbuf.at[lax.rem(u, 3)], load_sem.at[lax.rem(u, 3)])

    def weight(u):
        load(u).wait()
        return wbuf[lax.rem(u, 3)].reshape(width, width)

    def vector(i):
        return vectors[i : i + 1, :]

    def norm(v, i):
        return low(norm_rows(v, vector(i), vector(6 + i)))

    def prepare():
        for copy in small_copies():
            copy.wait()
        for s in range(8):
            vectors[:, s * 128 : s * 128 + 128] = f32(vec_all[s])
            columns = f32(seg_all[s]).T
            for r in range(rows):
                seg_cols[r, s * 128 : s * 128 + 128, :] = columns[:, r : r + 1]
                seg_rows[r : r + 1, s * 128 : s * 128 + 128] = f32(seg_all[s, r : r + 1, :])
        before = jnp.where(seq > 0, f32(seg_all[lax.max(seq - 1, 0)]), -1.0).T
        middle = f32(seg_all[seq]).T
        after = jnp.where(seq < 7, f32(seg_all[lax.min(seq + 1, 7)]), -1.0).T
        for r in range(rows):
            for first, col in (
                (0, before[frame_count - HALO :, r : r + 1]),
                (HALO, middle[:, r : r + 1]),
                (HALO + frame_count, after[:HALO, r : r + 1]),
            ):
                seg_plane[r, first : first + col.shape[0], :] = jnp.broadcast_to(col, (col.shape[0], 128))
        keys = lax.broadcasted_iota(jnp.int32, (TILE, TILE), 0)
        queries = lax.broadcasted_iota(jnp.int32, (TILE, TILE), 1)
        for i in range(2 * TILES - 1):
            apart = jnp.abs(keys - queries + TILE * (i - TILES + 1))
            e.distances[i] = jnp.log(1.0 + apart.astype(jnp.float32))
        norm0[...] = norm(f32(frames[...]), 0)

    def up(u, j, source):
        value = dot(source[...], weight(u))
        active = low(value * logistic(value))
        value = low(value)
        for half in range(2):
            to = pl.ds(pl.multiple_of((j * 2 + half) * 128, 128), 128)
            for i in range(4):
                first = half * 512 + i * 128
                pre[i, :, to] = value[:, first : first + 128]
                hid[i, :, to] = active[:, first : first + 128]

    def down(u, j, stream, target):
        value = dot(hid[j], weight(u))

        @pl.when(j == 0)
        def _():
            acc[...] = value

        @pl.when(j > 0)
        def _():
            acc[...] += value

        @pl.when(j == 3)
        def _():
            target[...] = f32(stream[...]) + 0.5 * acc[...]

    def keep_copies():
        return [
            pltpu.make_async_copy(pre, e.pre_keep, keep_sem.at[0]),
            pltpu.make_async_copy(hid, e.hid_keep, keep_sem.at[1]),
        ]

    def pk_copy(c, k, recv=False):
        there = peer(k)
        return remote_copy(
            pk_out.at[there, c],
            packed.at[there if recv else seq, c],
            pk_sem.at[0, there, c],
            pk_sem.at[1, there if recv else seq, c],
            (dp, there),
        )

    def project(u, c):
        value = low(dot(norm1[...], weight(u)))
        for s in range(8):
            pk_out[s, c] = value[:, s * 128 : s * 128 + 128].reshape(rows, frame_count, 128)
        packed[seq, c] = pk_out[seq, c]
        for k in range(1, 8):
            pk_copy(c, k).start()

    def att_copy(b, r, recv=False):
        return remote_copy(
            att_out.at[b, r],
            att_in.at[b if recv else seq, r],
            att_sem.at[0, b, r],
            att_sem.at[1, b if recv else seq, r],
            (dp, b),
        )

    def attend_step(i):
        row, block = i // 4, lax.rem(i, 4)
        out = attend_block(e, seq * 2, row, block)
        e.att_keep[row, pl.ds(pl.multiple_of(block * QUERIES, QUERIES), QUERIES), :] = out
        out = low(out)
        for half in range(2):
            b = block * 2 + half
            att_out[b, row] = out[half * 128 : half * 128 + 128]

            @pl.when(b != seq)
            def _():
                att_copy(b, row).start()

            @pl.when(b == seq)
            def _():
                att_in[b, row] = out[half * 128 : half * 128 + 128]

    def halo_copy(side):
        if side == 0:
            src, dst, there = gated.at[:, pl.ds(HALO, HALO)], gated.at[:, pl.ds(HALO + frame_count, HALO)], lax.rem(seq + 7, 8)
        else:
            src, dst, there = gated.at[:, pl.ds(frame_count, HALO)], gated.at[:, pl.ds(0, HALO)], lax.rem(seq + 1, 8)
        return remote_copy(src, dst, halo_sem.at[0, side], halo_sem.at[1, side], (dp, there))

    def convolve():
        @pl.when(seq > 0)
        def _():
            halo_copy(0).wait_send()
            halo_copy(1).wait_recv()

        @pl.when(seq < 7)
        def _():
            halo_copy(1).wait_send()
            halo_copy(0).wait_recv()

        gated_f[...] = f32(gated[...])

        def lanes(i, _):
            at = pl.ds(pl.multiple_of(i * 128, 128), 128)
            for r in range(rows):
                own = seg_plane[r, HALO : HALO + frame_count, :]
                total = jnp.zeros((frame_count, 128), jnp.float32)
                for shift in range(8):
                    near = gated_f[r, shift : shift + frame_count + 24, at]
                    seg_near = seg_plane[r, shift : shift + frame_count + 24, :]
                    for first in range(0, 32, 8):
                        tap = shift + first - 1
                        if 0 <= tap < 31:
                            same = seg_near[first : first + frame_count] == own
                            term = near[first : first + frame_count] * vectors[12 + tap : 13 + tap, at]
                            total = total + jnp.where(same, term, 0.0)
                mixed[r * frame_count : (r + 1) * frame_count, at] = total
            return 0

        lax.fori_loop(0, width // 128, lanes, 0)

    def step_work(step, _):
        gather_step(step)

        now = step - STEP

        def at(first, count=1):
            return pl.when((now >= first) & (now < first + count))

        @at(0)
        def _():
            prepare()

        @at(1, 4)
        def _():
            up(now - 1, now - 1, norm0)

        @at(5, 4)
        def _():
            down(now - 1, now - 5, frames, after_front)

        @at(9, 3)
        def _():
            @pl.when(now == 9)
            def _():
                norm1[...] = norm(after_front[...], 1)
                for copy in keep_copies():
                    copy.start()

            project(now - 1, now - 9)

        @at(14)
        def _():
            for c in range(3):
                for k in range(1, 8):
                    pk_copy(c, k, True).wait_recv()

        @at(14, 3)
        def _():
            def one(i, _):
                attend_step(i)
                return 0

            first = (now - 14) * 3
            lax.fori_loop(first, lax.min(first + 3, 8), one, 0)

        @at(18)
        def _():
            for r in range(rows):
                for k in range(1, 8):
                    att_copy(peer(k), r, True).wait_recv()
            for s in range(8):
                attended[:, s * 128 : s * 128 + 128] = att_in[s].reshape(rows * frame_count, 128)
            after_attend[...] = after_front[...] + dot(attended[...], weight(ATTEND_OUT))
            load(14).start()
            norm2[...] = norm(after_attend[...], 2)

        @at(18)
        def _():
            acc[...] = dot(norm2[...], weight(POINT_IN))
            conv_pre[0] = low(acc[...])
            gate = dot(norm2[...], weight(POINT_IN + 1))
            conv_pre[1] = low(gate)
            value = low(acc[...] * logistic(gate))
            gated[:, HALO : HALO + frame_count] = value.reshape(rows, frame_count, width)

            @pl.when(seq > 0)
            def _():
                halo_copy(0).start()

            @pl.when(seq < 7)
            def _():
                halo_copy(1).start()

        @at(19)
        def _():
            convolve()
            value = norm_rows(mixed[...], vector(3), vector(9))
            act[...] = low(value * logistic(value))
            after_conv[...] = after_attend[...] + dot(act[...], weight(POINT_OUT))
            norm4[...] = norm(after_conv[...], 4)

        @at(20, 2)
        def _():
            @pl.when(now == 20)
            def _():
                for copy in keep_copies():
                    copy.wait()

            for i in range(2):
                j = (now - 20) * 2 + i
                up(j + REAR_UP, j, norm4)

        @at(22, 2)
        def _():
            for i in range(2):
                j = (now - 22) * 2 + i
                down(j + REAR_DOWN, j, after_conv, after_rear)

        @at(0, 14)
        def _():
            load(now).start()

        for when, chunks in ((18, (15, 16)), (19, (17,)), (20, (18, 19)), (21, (20, 21)), (22, (22,))):

            @at(when)
            def _(chunks=chunks):
                for u in chunks:
                    load(u).start()

        return 0

    lax.fori_loop(0, STEP + 24, step_work, 0)

    for i in range(2):
        pltpu.make_async_copy(
            full.at[REAR_DOWN + i], wbuf.at[i], e.backward_sems[2].at[i]
        ).start()

    def drain(t, _):
        for kind in (to_x, to_y, on_x, on_y, to_core):
            for k in (1, 2, 3):
                kind(t, k).wait_send()
        for k in (1, 2, 3):

            @pl.when(direct(k))
            def _():
                line(t, k).wait_send()

        @pl.when(relays)
        def _():
            relay(t).wait_send()

        own_to_core(t).wait_send()
        return 0

    lax.fori_loop(0, CHUNKS, drain, 0)
    for c in range(3):
        for k in range(1, 8):
            pk_copy(c, k).wait_send()
    for r in range(rows):
        for k in range(1, 8):
            att_copy(peer(k), r).wait_send()


JOB_RU, JOB_PO, JOB_PI, JOB_AO, JOB_P, JOB_FD, JOB_FU, JOBS = 4, 8, 9, 11, 12, 15, 19, 23
RING, SHARES = 4, 5
GRADS = ((7, True), (6, False), (5, False), (4, False), (3, False), (2, False), (1, True), (0, False))
OUT_LAG = 6


def silu_slope(pre, grad):
    gate = logistic(pre)
    return grad * gate * (1.0 + pre * (1.0 - gate))


def tn(a, b):
    return lax.dot_general(a, b, (((0,), (0,)), ((), ())), preferred_element_type=jnp.float32)


def backward_part(e):
    full, gated, mixed, act, packed = e.full, e.gated, e.mixed, e.act, e.packed
    norm0, norm1, norm2, norm4, attended, conv_pre = (
        e.norm0,
        e.norm1,
        e.norm2,
        e.norm4,
        e.attended,
        e.conv_pre,
    )
    after_front, after_attend, after_conv, after_rear = (
        e.after_front,
        e.after_attend,
        e.after_conv,
        e.after_rear,
    )
    frames, cotangent, slopes = e.frames, e.cotangent, e.slopes
    result, frames_grad, vec_out, grads = e.result, e.frames_grad, e.vec_out, e.grads
    pre_grads, hid, wbuf, vectors, pool = e.pre, e.hid, e.wbuf, e.vectors, e.pool
    small, right, branch, conv_branch = e.small, e.right, e.branch, e.conv_branch
    gate_grads, attend_branch, parts = e.gate_grads, e.attend_branch, e.parts
    grad, total, gated_f, mixed_w, mixed_f = e.grad, e.total, e.gated_f, e.mixed_w, e.mixed_f
    seg_plane, seg_rows = e.seg_plane, e.seg_rows
    g_out, g_in, p_out, p_in = e.att_out, e.g_in, e.pk_out, e.p_in
    key_sum, value_sum, slope_sum, out_buf = e.key_sum, e.value_sum, e.slope_sum, e.out_buf
    h_buf, a_buf, b_buf, q_buf = e.h_buf, e.a_buf, e.b_buf, e.q_buf
    a_in, b_in, a2_in, b2_in, z_in, o_buf = e.a_in, e.b_in, e.a2_in, e.b2_in, e.z_in, e.o_buf
    vec_send, vec_in, vec_dp = e.vec_send, e.vec_in, e.vec_dp
    sem, vec_sem, load_sem, keep_sem, ga_sem, pk_sem, halo_sem, out_sem, sync = e.backward_sems
    y, x, z, core = place()
    dp, seq = y * 2 + x, z * 2 + core
    rows, width, frame_count = 2, 1024, 128
    length = 8 * frame_count
    over_x = (y * 2 + 1 - x, seq)
    over_y = ((1 - y) * 2 + x, seq)
    over_core = (dp, z * 2 + 1 - core)

    def peer(k):
        return lax.rem(seq + k, 8)

    def dp_peer(k):
        return (lax.rem(dp + k, 4), seq)

    pl.semaphore_signal(sync, inc=1, device_id=over_core, device_id_type=MESH_ID)
    pl.semaphore_wait(sync, 1)
    mine = 4 * RING

    def remote(src, dst, t, slot, there):
        return remote_copy(
            src, dst, sem.at[0, slot, lax.rem(t, RING)], sem.at[1, slot, lax.rem(t, RING)], there
        )

    def turn(t):
        return lax.rem(t, 2)

    def core_copies(t, r):
        return [
            remote(pool.at[pl.ds(mine + 4, 4)], pool.at[pl.ds(4 * r, 4)], t, 0, over_core)
        ]

    def first_copies(t, r):
        return [
            remote(h_buf.at[turn(t), pl.ds(0, 2), :, 1 - x], a_in.at[r], t, 1, over_x),
            remote(h_buf.at[turn(t), pl.ds(2, 2), 1 - y], b_in.at[r], t, 2, over_y),
        ]

    def second_copies(t, r):
        return [
            remote(a_buf.at[turn(t), :, 1 - y], a2_in.at[r], t, 3, over_y),
            remote(b_buf.at[turn(t), :, 1 - x], b2_in.at[r], t, 4, over_x),
        ]

    def line_copies(t, r):
        copies = []
        for k in (1, 2, 3):
            to = lax.rem(z + k, 4)
            copies.append(remote(q_buf.at[turn(t), to], z_in.at[r, k - 1], t, 4 + k, (dp, to * 2 + core)))
        return copies

    def share_copies(t, r):
        where = o_buf.at[lax.rem(t, SHARES), dp]
        return [remote(where, where, t, 8, over_x), remote(where, where, t, 9, over_y)]

    def across_copies(t, r):
        one = o_buf.at[lax.rem(t, SHARES), (1 - y) * 2 + x, pl.ds(0, PIECE // 2)]
        two = o_buf.at[lax.rem(t, SHARES), y * 2 + 1 - x, pl.ds(PIECE // 2, PIECE // 2)]
        return [remote(one, one, t, 10, over_x), remote(two, two, t, 11, over_y)]

    def out_start(t):
        slot = lax.rem(t, 2)
        first = 0
        for out, tall in GRADS:
            ref = grads[out]
            size = 128 if tall else width
            count = ref.shape[0] // size if tall else ref.shape[1] // size

            @pl.when((t >= first) & (t < first + count))
            def _(ref=ref, tall=tall, size=size, first=first):
                at = pl.ds(pl.multiple_of((t - first) * size, size), size)
                where = ref.at[at, :] if tall else ref.at[:, at]
                pltpu.make_async_copy(out_buf.at[slot], where, out_sem.at[slot]).start()

            first += count

    def out_done(t):
        slot = lax.rem(t, 2)
        pltpu.make_async_copy(out_buf.at[slot], out_buf.at[slot], out_sem.at[slot]).wait()

    def finish(copies):
        for copy in copies:
            copy.wait()

    def begin(copies):
        for copy in copies:
            copy.start()

    def write_out(t, r):
        finish(across_copies(t, r))

        @pl.when(t >= 2)
        def _():
            out_done(t - 2)

        out_buf[lax.rem(t, 2)] = f32(o_buf[lax.rem(t, SHARES)].reshape(128, width))
        out_start(t)

    def pass_on(t, r):
        finish(share_copies(t, r))
        begin(across_copies(t, r))

    def total_line(t, r):
        finish(line_copies(t, r))
        value = f32(q_buf[turn(t), z]) + f32(z_in[r, 0]) + f32(z_in[r, 1]) + f32(z_in[r, 2])
        o_buf[lax.rem(t, SHARES), dp] = low(value)
        begin(share_copies(t, r))

    def total_second(t, r):
        finish(second_copies(t, r))
        q_buf[turn(t), 0:2] = a_buf[turn(t), :, y] + a2_in[r]
        q_buf[turn(t), 2:4] = b_buf[turn(t), :, x] + b2_in[r]
        begin(line_copies(t, r))

    def total_first(t, r):
        finish(first_copies(t, r))
        a_buf[turn(t)] = h_buf[turn(t), 0:2, :, x] + a_in[r]
        b_buf[turn(t)] = h_buf[turn(t), 2:4, y] + b_in[r]
        begin(second_copies(t, r))

    def total_core(t, r):
        finish(core_copies(t, r))
        for i in range(4):
            value = pool[mine + i] + pool[4 * r + i]
            h_buf[turn(t), i] = value.reshape(2, 2, PIECE, width)
        begin(first_copies(t, r))

    def product(t, left, right):
        for i in range(8):
            part = tn(left[:, 128 * i : 128 * i + 128], right[...])
            pool[mine + 4 * lax.rem(core + i, 2) + i // 2] = low(part)
        begin(core_copies(t, lax.rem(t, RING)))

    sums = [total_core, total_first, total_second, total_line, pass_on, write_out]

    def sum_step(step):
        for depth in range(1, 7):
            t = step - depth

            @pl.when((t >= 0) & (t < JOBS))
            def _(t=t, depth=depth):
                sums[depth - 1](t, lax.rem(t, RING))

    def load(i, u):
        return pltpu.make_async_copy(full.at[u], wbuf.at[i], load_sem.at[i])

    def weight(i, u):
        load(i, u).wait()
        return wbuf[i].reshape(width, width)

    def keep_copies():
        return [
            pltpu.make_async_copy(e.pre_keep, pre_grads, keep_sem.at[0]),
            pltpu.make_async_copy(e.hid_keep, hid, keep_sem.at[1]),
        ]

    def vector(i):
        return vectors[i : i + 1, :]

    def norm_back(v, i, dy):
        centred = v - jnp.mean(v, axis=-1, keepdims=True)
        rstd = lax.rsqrt(jnp.mean(centred * centred, axis=-1, keepdims=True) + 1e-05)
        n = centred * rstd
        small[i : i + 1, :] = jnp.sum(dy * n, axis=0, keepdims=True)
        small[6 + i : 7 + i, :] = jnp.sum(dy, axis=0, keepdims=True)
        dn = dy * vector(i)
        first = jnp.mean(dn, axis=-1, keepdims=True)
        second = jnp.mean(dn * n, axis=-1, keepdims=True)
        return rstd * (dn - first - n * second)

    def strided(b):
        blocks = []
        for half in range(2):
            at = pl.ds(pl.multiple_of((b * 2 + half) * 128, 128), 128)
            blocks += [pre_grads[j, :, at] for j in range(4)]
        return jnp.concatenate(blocks, axis=1)

    def down_back(j, down):
        hidden_grad = nt(branch[...], weight(lax.rem(j, 2), down + j))
        pre_grads[j] = low(silu_slope(f32(pre_grads[j]), hidden_grad))

    def up_back(b, up):
        value = nt(strided(b), weight(lax.rem(b, 2), up + b))

        @pl.when(b == 0)
        def _():
            total[...] = value

        @pl.when(b > 0)
        def _():
            total[...] += value

    def prepare():
        small[...] = jnp.zeros_like(small)
        slope_sum[...] = jnp.zeros_like(slope_sum)

    def halo_copy(side):
        if side == 0:
            src, dst = pl.ds(HALO, HALO), pl.ds(HALO + frame_count, HALO)
            there = lax.rem(seq + 7, 8)
        else:
            src, dst = pl.ds(frame_count, HALO), pl.ds(0, HALO)
            there = lax.rem(seq + 1, 8)
        return remote_copy(
            mixed_w.at[:, src],
            mixed_w.at[:, dst],
            halo_sem.at[0, side],
            halo_sem.at[1, side],
            (dp, there),
        )

    def convolve_back(r):
        def lanes(i, _):
            at = pl.ds(pl.multiple_of(i * 128, 128), 128)
            own = seg_plane[r, HALO : HALO + frame_count, :]
            mine = mixed_f[r, HALO : HALO + frame_count, at]
            value = jnp.zeros((frame_count, 128), jnp.float32)
            for shift in range(8):
                window = slice(shift, shift + frame_count + 24)
                seg_near = seg_plane[r, window, :]
                gated_near = gated_f[r, window, at]
                mixed_near = mixed_f[r, window, at]
                for first in range(0, 32, 8):
                    tap = shift + first - 1
                    if 0 <= tap < 31:
                        here = slice(first, first + frame_count)
                        same = seg_near[here] == own
                        near = jnp.where(same, gated_near[here], 0.0)
                        small[12 + tap : 13 + tap, at] += jnp.sum(near * mine, axis=0, keepdims=True)
                        came = jnp.where(same, mixed_near[here], 0.0)
                        value = value + came * vectors[12 + 30 - tap : 13 + 30 - tap, at]
            total[r * frame_count : (r + 1) * frame_count, at] = value
            return 0

        lax.fori_loop(0, width // 128, lanes, 0)

    def ga_copy(k, recv=False):
        there = peer(k)
        return remote_copy(
            g_out.at[there],
            g_in.at[there if recv else seq],
            ga_sem.at[0, there],
            ga_sem.at[1, there if recv else seq],
            (dp, there),
        )

    def pk_copy(there, c, r, recv=False):
        return remote_copy(
            p_out.at[there, c, r],
            p_in.at[there if recv else seq, c, r],
            pk_sem.at[0, there, c, r],
            pk_sem.at[1, there if recv else seq, c, r],
            (dp, there),
        )

    def attend_back_step(i):
        row, block = i // 4, lax.rem(i, 4)
        first = pl.multiple_of(block * QUERIES, QUERIES)
        query_seg = seg_rows[pl.ds(row, 1), pl.ds(first, QUERIES)]
        q = packed[pl.ds(block * 2, 2), 0, row].reshape(QUERIES, 128)
        g = g_in[pl.ds(block * 2, 2), row].reshape(QUERIES, 128)
        key_t = packed[:, 1, row].reshape(length, 128).T
        deltas = (f32(g) * e.att_keep[row, pl.ds(first, QUERIES), :]).T

        @pl.when(block == 0)
        def _():
            key_sum[...] = jnp.zeros_like(key_sum)
            value_sum[...] = jnp.zeros_like(value_sum)

        outs = []
        for head in range(2):
            q_head = head_lanes(q, head, 0.125)
            g_head = head_lanes(g, head)
            slope = slopes[seq * 2 + head]
            log_sum = e.log_sum[row, head, :, pl.ds(first, QUERIES)]
            delta = jnp.sum(deltas[64 * head : 64 * head + 64], axis=0, keepdims=True)
            slope_total = jnp.zeros((8, QUERIES), jnp.float32)
            for kb in range(TILES):
                at = slice(kb * TILE, kb * TILE + TILE)
                logit, distance = logit_tile(e, q_head, slope, query_seg, row, block, kb)
                prob = jnp.exp(logit - log_sum)
                prob_grad = nt(packed[kb, 2, row], g_head)
                value_sum[at, :] += dot(low(prob), g_head)
                logit_grad = prob * (prob_grad - delta)
                slope_total = slope_total + jnp.sum(
                    (logit_grad * distance).reshape(TILE // 8, 8, QUERIES), axis=0
                )
                score = low(logit_grad)
                e.scores[at, :] = score
                key_sum[at, :] += dot(score, q_head)
            slope_sum[head] -= slope_total
            query_t = dot(key_t, e.scores[...])
            outs.append(query_t[64 * head : 64 * head + 64] * 0.125)
        query = low(jnp.concatenate(outs, axis=0).T)

        def deliver(b, c, value):
            p_out[b, c, row] = value

            @pl.when(b != seq)
            def _():
                pk_copy(b, c, row).start()

            @pl.when(b == seq)
            def _():
                p_in[b, c, row] = value

        for half in range(2):
            deliver(block * 2 + half, 0, query[half * 128 : half * 128 + 128])

        @pl.when(block == 3)
        def _():
            for b in range(8):
                at = slice(b * 128, b * 128 + 128)
                deliver(b, 1, low(key_sum[at, :]))
                deliver(b, 2, low(value_sum[at, :]))

    def vec_copies():
        copies = []
        for k in range(1, 8):
            copies.append(
                remote_copy(
                    vec_send.at[peer(k)],
                    vec_in.at[seq],
                    vec_sem.at[0, k - 1],
                    vec_sem.at[1, k - 1],
                    (dp, peer(k)),
                )
            )
        return copies

    def vec_dp_copies():
        where = vec_dp.at[dp]
        return [
            remote_copy(where, where, vec_sem.at[0, 6 + k], vec_sem.at[1, 6 + k], dp_peer(k))
            for k in (1, 2, 3)
        ]

    def send_vectors():
        lane = lax.broadcasted_iota(jnp.int32, (1, 128), 1)
        mine = jnp.zeros((1, 128), jnp.float32)
        for head in range(2):
            value = jnp.sum(jnp.sum(slope_sum[head], axis=0, keepdims=True), axis=-1, keepdims=True)
            mine = mine + jnp.where(lane == seq * 2 + head, value, 0.0)
        for s in range(8):
            vec_send[s] = small[:, s * 128 : s * 128 + 128]
            vec_send[s, 43:44, :] = mine
        vec_in[seq] = vec_send[seq]
        begin(vec_copies())

    def sum_vectors():
        finish(vec_copies())
        value = vec_in[0]
        for i in range(1, 8):
            value = value + vec_in[i]
        vec_dp[dp] = value
        begin(vec_dp_copies())

    def finish_vectors():
        finish(vec_dp_copies())
        vec_out[...] = (vec_dp[0] + vec_dp[1]) + (vec_dp[2] + vec_dp[3])

    def step_work(step, _):
        sum_step(step)

        def at(first, count=1):
            return pl.when((step >= first) & (step < first + count))

        @at(0)
        def _():
            prepare()
            result[...] = low(norm_rows(after_rear[...], vector(5), vector(11)))
            grad[...] = norm_back(after_rear[...], 5, f32(cotangent[...]))
            branch[...] = low(0.5 * grad[...])

        @at(12, 3)
        def _():
            c = step - 12
            for r in range(rows):
                for k in range(1, 8):
                    pk_copy(peer(k), c, r, True).wait_recv()
                    pk_copy(peer(k), c, r).wait_send()
            for s in range(8):
                parts[c, :, s * 128 : s * 128 + 128] = p_in[s, c].reshape(rows * frame_count, 128)

        @at(0, JOB_RU)
        def _():
            product(step, hid.at[step], branch)

        @at(JOB_RU, 4)
        def _():
            right[...] = strided(step - JOB_RU)
            product(step, norm4, right)

        @at(JOB_PO)
        def _():
            product(step, act, conv_branch)

        @at(JOB_PI, 2)
        def _():
            product(step, norm2, gate_grads.at[step - JOB_PI])

        @at(JOB_AO)
        def _():
            product(step, attended, attend_branch)

        @at(JOB_P, 3)
        def _():
            product(step, norm1, parts.at[step - JOB_P])

        @at(JOB_FD, 4)
        def _():
            product(step, hid.at[step - JOB_FD], branch)

        @at(JOB_FU, 4)
        def _():
            right[...] = strided(step - JOB_FU)
            product(step, norm0, right)

        @at(0)
        def _():
            for j in range(4):
                down_back(j, REAR_DOWN)
                load(j % 2, REAR_DOWN + 2 + j if j < 2 else REAR_UP + j - 2).start()

        @at(1)
        def _():
            for b in range(4):
                up_back(b, REAR_UP)
                if b < 2:
                    load(b, REAR_UP + 2 + b).start()
            load(0, POINT_OUT).start()
            grad[...] += norm_back(after_conv[...], 4, total[...])
            conv_branch[...] = low(grad[...])

        @at(2)
        def _():
            act_grad = nt(conv_branch[...], weight(0, POINT_OUT))
            act_grad = silu_slope(norm_rows(mixed[...], vector(3), vector(9)), act_grad)
            value = low(norm_back(mixed[...], 3, act_grad))
            mixed_w[:, HALO : HALO + frame_count] = value.reshape(rows, frame_count, width)

            @pl.when(seq > 0)
            def _():
                halo_copy(0).start()

            @pl.when(seq < 7)
            def _():
                halo_copy(1).start()

            load(0, POINT_IN).start()
            load(1, POINT_IN + 1).start()

        @at(3)
        def _():
            @pl.when(seq > 0)
            def _():
                halo_copy(0).wait_send()
                halo_copy(1).wait_recv()

            @pl.when(seq < 7)
            def _():
                halo_copy(1).wait_send()
                halo_copy(0).wait_recv()

            mixed_f[...] = f32(mixed_w[...])
            convolve_back(0)

        @at(4)
        def _():
            convolve_back(1)

        @at(5)
        def _():
            gate = logistic(f32(conv_pre[1]))
            gate_grads[0] = low(total[...] * gate)
            gate_grads[1] = low(total[...] * f32(conv_pre[0]) * gate * (1.0 - gate))
            norm_grad = nt(gate_grads[0], weight(0, POINT_IN))
            load(0, ATTEND_OUT).start()
            norm_grad = norm_grad + nt(gate_grads[1], weight(1, POINT_IN + 1))
            grad[...] += norm_back(after_attend[...], 2, norm_grad)
            attend_branch[...] = low(grad[...])
            value = low(nt(attend_branch[...], weight(0, ATTEND_OUT)))
            for s in range(8):
                g_out[s] = value[:, s * 128 : s * 128 + 128].reshape(rows, frame_count, 128)
            g_in[seq] = g_out[seq]
            for k in range(1, 8):
                ga_copy(k).start()
            load(0, PROJECT).start()
            load(1, PROJECT + 1).start()

        @at(7)
        def _():
            for k in range(1, 8):
                ga_copy(k, True).wait_recv()
                ga_copy(k).wait_send()

        @at(7, 4)
        def _():
            def one(i, _):
                attend_back_step((step - 7) * 2 + i)
                return 0

            lax.fori_loop(0, 2, one, 0)

        @at(12)
        def _():
            total[...] = nt(parts[0], weight(0, PROJECT))
            load(0, PROJECT + 2).start()

        @at(13)
        def _():
            total[...] += nt(parts[1], weight(1, PROJECT + 1))
            load(1, DOWN + 1).start()

        @at(14)
        def _():
            for copy in keep_copies():
                copy.wait()
            norm_grad = total[...] + nt(parts[2], weight(0, PROJECT + 2))
            load(0, DOWN).start()
            grad[...] += norm_back(after_front[...], 1, norm_grad)
            branch[...] = low(0.5 * grad[...])

        @at(8)
        def _():
            for copy in keep_copies():
                copy.start()

        @at(15, 2)
        def _():
            for i in range(2):
                j = (step - 15) * 2 + i
                down_back(j, DOWN)
                load(i, lax.rem(DOWN + 2 + j, PROJECT)).start()

        @at(17, 2)
        def _():
            for i in range(2):
                b = (step - 17) * 2 + i
                up_back(b, UP)

                @pl.when(b < 2)
                def _(b=b, i=i):
                    load(i, UP + 2 + b).start()

        @at(19)
        def _():
            frames_grad[...] = low(
                grad[...] + norm_back(f32(frames[...]), 0, total[...])
            )
            send_vectors()

        @at(22)
        def _():
            sum_vectors()

        @at(24)
        def _():
            finish_vectors()

        return 0

    lax.fori_loop(0, JOBS + OUT_LAG, step_work, 0)
    out_done(JOBS - 2)
    out_done(JOBS - 1)


class Refs:
    pass


def layer(weights, gains, biases, depth, segments, frames, cotangent, slopes):
    bf16, single = jnp.bfloat16, jnp.float32
    tokens, width = frames.shape
    tall = 128 + 2 * HALO
    dma = pltpu.SemaphoreType.DMA
    vmem, hbm = pl.BlockSpec(memory_space=pltpu.VMEM), pl.BlockSpec(memory_space=pltpu.HBM)

    def buf(kind, *sizes):
        return pltpu.VMEM(sizes, kind)

    plain, wide = buf(bf16, tokens, width), buf(single, tokens, width)
    four = buf(bf16, 4, tokens, width)
    quarter = (PIECE, width)
    scratch = dict(
        vec_all=buf(bf16, 8, VECTORS, 128),
        seg_all=buf(jnp.int32, 8, 8, 128),
        norm0=plain,
        norm1=plain,
        norm2=plain,
        norm4=plain,
        attended=plain,
        act=plain,
        pre=four,
        hid=four,
        packed=buf(bf16, 8, 3, 2, 128, 128),
        conv_pre=buf(bf16, 2, tokens, width),
        gated=buf(bf16, 2, tall, width),
        mixed=wide,
        after_front=wide,
        after_attend=wide,
        after_conv=wide,
        after_rear=wide,
        wbuf=buf(bf16, 3, 8, 128, width),
        vectors=buf(single, VECTORS, width),
        pool=buf(bf16, 4 * RING + 8, 128, width),
        pk_out=buf(bf16, 8, 3, 2, 128, 128),
        att_out=buf(bf16, 8, 2, 128, 128),
        att_in=buf(bf16, 8, 2, 128, 128),
        att_keep=buf(single, 2, 1024, 128),
        log_sum=buf(single, 2, 2, 1, 1024),
        logits=buf(single, TILES, TILE, QUERIES),
        scores=buf(bf16, TILES * TILE, QUERIES),
        distances=buf(single, 2 * TILES - 1, TILE, TILE),
        gated_f=buf(single, 2, tall, width),
        seg_plane=buf(single, 2, tall, 128),
        seg_cols=buf(single, 2, 1024, 1),
        seg_rows=buf(single, 8, 1024),
        vec_wide=buf(single, VECTORS, 128),
        vec=buf(bf16, VECTORS, 128),
        seg=buf(jnp.int32, 8, 128),
        small=buf(single, VECTORS, width),
        right=plain,
        branch=plain,
        conv_branch=plain,
        gate_grads=buf(bf16, 2, tokens, width),
        attend_branch=plain,
        parts=buf(bf16, 3, tokens, width),
        grad=wide,
        total=wide,
        mixed_w=buf(bf16, 2, tall, width),
        mixed_f=buf(single, 2, tall, width),
        g_in=buf(bf16, 8, 2, 128, 128),
        p_in=buf(bf16, 8, 3, 2, 128, 128),
        key_sum=buf(single, 1024, 128),
        value_sum=buf(single, 1024, 128),
        slope_sum=buf(single, 2, 8, QUERIES),
        out_buf=buf(single, 2, 128, width),
        h_buf=buf(bf16, 2, 4, 2, 2, *quarter),
        a_buf=buf(bf16, 2, 2, 2, *quarter),
        b_buf=buf(bf16, 2, 2, 2, *quarter),
        q_buf=buf(bf16, 2, 4, *quarter),
        a_in=buf(bf16, RING, 2, 2, *quarter),
        b_in=buf(bf16, RING, 2, 2, *quarter),
        a2_in=buf(bf16, RING, 2, *quarter),
        b2_in=buf(bf16, RING, 2, *quarter),
        z_in=buf(bf16, RING, 3, *quarter),
        o_buf=buf(bf16, SHARES, 4, *quarter),
        vec_send=buf(single, 8, VECTORS, 128),
        vec_in=buf(single, 8, VECTORS, 128),
        vec_dp=buf(single, 4, VECTORS, 128),
    )
    forward_sems = [(2, 7, CHUNKS, 3), (4, CHUNKS), (2, 2, 7), (2, 8, 3), (2, 8, 2), (2, 2), (3,), (2,)]
    backward_sems = [(2, 12, RING), (2, 10), (2,), (2,), (2, 8), (2, 8, 3, 2), (2, 2), (2,)]
    count = len(forward_sems)

    def kernel(*refs):
        e = Refs()
        e.sources = refs[:8]
        e.gains, e.biases, e.depth, e.segments, e.frames, e.cotangent, e.slopes = refs[8:15]
        e.result, e.frames_grad, e.vec_out = refs[15:18]
        e.grads = refs[18:26]
        e.full, e.pre_keep, e.hid_keep = refs[26:29]
        for name, ref in zip(scratch, refs[29:]):
            setattr(e, name, ref)
        sems = refs[29 + len(scratch) :]
        e.forward_sems, e.backward_sems = sems[:count], sems[count:]
        for wide_ref in (e.gated, e.mixed_w):
            wide_ref[:, :HALO] = jnp.zeros((2, HALO, width), bf16)
            wide_ref[:, HALO + 128 :] = jnp.zeros((2, HALO, width), bf16)
        forward_part(e)
        backward_part(e)

    shape = jax.ShapeDtypeStruct
    return pl.pallas_call(
        kernel,
        in_specs=[hbm] * 8 + [vmem] * 6 + [pl.BlockSpec(memory_space=pltpu.SMEM)],
        out_specs=[vmem] * 3 + [hbm] * 11,
        out_shape=[
            shape((tokens, width), bf16),
            shape((tokens, width), bf16),
            shape((VECTORS, 128), single),
        ]
        + [shape(weight.shape, single) for weight in weights]
        + [shape((CHUNKS, 8, 128, width), bf16)]
        + [shape((4, tokens, width), bf16)] * 2,
        scratch_shapes=list(scratch.values())
        + [dma(sizes) for sizes in forward_sems + backward_sems]
        + [pltpu.SemaphoreType.REGULAR],
        compiler_params=pltpu.CompilerParams(
            collective_id=0, has_side_effects=True, vmem_limit_bytes=VMEM_LIMIT
        ),
        name="layer",
    )(*weights, gains, biases, depth, segments, frames, cotangent, slopes)


def copy_kernel(*refs):
    count = 10
    sources, vec, targets = refs[:count], refs[count], refs[count + 1 : 2 * count + 1]
    gains, biases, depth, slopes = refs[2 * count + 1 : 2 * count + 5]
    buffers = refs[2 * count + 5 : 3 * count + 5]
    read_sem, write_sem = refs[3 * count + 5 :]
    jobs = []
    for i in range(count):
        rows = sources[i].shape[0]
        height = rows // 4
        for part in range(4):
            at = pl.ds(part * height, height)
            jobs.append((i, at, 4 * i + part))

    def read(job):
        i, at, n = job
        return pltpu.make_async_copy(sources[i].at[at], buffers[i].at[at], read_sem.at[n])

    def write(job):
        i, at, n = job
        return pltpu.make_async_copy(buffers[i].at[at], targets[i].at[at], write_sem.at[n])

    for job in jobs:
        read(job).start()
    gains[...] = vec[0:6, :]
    biases[...] = vec[6:12, :]
    depth[...] = vec[12:43, :]
    slopes[...] = vec[43:44, :]
    for job in jobs:
        read(job).wait()
        write(job).start()
    for job in jobs:
        write(job).wait()


def copy_out(arrays, vec):
    shape = jax.ShapeDtypeStruct
    vmem, hbm = pl.BlockSpec(memory_space=pltpu.VMEM), pl.BlockSpec(memory_space=pltpu.HBM)
    size = sum(array.size * array.dtype.itemsize for array in arrays)
    return pl.pallas_call(
        copy_kernel,
        in_specs=[hbm] * len(arrays) + [vmem],
        out_specs=[hbm] * len(arrays) + [vmem] * 4,
        out_shape=[shape(array.shape, array.dtype) for array in arrays]
        + [shape((height, 128), jnp.float32) for height in (6, 6, 31, 1)],
        scratch_shapes=[pltpu.VMEM(array.shape, array.dtype) for array in arrays]
        + [pltpu.SemaphoreType.DMA((4 * len(arrays),))] * 2,
        compiler_params=pltpu.CompilerParams(vmem_limit_bytes=VMEM_LIMIT),
        cost_estimate=pl.CostEstimate(flops=0, bytes_accessed=2 * size, transcendentals=0),
        name="copy_out",
    )(*arrays, vec)


def body_staged(
    frames,
    segments,
    cotangent,
    norm_gains,
    norm_biases,
    front_up,
    front_down,
    attend_in,
    attend_out,
    slopes,
    point_in,
    depthwise,
    point_out,
    rear_up,
    rear_down,
):
    width = frames.shape[2]
    token_count = frames.shape[0] * frames.shape[1]

    weights = (
        front_up,
        front_down,
        attend_in,
        attend_out,
        point_in,
        point_out,
        rear_up,
        rear_down,
    )
    tokens = frames.reshape(token_count, width)
    result, frames_grad, vectors, *grads = layer(
        weights,
        norm_gains,
        norm_biases,
        depthwise,
        segments,
        tokens,
        cotangent.reshape(token_count, width),
        slopes,
    )
    *arrays, gains_grad, biases_grad, depth_grad, slopes_grad = copy_out(
        [result, frames_grad, *grads[:8]], vectors
    )
    result, frames_grad, *grads = arrays
    return (
        result.reshape(frames.shape),
        frames_grad.reshape(frames.shape),
        gains_grad,
        biases_grad,
        *grads[:4],
        slopes_grad[0, : slopes.shape[0]],
        grads[4],
        depth_grad,
        *grads[5:],
    )


def solution(mesh):
    placed = (
        P("dp", "seq", None),
        P("dp", "seq"),
        P("dp", "seq", None),
        P(None, "seq"),
        P(None, "seq"),
        P("seq", None),
        P("seq", None),
        P("seq", None),
        P("seq", None),
        P(),
        P("seq", None),
        P(None, "seq"),
        P("seq", None),
        P("seq", None),
        P("seq", None),
    )
    sizes = mesh.shape
    staged = sizes["dp"] == 4 and sizes["seq"] == 8
    return jax.shard_map(
        body_staged if staged else body,
        mesh=mesh,
        in_specs=placed,
        out_specs=(
            P("dp", "seq", None),
            P("dp", "seq", None),
            P(None, "seq"),
            P(None, "seq"),
            P("seq", None),
            P("seq", None),
            P("seq", None),
            P("seq", None),
            P(),
            P("seq", None),
            P(None, "seq"),
            P("seq", None),
            P("seq", None),
            P("seq", None),
        ),
        check_vma=False,
    )
```
